32 devices in a mesh: dp: 8 (over z, core), seq: 4 (over y, x).
Axes of the slice: x: 2, y: 2, z: 4, core: 2. Of those that a mesh axis runs over, the one named last changes fastest.
Arguments:
- tokens: bfloat16 [16, 1024, 1024], P('dp', 'seq'), may hold values from -6 to 6
- lengths: int32 [16, 8], P('dp'), may hold values from 0 to 1024, as said below
- timesteps: int32 [16, 8], P('dp'), may hold values from 0 to 4999
- w_query: bfloat16 [1024, 1024], P(('dp', 'seq')), may hold values from -0.1875 to 0.1875
- b_query: bfloat16 [1024], P(('dp', 'seq')), may hold values from -4 to 4
- w_key: bfloat16 [1024, 1024], P(('dp', 'seq')), may hold values from -0.1875 to 0.1875
- w_value: bfloat16 [1024, 1024], P(('dp', 'seq')), may hold values from -0.1875 to 0.1875
- b_value: bfloat16 [1024], P(('dp', 'seq')), may hold values from -4 to 4
- w_out: bfloat16 [1024, 1024], P(('dp', 'seq')), may hold values from -1.5 to 1.5
- b_out: bfloat16 [1024], P(('dp', 'seq')), may hold values from -4 to 4
- gain_one: bfloat16 [1024], P(('dp', 'seq')), may hold values from 0.099609375 to 1.8984375
- shift_one: bfloat16 [1024], P(('dp', 'seq')), may hold values from -4 to 4
- w_up: bfloat16 [1024, 4096], P(('dp', 'seq')), may hold values from -0.1875 to 0.1875
- b_up: bfloat16 [4096], P(('dp', 'seq')), may hold values from -4 to 4
- w_down: bfloat16 [4096, 1024], P(('dp', 'seq')), may hold values from -0.09375 to 0.09375
- b_down: bfloat16 [1024], P(('dp', 'seq')), may hold values from -4 to 4
- gain_two: bfloat16 [1024], P(('dp', 'seq')), may hold values from 0.099609375 to 1.8984375
- shift_two: bfloat16 [1024], P(('dp', 'seq')), may hold values from -4 to 4
- w_time: bfloat16 [1024], P(('dp', 'seq')), may hold values from -6 to 6
- b_time: bfloat16 [1024], P(('dp', 'seq')), may hold values from -6 to 6
- cotangent: bfloat16 [16, 1024, 1024], P('dp', 'seq'), may hold values from -6 to 6
Outputs:
- output: bfloat16 [16, 1024, 1024], P('dp', 'seq')
- grad_tokens: bfloat16 [16, 1024, 1024], P('dp', 'seq')
- grad_w_query: float32 [1024, 1024], P(('dp', 'seq'))
- grad_b_query: float32 [1024], P(('dp', 'seq'))
- grad_w_key: float32 [1024, 1024], P(('dp', 'seq'))
- grad_w_value: float32 [1024, 1024], P(('dp', 'seq'))
- grad_b_value: float32 [1024], P(('dp', 'seq'))
- grad_w_out: float32 [1024, 1024], P(('dp', 'seq'))
- grad_b_out: float32 [1024], P(('dp', 'seq'))
- grad_gain_one: float32 [1024], P(('dp', 'seq'))
- grad_shift_one: float32 [1024], P(('dp', 'seq'))
- grad_w_up: float32 [1024, 4096], P(('dp', 'seq'))
- grad_b_up: float32 [4096], P(('dp', 'seq'))
- grad_w_down: float32 [4096, 1024], P(('dp', 'seq'))
- grad_b_down: float32 [1024], P(('dp', 'seq'))
- grad_gain_two: float32 [1024], P(('dp', 'seq'))
- grad_shift_two: float32 [1024], P(('dp', 'seq'))
- grad_w_time: float32 [1024], P(('dp', 'seq'))
- grad_b_time: float32 [1024], P(('dp', 'seq'))
The draws below stay inside these ranges and needn't reach their ends.
Inputs may be any that keep to these rules, and one draw needn't show every extreme that they name: `lengths`: items are packed in order from position 0. Among the 2 sequences of each index of dp, one, chosen by the seed, is a single item of 1024 tokens, with the other slots 0. In every other sequence each item holds 128 or 512 tokens, except that the last nonempty one may be cut shorter, and the slots after it hold 0; fewer than 128 padding positions end it; its first item holds 128 tokens, its second 4 * 128.
All inputs are finite; a program needn't handle non-finite values.
Results may differ from the reference program's by a relative error of at most 0.017.
The reference program's roundings to bfloat16 on the way count: a program that leaves them out, or rounds other values in their place, can miss the bound.
Values may be sent and summed in bfloat16 or wider, within the bound.
No kernel may reach another device: no remote copies, remote signals or barrier semaphores. Data moves between devices by JAX's collectives and lax.ppermute only.
A program may use at most 192 MiB of HBM per device.

```python
import jax
import jax.numpy as jnp
from jax import lax

D = 1024
HEADS = 16
HD = 64
FF = 4096
SEQS_DEV = 2
SHORT = 128
TSTEPS = 5000
NSEQ = 16
LEN = 1024
ITEMS = 8


def draw_lengths(key, part):
    key = jax.random.fold_in(key, 7)
    pick_key, pad_key, whole_key = jax.random.split(key, 3)
    long_pick = jax.random.randint(pick_key, (NSEQ, ITEMS), 0, 2)
    wanted = jnp.where(long_pick == 1, 4 * SHORT, SHORT).astype(jnp.int32)
    wanted = wanted.at[:, 0].set(SHORT).at[:, 1].set(4 * SHORT)
    padding = jax.random.randint(pad_key, (NSEQ,), 0, SHORT).astype(jnp.int32)

    def place(remaining, want):
        taken = jnp.minimum(want, remaining)
        return (remaining - taken, taken)
    unused, taken = lax.scan(place, (LEN - padding).astype(jnp.int32), jnp.transpose(wanted))
    packed = jnp.transpose(taken).astype(jnp.int32)
    whole_pick = jax.random.randint(whole_key, (NSEQ // SEQS_DEV,), 0, SEQS_DEV).astype(jnp.int32)
    seq_ids = jnp.arange(NSEQ, dtype=jnp.int32)
    is_whole = seq_ids % SEQS_DEV == jnp.repeat(whole_pick, SEQS_DEV)
    slot_ids = jnp.arange(ITEMS, dtype=jnp.int32)
    whole_row = jnp.where(slot_ids == 0, LEN, 0).astype(jnp.int32)
    return jnp.where(is_whole[:, None], whole_row[None, :], packed).astype(jnp.int32)


def touch_ends(values, own_key, least, high):
    longest = values.shape.index(max(values.shape))
    spots = []
    for shift in (0, 1):
        where = [jax.random.randint(jax.random.fold_in(own_key, axis), (), 0, length) for axis, length in enumerate(values.shape)]
        where[longest] = (where[longest] + shift) % values.shape[longest]
        spots.append(tuple(where))
    return values.at[spots[0]].set(least).at[spots[1]].set(high)


def shard_levels(stream_key, shape, cuts, least, high):
    loudness = 1.0
    for dim, blocks in cuts:
        draws = jax.random.uniform(jax.random.fold_in(jax.random.fold_in(stream_key, 6), dim), (blocks,), jnp.float32, least / len(cuts), high / len(cuts))
        loudness = loudness * jnp.repeat(jnp.exp(draws), shape[dim] // blocks).reshape((-1,) + (1,) * (len(shape) - 1 - dim))
    return loudness


def normal_values(rng, shape, deviation, most, pieces=(), kind=jnp.bfloat16):
    values = jax.random.normal(rng, shape, jnp.float32) * deviation
    if len(pieces) > 0:
        values = shard_levels(rng, shape, pieces, -0.22, 0.18) * values
    return jnp.clip(values, min=-most, max=most).astype(kind)


def setup_inputs(seed: int = 0) -> dict:
    key_of = jax.random.split(jax.random.key(seed), 22)
    return {
        "tokens": normal_values(key_of[0], (NSEQ, LEN, D), 1.0, 6.0, ((0, 8), (1, 4))),
        "lengths": draw_lengths(jax.random.fold_in(key_of[21], 71), 0),
        "timesteps": touch_ends(jax.random.randint(key_of[2], (NSEQ, ITEMS), 0, TSTEPS), jax.random.fold_in(key_of[2], 1), 0, TSTEPS - 1).astype(jnp.int32),
        "w_query": normal_values(key_of[3], (D, D), D ** -0.5, 0.1875, ((0, 32),)),
        "b_query": normal_values(key_of[4], (D,), 0.3, 4.0, ((0, 32),)),
        "w_key": normal_values(key_of[5], (D, D), D ** -0.5, 0.1875, ((0, 32),)),
        "w_value": normal_values(key_of[6], (D, D), D ** -0.5, 0.1875, ((0, 32),)),
        "b_value": normal_values(key_of[7], (D,), 0.3, 4.0, ((0, 32),)),
        "w_out": normal_values(key_of[8], (D, D), (max(D * 16 // LEN, 1)) ** -0.5, 1.5, ((0, 32),)),
        "b_out": normal_values(key_of[9], (D,), 0.3, 4.0, ((0, 32),)),
        "gain_one": jnp.clip(1.0 + 0.18 * jax.random.normal(key_of[10], (D,), jnp.float32), 0.099609375, 1.8984375).astype(jnp.bfloat16),
        "shift_one": normal_values(key_of[11], (D,), 0.3, 4.0, ((0, 32),)),
        "w_up": normal_values(key_of[12], (D, FF), D ** -0.5, 0.1875, ((0, 32),)),
        "b_up": normal_values(key_of[13], (FF,), 0.3, 4.0, ((0, 32),)),
        "w_down": normal_values(key_of[14], (FF, D), FF ** -0.5, 0.09375, ((0, 32),)),
        "b_down": normal_values(key_of[15], (D,), 0.3, 4.0, ((0, 32),)),
        "gain_two": jnp.clip(1.0 + 0.18 * jax.random.normal(key_of[16], (D,), jnp.float32), 0.099609375, 1.8984375).astype(jnp.bfloat16),
        "shift_two": normal_values(key_of[17], (D,), 0.3, 4.0, ((0, 32),)),
        "w_time": normal_values(key_of[18], (D,), 1 ** -0.5, 6.0, ((0, 32),)),
        "b_time": normal_values(key_of[19], (D,), 0.5, 6.0, ((0, 32),)),
        "cotangent": normal_values(key_of[20], (NSEQ, LEN, D), 1.0, 6.0, ((0, 8), (1, 4))),
    }


EPSILON = 1e-05
NEGATIVE = -1e+30
PRECISE = lax.Precision.HIGHEST

@jax.custom_vjp
def low(v):
    return lax.optimization_barrier(v.astype(jnp.bfloat16)).astype(jnp.float32)

@jax.custom_vjp
def low_back(v):
    return v

def low_keep(v):
    return (low(v), None)

def low_pass(kept, grad):
    return (grad,)

def back_keep(v):
    return (v, None)

def back_low(kept, grad):
    return (low(grad),)
low.defvjp(low_keep, low_pass)
low_back.defvjp(back_keep, back_low)

def segment_of(lengths, positions):
    item_ends = jnp.cumsum(lengths, axis=1, dtype=jnp.int32)
    reached = (item_ends[:, None, :] <= positions[None, :, None]).astype(jnp.int32)
    return lax.optimization_barrier(jnp.sum(reached, axis=2, dtype=jnp.int32))

def step_scale(segment, timesteps):
    slot_ids = jnp.arange(timesteps.shape[1], dtype=jnp.int32)
    member = (segment[:, :, None] == slot_ids[None, None, :]).astype(jnp.float32)
    return lax.optimization_barrier(jnp.sum(member * timesteps[:, None, :].astype(jnp.float32), axis=2)) / TSTEPS

def product(left, right):
    return jnp.dot(left, right, precision=PRECISE)

def norm_rows(residual, norm_gain, norm_shift):
    center = residual - lax.optimization_barrier(jnp.mean(residual, axis=-1, keepdims=True))
    variance = lax.optimization_barrier(jnp.mean(center * center, axis=-1, keepdims=True))
    return center * lax.rsqrt(variance + EPSILON) * norm_gain + norm_shift

def split_heads(matrix):
    return jnp.transpose(matrix.reshape(matrix.shape[0], HEADS, HD), (1, 0, 2))

def one_sequence(tokens_seq, tau_seq, segment_seq, params):
    query_weight, query_bias, key_weight, value_weight, value_bias, out_weight, out_bias, first_gain, first_shift, up_weight, up_bias, down_weight, down_bias, second_gain, second_shift, time_weight, time_bias = params
    start = tokens_seq + tau_seq[:, None] * time_weight[None, :] + time_bias[None, :]
    start_low = low(start)
    queries = low_back(low((product(start_low, query_weight) + query_bias) * HD ** (-0.5)))
    keys_seq = low_back(low(product(start_low, key_weight)))
    values_seq = low_back(low(product(start_low, value_weight) + value_bias))
    same_item = segment_seq[:, None] == segment_seq[None, :]

    def one_head(operands):
        single_query_head, single_key_head, single_value_head = operands
        attention_scores = jnp.einsum('qd,kd->qk', single_query_head, single_key_head, precision=PRECISE)
        attention_scores = jnp.where(same_item, low_back(attention_scores), NEGATIVE)
        raised = jnp.exp(attention_scores - lax.optimization_barrier(jnp.max(attention_scores, axis=1, keepdims=True)))
        weights_p = raised / lax.optimization_barrier(jnp.sum(raised, axis=1, keepdims=True))
        return jnp.einsum('qk,kd->qd', low(weights_p), single_value_head, precision=PRECISE)
    stacked = lax.map(jax.checkpoint(one_head), (split_heads(queries), split_heads(keys_seq), split_heads(values_seq)))
    attended_context = jnp.transpose(stacked, (1, 0, 2)).reshape(tokens_seq.shape[0], HEADS * HD)
    attended_context = low_back(low(attended_context))
    attn_out = low_back(product(attended_context, out_weight) + out_bias)
    first = norm_rows(start + attn_out, first_gain, first_shift)
    up_pre = low_back(product(low(first), up_weight) + up_bias)
    activ = jax.nn.gelu(up_pre, approximate=False)
    down_out = low_back(product(low(activ), down_weight) + down_bias)
    return norm_rows(first + down_out, second_gain, second_shift)

def reference(tokens, lengths, timesteps, w_query, b_query, w_key, w_value, b_value, w_out, b_out, gain_one, shift_one, w_up, b_up, w_down, b_down, gain_two, shift_two, w_time, b_time, cotangent):
    positions = jnp.arange(LEN, dtype=jnp.int32)
    segment = segment_of(lengths, positions)
    tau = step_scale(segment, timesteps)
    params = tuple((weight.astype(jnp.float32) for weight in (w_query, b_query, w_key, w_value, b_value, w_out, b_out, gain_one, shift_one, w_up, b_up, w_down, b_down, gain_two, shift_two, w_time, b_time)))

    def whole_layer(tokens_in, params_in):

        def per_sequence(carry, operands):
            return (carry, one_sequence(operands[0], operands[1], operands[2], params_in))
        unused, result = lax.scan(per_sequence, jnp.zeros((), jnp.float32), (tokens_in, tau, segment))
        return result
    output, pull_back = jax.vjp(whole_layer, tokens.astype(jnp.float32), params)
    grad_tokens, grads = pull_back(cotangent.astype(jnp.float32))
    grad_w_query, grad_b_query, grad_w_key, grad_w_value, grad_b_value, grad_w_out, grad_b_out, grad_gain_one, grad_shift_one, grad_w_up, grad_b_up, grad_w_down, grad_b_down, grad_gain_two, grad_shift_two, grad_w_time, grad_b_time = grads
    return (output.astype(jnp.bfloat16), grad_tokens.astype(jnp.bfloat16), grad_w_query, grad_b_query, grad_w_key, grad_w_value, grad_b_value, grad_w_out, grad_b_out, grad_gain_one, grad_shift_one, grad_w_up, grad_b_up, grad_w_down, grad_b_down, grad_gain_two, grad_shift_two, grad_w_time, grad_b_time)
```

```python
import functools

import jax
import jax.numpy as jnp
from jax import lax
from jax.experimental import pallas as pl
from jax.experimental.pallas import tpu as pltpu
from jax.sharding import PartitionSpec as P

HD = 64
TSTEPS = 5000
EPSILON = 1e-05
NEGATIVE = -1e30
ROOT_HALF = 0.7071067811865476
DENSITY_SCALE = 0.3989422804014327
PAD = 16
WIDE = 512
BF16 = jnp.bfloat16
F32 = jnp.float32
VMEM = pltpu.VMEM
SMEM = pltpu.SMEM


def nn(a, b):
    return lax.dot_general(a, b, (((1,), (0,)), ((), ())), preferred_element_type=F32)


def nt(a, b):
    return lax.dot_general(a, b, (((1,), (1,)), ((), ())), preferred_element_type=F32)


def vspec():
    return pl.BlockSpec(memory_space=VMEM)


def sspec():
    return pl.BlockSpec(memory_space=SMEM)


def aspec():
    return pl.BlockSpec(memory_space=pl.ANY)


def params(mib, grid=0):
    if grid:
        return pltpu.CompilerParams(
            vmem_limit_bytes=mib << 20, dimension_semantics=("arbitrary",) * grid
        )
    return pltpu.CompilerParams(vmem_limit_bytes=mib << 20)


def cost(flops, nbytes, trans=0):
    return pl.CostEstimate(flops=int(flops), bytes_accessed=int(nbytes), transcendentals=int(trans))


def tau_rows(len_ref, tim_ref, seq, first, rows):
    spot = first + lax.broadcasted_iota(jnp.int32, (rows, 128), 0)
    begin = jnp.int32(0)
    step = jnp.zeros((rows, 128), jnp.int32)
    for i in range(len_ref.shape[1]):
        end = begin + len_ref[seq, i]
        step = jnp.where((spot >= begin) & (spot < end), tim_ref[seq, i], step)
        begin = end
    return (step.astype(F32) / TSTEPS)[:, :1]


def segments(len_ref, seq, spot):
    end = jnp.int32(0)
    found = jnp.zeros(spot.shape, jnp.int32)
    for i in range(len_ref.shape[1]):
        end = end + len_ref[seq, i]
        found = found + (spot >= end).astype(jnp.int32)
    return found


def item_bias(len_ref, seq, first, keys, rows, out_ref):
    mine = segments(len_ref, seq, first + lax.broadcasted_iota(jnp.int32, (8, rows), 1))
    theirs = segments(len_ref, seq, lax.broadcasted_iota(jnp.int32, (keys, 128), 0))
    for lane in range(rows // 128):
        same = theirs == mine[:1, lane * 128 : (lane + 1) * 128]
        out_ref[:, lane * 128 : (lane + 1) * 128] = jnp.where(same, 0.0, NEGATIVE)


def fold(block):
    rows, width = block.shape
    return block.reshape(rows // 8, 8, width)


def qkv_kernel(ns, nz, r, len_ref, tim_ref, idx, *refs):
    toks = refs[:ns]
    qa, qb = refs[ns : ns + 2]
    q_ref, k_ref, v_ref, low_ref, w_ref, small_ref, bup_ref = refs[ns + 2 : ns + 9]
    wide = refs[ns + 9]
    z, c, j = idx[0], idx[1], idx[2]
    ndev = ns * nz * 2
    seqs, rows, model = toks[0].shape
    hg = q_ref.shape[2]
    for cc, src in enumerate((qa, qb)):
        for a in range(nz):
            for b in range(ns):
                d = ((z ^ a) * 2 + (c ^ cc)) * ns + (j ^ b)
                wide[pl.ds(pl.multiple_of(d * r, r), r), :] = src[a, b, PAD : PAD + r, :].astype(
                    wide.dtype
                )
    w_ref[...] = wide[...].astype(BF16)
    lanes = 14 * r
    count = nz * ns * PAD
    by_owner = jnp.zeros((ndev, lanes), F32)
    for cc, src in enumerate((qa, qb)):
        col = lax.broadcasted_iota(jnp.int32, (ndev, count), 1)
        row = lax.broadcasted_iota(jnp.int32, (ndev, count), 0)
        a = col // (ns * PAD)
        b = (col // PAD) % ns
        d = ((z ^ a) * 2 + (c ^ cc)) * ns + (j ^ b)
        pick = jnp.where((d == row) & (col % PAD == 0), 1.0, 0.0).astype(BF16)
        piece = src[:, :, 0:PAD, :].reshape(count, 3 * hg)
        by_owner = by_owner + nn(pick, piece)[:, :lanes]
    by_owner = by_owner.astype(BF16)

    def whole(part, width):
        i = lax.broadcasted_iota(jnp.int32, (width, ndev * width), 0)
        l = lax.broadcasted_iota(jnp.int32, (width, ndev * width), 1)
        spread = nn(part, jnp.where(l % width == i, 1.0, 0.0).astype(BF16))
        d = lax.broadcasted_iota(jnp.int32, (ndev, ndev * width), 0)
        l = lax.broadcasted_iota(jnp.int32, (ndev, ndev * width), 1)
        return jnp.sum(jnp.where(l // width == d, spread, 0.0), axis=0, keepdims=True)

    for g in range(10):
        small_ref[g : g + 1, :] = whole(by_owner[:, g * r : (g + 1) * r], r)
    small_ref[10:16, :] = jnp.zeros((6, model), F32)
    bup_ref[...] = jnp.broadcast_to(whole(by_owner[:, 10 * r :], 4 * r), bup_ref.shape)
    heads = pl.ds(pl.multiple_of(j * hg, 128), hg)
    bq = small_ref[0:1, heads]
    bv = small_ref[1:2, heads]
    wt = small_ref[8:9, :]
    bt = small_ref[9:10, :]
    for k in range(ns):
        first = pl.multiple_of((j ^ k) * rows, rows)
        here = pl.ds(first, rows)
        for s in range(seqs):
            tau = tau_rows(len_ref, tim_ref, s, first, rows)
            low = (toks[k][s].astype(F32) + tau * wt + bt).astype(BF16)
            low_ref[s, here, :] = low
            got = nn(low, w_ref[...])
            q_ref[s, here, :] = ((got[:, :hg] + bq) * (HD**-0.5)).astype(BF16)
            k_ref[s, here, :] = got[:, hg : 2 * hg].astype(BF16)
            v_ref[s, here, :] = (got[:, 2 * hg :] + bv).astype(BF16)


def project(ns, nz, lengths, timesteps, idx, toks, qa, qb):
    seqs, rows, model = toks[0].shape
    r = qa.shape[2] - PAD
    hg = qa.shape[3] // 3
    full = rows * ns
    heads = jax.ShapeDtypeStruct((seqs, full, hg), BF16)
    outs = [
        heads,
        heads,
        heads,
        jax.ShapeDtypeStruct((seqs, full, model), BF16),
        jax.ShapeDtypeStruct((model, 3 * hg), BF16),
        jax.ShapeDtypeStruct((16, model), F32),
        jax.ShapeDtypeStruct((8, 4 * model), F32),
    ]
    return pl.pallas_call(
        functools.partial(qkv_kernel, ns, nz, r),
        name="project",
        out_shape=outs,
        in_specs=[sspec()] * 3 + [vspec()] * (ns + 2),
        out_specs=[vspec()] * 7,
        scratch_shapes=[VMEM((model, 3 * hg), BF16 if r % 16 == 0 else F32)],
        compiler_params=params(40),
        cost_estimate=cost(2 * seqs * full * model * 3 * hg, 14 << 20),
    )(lengths, timesteps, idx, *toks, qa, qb)


def attend_kernel(ns, len_ref, idx, q_ref, k_ref, v_ref, *refs):
    ctx_refs = refs[:ns]
    ctxt_ref, lse_ref, kh, vt, bias, score = refs[ns:]
    s, i = pl.program_id(0), pl.program_id(1)
    j = idx[2]
    keys, hg = k_ref.shape[1:]
    rows = q_ref.shape[1]
    heads = hg // HD
    step = 256

    @pl.when(i == 0)
    def _():
        for h in range(heads):
            kh[h] = k_ref[0, :, h * HD : (h + 1) * HD]
        vt[...] = v_ref[0].T

    item_bias(len_ref, s, i * rows, keys, rows, bias)
    lse_ref[0] = jnp.zeros(lse_ref.shape[1:], F32)
    parts = []
    for h in range(heads):
        qh = q_ref[0, :, h * HD : (h + 1) * HD]
        top = jnp.full((8, rows), NEGATIVE, F32)
        for b in range(keys // step):
            at = slice(b * step, (b + 1) * step)
            st = nt(kh[h, at, :], qh) + bias[at, :]
            score[h % 2, at, :] = st
            top = jnp.maximum(top, jnp.max(fold(st), axis=0))
        top = jnp.max(top, axis=0, keepdims=True)
        total = jnp.zeros((8, rows), F32)
        acc = jnp.zeros((HD, rows), F32)
        for b in range(keys // step):
            at = slice(b * step, (b + 1) * step)
            p = jnp.exp(score[h % 2, at, :] - top)
            total = total + jnp.sum(fold(p), axis=0)
            acc = acc + nn(vt[h * HD : (h + 1) * HD, at], p.astype(BF16))
        total = jnp.sum(total, axis=0, keepdims=True)
        acc = acc / total
        ctxt_ref[0, h * HD : (h + 1) * HD, :] = acc
        lse_ref[0, h : h + 1, :] = top + jnp.log(total)
        parts.append(acc)
    done = jnp.concatenate(parts, axis=0).T.astype(BF16)
    for k in range(ns):

        @pl.when((j ^ k) == i)
        def _():
            ctx_refs[k][s] = done


def attend(ns, lengths, idx, q, k, v):
    seqs, full, hg = q.shape
    rows = full // ns
    heads = hg // HD
    outs = [jax.ShapeDtypeStruct((seqs, rows, hg), BF16)] * ns + [
        jax.ShapeDtypeStruct((seqs, hg, full), F32),
        jax.ShapeDtypeStruct((seqs, 8, full), F32),
    ]
    whole = pl.BlockSpec((seqs, rows, hg), lambda s, i: (0, 0, 0))
    keyed = pl.BlockSpec((1, full, hg), lambda s, i: (s, 0, 0))
    res = pl.pallas_call(
        functools.partial(attend_kernel, ns),
        name="attend",
        out_shape=outs,
        grid=(seqs, ns),
        in_specs=[
            sspec(),
            sspec(),
            pl.BlockSpec((1, rows, hg), lambda s, i: (s, i, 0)),
            keyed,
            keyed,
        ],
        out_specs=[whole] * ns
        + [
            pl.BlockSpec((1, hg, rows), lambda s, i: (s, 0, i)),
            pl.BlockSpec((1, 8, rows), lambda s, i: (s, 0, i)),
        ],
        scratch_shapes=[
            VMEM((heads, full, HD), BF16),
            VMEM((hg, full), BF16),
            VMEM((full, rows), F32),
            VMEM((2, full, rows), F32),
        ],
        compiler_params=params(40, 2),
        cost_estimate=cost(
            4 * 4 * seqs * full * full * hg, 8 << 20, seqs * full * full * heads
        ),
    )(lengths, idx, q, k, v)
    return res[:ns], res[ns], res[ns + 1]


def attend_back_kernel(ns, seq, len_ref, tim_ref, idx, q_ref, k_ref, v_ref, ctxt_ref, lse_ref, w_ref, *refs):
    dctx = refs[:ns]
    grad_ref = refs[ns]
    p_refs = refs[ns + 1 : 2 * ns + 1]
    sum_ref, bsum_ref, kh, vh, kt, dcx, dk, dv, bias = refs[2 * ns + 1 :]
    i = pl.program_id(0)
    j = idx[2]
    keys, hg = k_ref.shape[1:]
    rows = q_ref.shape[1]
    heads = hg // HD
    step = 256

    @pl.when(i == 0)
    def _():
        for h in range(heads):
            kh[h] = k_ref[0, :, h * HD : (h + 1) * HD]
            vh[h] = v_ref[0, :, h * HD : (h + 1) * HD]
        kt[...] = k_ref[0].T
        for k in range(ns):
            dcx[pl.ds(pl.multiple_of((j ^ k) * rows, rows), rows), :] = dctx[k][0]
        dk[...] = jnp.zeros_like(dk)
        dv[...] = jnp.zeros_like(dv)

    item_bias(len_ref, seq, i * rows, keys, rows, bias)
    here = pl.ds(pl.multiple_of(i * rows, rows), rows)
    dc = dcx[here, :]
    dct = dc.T.astype(F32)
    parts = []
    for h in range(heads):
        cols = slice(h * HD, (h + 1) * HD)
        qh = q_ref[0, :, cols]
        dch = dc[:, cols]
        row_total = jnp.sum(ctxt_ref[0, cols, :] * dct[cols, :], axis=0, keepdims=True)
        lse = lse_ref[0, h : h + 1, :]
        acc = jnp.zeros((HD, rows), F32)
        for b in range(keys // step):
            at = slice(b * step, (b + 1) * step)
            p = jnp.exp(nt(kh[h, at, :], qh) + bias[at, :] - lse)
            dp = nt(vh[h, at, :], dch)
            ds = (p * (dp - row_total)).astype(BF16)
            dv[h, at, :] += nn(p.astype(BF16), dch)
            dk[h, at, :] += nn(ds, qh)
            acc = acc + nn(kt[cols, at], ds)
        parts.append(acc)
    dq = jnp.concatenate(parts, axis=0).T.astype(BF16).astype(F32) * (HD**-0.5)
    grad_ref[here, 0:hg] = dq.astype(BF16)

    @pl.when(i == ns - 1)
    def _():
        for h in range(heads):
            grad_ref[:, hg + h * HD : hg + (h + 1) * HD] = dk[h].astype(BF16)
            grad_ref[:, 2 * hg + h * HD : 2 * hg + (h + 1) * HD] = dv[h].astype(BF16)
        plain = jnp.zeros((8, w_ref.shape[0]), F32)
        timed = jnp.zeros((8, w_ref.shape[0]), F32)
        bias_sum = jnp.zeros((8, 3 * hg), F32)
        for k in range(ns):
            first = pl.multiple_of((j ^ k) * rows, rows)
            block = grad_ref[pl.ds(first, rows), :]
            part = nt(block, w_ref[...])
            p_refs[k][...] = part.astype(BF16)
            plain = plain + jnp.sum(fold(part), axis=0)
            tau = tau_rows(len_ref, tim_ref, seq, first, rows)
            timed = timed + jnp.sum(fold(part * tau), axis=0)
            bias_sum = bias_sum + jnp.sum(fold(block.astype(F32)), axis=0)
        sum_ref[...] = jnp.zeros_like(sum_ref)
        sum_ref[0:1, :] = jnp.sum(timed, axis=0, keepdims=True)
        sum_ref[1:2, :] = jnp.sum(plain, axis=0, keepdims=True)
        bsum_ref[...] = jnp.broadcast_to(jnp.sum(bias_sum, axis=0, keepdims=True), bsum_ref.shape)


def attend_back(ns, seq, lengths, timesteps, idx, q, k, v, ctxt, lse, w, dctx):
    seqs, full, hg = q.shape
    rows = full // ns
    heads = hg // HD
    model = w.shape[0]
    one = lambda shape: pl.BlockSpec(shape, lambda i: (0,) * len(shape))
    keyed = pl.BlockSpec((1, full, hg), lambda i: (seq, 0, 0))
    outs = (
        [jax.ShapeDtypeStruct((full, 3 * hg), BF16)]
        + [jax.ShapeDtypeStruct((rows, model), BF16)] * ns
        + [jax.ShapeDtypeStruct((8, model), F32), jax.ShapeDtypeStruct((8, 3 * hg), F32)]
    )
    res = pl.pallas_call(
        functools.partial(attend_back_kernel, ns, seq),
        name="attend_back",
        out_shape=outs,
        grid=(ns,),
        in_specs=[sspec()] * 3
        + [
            pl.BlockSpec((1, rows, hg), lambda i: (seq, i, 0)),
            keyed,
            keyed,
            pl.BlockSpec((1, hg, rows), lambda i: (seq, 0, i)),
            pl.BlockSpec((1, 8, rows), lambda i: (seq, 0, i)),
            one((model, 3 * hg)),
        ]
        + [pl.BlockSpec((1, rows, hg), lambda i: (seq, 0, 0))] * ns,
        out_specs=[one((full, 3 * hg))]
        + [one((rows, model))] * ns
        + [one((8, model)), one((8, 3 * hg))],
        scratch_shapes=[
            VMEM((heads, full, HD), BF16),
            VMEM((heads, full, HD), BF16),
            VMEM((hg, full), BF16),
            VMEM((full, hg), BF16),
            VMEM((heads, full, HD), F32),
            VMEM((heads, full, HD), F32),
            VMEM((full, rows), F32),
        ],
        compiler_params=params(48, 1),
        cost_estimate=cost(
            10 * 4 * full * full * hg + 2 * full * model * 3 * hg,
            10 << 20,
            full * full * heads,
        ),
    )(lengths, timesteps, idx, q, k, v, ctxt, lse, w, *dctx)
    return res[0], res[1 : ns + 1], res[ns + 1], res[ns + 2]


def middle_kernel(ns, nz, r, rels, len_ref, tim_ref, idx, tok_ref, cot_ref, small_ref, bup_ref, *refs):
    ctxs = refs[:ns]
    nu = len(rels[0])
    u1 = refs[ns : ns + nu]
    u2 = refs[ns + nu : ns + 2 * nu]
    dn = refs[ns + 2 * nu : ns + 2 * nu + 2 * nz]
    rest = refs[ns + 2 * nu + 2 * nz :]
    out_ref, act_o, dg_o, ug_o, fl_o, cx_o, ag_o, r1_o = rest[:8]
    dctx = rest[8 : 8 + ns]
    sum_ref, gbup_ref = rest[8 + ns : 10 + ns]
    wu, wd, act, slope, ug, fl, cx, dg, first, norm, r2, inv, stage, wsem, osem = rest[10 + ns :]
    z, c, j = idx[0], idx[1], idx[2]
    seqs, rows, model = tok_ref.shape
    ff = wd.shape[0]
    hg = ctxs[0].shape[2]
    tokens = seqs * rows
    half = wu.shape[1] // 2
    for part, (arrays, rel) in enumerate(((u1, rels[0]), (u2, rels[1]))):
        for src, (cc, offs) in zip(arrays, rel):
            for m, b in enumerate(offs):
                for a in range(nz):
                    d = ((z ^ a) * 2 + (c ^ cc)) * ns + (j ^ b)
                    pltpu.make_async_copy(
                        src.at[m, a],
                        wu.at[pl.ds(pl.multiple_of(d * r, r), r), pl.ds(part * half, half)],
                        wsem.at[part],
                    ).start()
    for n, src in enumerate(dn):
        t, cc = n // 2, n % 2
        for m, b in enumerate(rels[2]):
            d = (lax.rem(z + nz - t, nz) * 2 + (c ^ cc)) * ns + (j ^ b)
            pltpu.make_async_copy(
                src.at[m],
                wd.at[pl.ds(pl.multiple_of(d * 4 * r, 4 * r), 4 * r), :],
                wsem.at[2],
            ).start()
    for k in range(ns):
        at = pl.ds(pl.multiple_of((j ^ k) * hg, 128), hg)
        for s in range(seqs):
            cx[s * rows : (s + 1) * rows, at] = ctxs[k][s]
    sum_ref[...] = jnp.zeros_like(sum_ref)
    pltpu.make_async_copy(cx, cx_o, osem.at[0]).start()
    u1_all = wu.at[:, pl.ds(0, half)]
    pltpu.make_async_copy(u1_all, u1_all, wsem.at[0]).wait()

    b_out = small_ref[2:3, :]
    gain_one, shift_one = small_ref[3:4, :], small_ref[4:5, :]
    b_down = small_ref[5:6, :]
    gain_two, shift_two = small_ref[6:7, :], small_ref[7:8, :]
    w_time, b_time = small_ref[8:9, :], small_ref[9:10, :]
    block = 128
    per = rows // block

    def add_sum(row, value):
        sum_ref[row : row + 1, :] += jnp.sum(jnp.sum(fold(value), axis=0), axis=0, keepdims=True)

    def mean(value):
        return jnp.sum(value, axis=-1, keepdims=True) * (1.0 / model)

    def one_first(s, b):
        at = pl.ds(pl.multiple_of((s * per + b) * block, block), block)
        inside = pl.ds(pl.multiple_of(b * block, block), block)
        attn = nn(cx[at, :], wu[:, 0:model])
        tau = tau_rows(len_ref, tim_ref, s, j * rows + b * block, block)
        start = tok_ref[s, inside, :].astype(F32) + tau * w_time + b_time
        res = start + (attn + b_out)
        center = res - mean(res)
        inverse = lax.rsqrt(mean(center * center) + EPSILON)
        normed = center * inverse
        norm[at, :] = normed
        inv[at, :] = jnp.broadcast_to(inverse, (block, 128))
        value = normed * gain_one + shift_one
        first[at, :] = value
        fl[at, :] = value.astype(BF16)

    for s in range(seqs):
        lax.fori_loop(0, per, lambda b, _: (one_first(s, b), 0)[1], 0)
    pltpu.make_async_copy(fl, fl_o, osem.at[1]).start()
    u2_all = wu.at[:, pl.ds(half, half)]
    pltpu.make_async_copy(u2_all, u2_all, wsem.at[1]).wait()

    def one_up(n, _):
        at = pl.ds(pl.multiple_of(n * WIDE, WIDE), WIDE)
        wat = pl.ds(pl.multiple_of(model + n * WIDE, WIDE), WIDE)
        for h in range(2):
            rr = slice(h * tokens // 2, (h + 1) * tokens // 2)
            pre = nn(fl[rr, :], wu[:, wat]) + bup_ref[0:1, at]
            cumulative = 0.5 * (1.0 + lax.erf(pre * ROOT_HALF))
            density = jnp.exp(-0.5 * pre * pre) * DENSITY_SCALE
            act[rr, at] = (pre * cumulative).astype(BF16)
            slope[rr, at] = cumulative + pre * density
        return 0

    lax.fori_loop(0, ff // WIDE, one_up, 0)
    pltpu.make_async_copy(act, act_o, osem.at[2]).start()
    pltpu.make_async_copy(wd, wd, wsem.at[2]).wait()

    def one_second(s, b):
        at = pl.ds(pl.multiple_of((s * per + b) * block, block), block)
        inside = pl.ds(pl.multiple_of(b * block, block), block)
        res = first[at, :] + (nn(act[at, :], wd[...]) + b_down)
        center = res - mean(res)
        inverse = lax.rsqrt(mean(center * center) + EPSILON)
        normed = center * inverse
        out_ref[s, inside, :] = (normed * gain_two + shift_two).astype(BF16)
        g = cot_ref[s, inside, :].astype(F32)
        add_sum(4, g * normed)
        add_sum(5, g)
        gn = g * gain_two
        grad = inverse * (gn - mean(gn) - normed * mean(gn * normed))
        r2[at, :] = grad
        low = grad.astype(BF16)
        dg[at, :] = low
        add_sum(3, low.astype(F32))

    for s in range(seqs):
        lax.fori_loop(0, per, lambda b, _: (one_second(s, b), 0)[1], 0)
    pltpu.make_async_copy(dg, dg_o, osem.at[3]).start()

    def one_up_grad(n, _):
        at = pl.ds(pl.multiple_of(n * WIDE, WIDE), WIDE)
        total = jnp.zeros((8, WIDE), F32)
        for h in range(2):
            rr = slice(h * tokens // 2, (h + 1) * tokens // 2)
            low = (nt(dg[rr, :], wd[at, :]) * slope[rr, at]).astype(BF16)
            ug[rr, at] = low
            total = total + jnp.sum(fold(low.astype(F32)), axis=0)
        gbup_ref[:, at] = jnp.broadcast_to(jnp.sum(total, axis=0, keepdims=True), (8, WIDE))
        return 0

    lax.fori_loop(0, ff // WIDE, one_up_grad, 0)
    pltpu.make_async_copy(ug, ug_o, osem.at[4]).start()
    pltpu.make_async_copy(fl, fl_o, osem.at[1]).wait()

    def one_first_grad(s, b):
        at = pl.ds(pl.multiple_of((s * per + b) * block, block), block)
        inside = pl.ds(pl.multiple_of(b * block, block), block)
        fg = nt(ug[at, :], wu[:, model:]) + r2[at, :]
        normed = norm[at, :]
        add_sum(1, fg * normed)
        add_sum(2, fg)
        gn = fg * gain_one
        grad = inv[at, :][:, :1] * (gn - mean(gn) - normed * mean(gn * normed))
        first[at, :] = grad
        low = grad.astype(BF16)
        fl[at, :] = low
        add_sum(0, low.astype(F32))
        tau = tau_rows(len_ref, tim_ref, s, j * rows + b * block, block)
        add_sum(6, grad * tau)
        add_sum(7, grad)
        stage[...] = nt(low, wu[:, 0:model]).astype(BF16)
        for k in range(ns):
            cols = pl.ds(pl.multiple_of((j ^ k) * hg, 128), hg)
            dctx[k][s, inside, :] = stage[:, cols]

    for s in range(seqs):
        lax.fori_loop(0, per, lambda b, _: (one_first_grad(s, b), 0)[1], 0)
    ag_copy = pltpu.make_async_copy(fl, ag_o, osem.at[5])
    ag_copy.start()
    r1_copy = pltpu.make_async_copy(first, r1_o, osem.at[6])
    r1_copy.start()
    pltpu.make_async_copy(cx, cx_o, osem.at[0]).wait()
    pltpu.make_async_copy(act, act_o, osem.at[2]).wait()
    pltpu.make_async_copy(dg, dg_o, osem.at[3]).wait()
    pltpu.make_async_copy(ug, ug_o, osem.at[4]).wait()
    ag_copy.wait()
    r1_copy.wait()


def middle(ns, nz, r, rels, lengths, timesteps, idx, tokens, cotangent, small, bup, ctxs, u1, u2, dn):
    seqs, rows, model = tokens.shape
    total = seqs * rows
    ff = bup.shape[1]
    hg = ctxs[0].shape[2]
    sh = lambda *a: jax.ShapeDtypeStruct(a[:-1], a[-1])
    outs = [
        sh(seqs, rows, model, BF16),
        sh(total, ff, BF16),
        sh(total, model, BF16),
        sh(total, ff, BF16),
        sh(total, model, BF16),
        sh(total, model, BF16),
        sh(total, model, BF16),
        sh(total, model, F32),
    ]
    outs += [sh(seqs, rows, hg, BF16)] * ns + [sh(16, model, F32), sh(8, ff, F32)]
    res = pl.pallas_call(
        functools.partial(middle_kernel, ns, nz, r, rels),
        name="middle",
        out_shape=outs,
        in_specs=[sspec()] * 3
        + [vspec()] * (4 + ns)
        + [aspec()] * (len(u1) + len(u2) + len(dn)),
        out_specs=[vspec()] + [aspec()] * 7 + [vspec()] * (ns + 2),
        scratch_shapes=[
            VMEM((model, model + ff), BF16),
            VMEM((ff, model), BF16),
            VMEM((total, ff), BF16),
            VMEM((total, ff), F32),
            VMEM((total, ff), BF16),
            VMEM((total, model), BF16),
            VMEM((total, model), BF16),
            VMEM((total, model), BF16),
            VMEM((total, model), F32),
            VMEM((total, model), F32),
            VMEM((total, model), F32),
            VMEM((total, 128), F32),
            VMEM((128, model), BF16),
            pltpu.SemaphoreType.DMA((3,)),
            pltpu.SemaphoreType.DMA((7,)),
        ],
        compiler_params=params(54),
        cost_estimate=cost(
            2 * total * (2 * model * model + 4 * model * ff), 40 << 20, 3 * total * ff
        ),
    )(lengths, timesteps, idx, tokens, cotangent, small, bup, *ctxs, *u1, *u2, *dn)
    return res[:8], res[8 : 8 + ns], res[8 + ns], res[9 + ns]


def scatter_rows(ns, nz, r, ring, idx, total, keep_ref, send_ref):
    z, c, j = idx[0], idx[1], idx[2]
    for cc, dst in enumerate((keep_ref, send_ref)):
        for a in range(nz):
            owner = lax.rem(z + a, nz) if ring else z ^ a
            for b in range(ns):
                d = (owner * 2 + (c ^ cc)) * ns + (j ^ b)
                dst[a, b] = total[pl.ds(pl.multiple_of(d * r, r), r), :].astype(BF16)


def up_grad_kernel(ns, nz, r, split, idx, *refs):
    if split:
        cx_ref, ag_ref, fl_ref, ug_ref, keep_ref, send_ref, flipped, total = refs
    else:
        fl_ref, ug_ref, keep_ref, send_ref, flipped, total = refs
    i = pl.program_id(0)
    if split:

        @pl.when(i == 0)
        def _():
            flipped[...] = cx_ref[...].T

        @pl.when(i < split)
        def _():
            at = pl.ds(pl.multiple_of(jnp.minimum(i, split - 1) * WIDE, WIDE), WIDE)
            total[...] = nn(flipped[...], ag_ref[:, at])

    @pl.when(i == split)
    def _():
        flipped[...] = fl_ref[...].T

    @pl.when(i >= split)
    def _():
        total[...] = nn(flipped[...], ug_ref[...])

    scatter_rows(ns, nz, r, False, idx, total, keep_ref, send_ref)


def up_grad(ns, nz, r, idx, cx, ag, fl, ug, part):
    total, model = fl.shape
    ff = ug.shape[1]
    width = (model + ff) // 2
    split = model // WIDE if part == 0 else 0
    skip = 0 if part == 0 else width // WIDE - model // WIDE
    one = lambda shape: pl.BlockSpec(shape, lambda i: (0,) * len(shape))
    block = pl.BlockSpec((nz, ns, r, WIDE), lambda i: (0, 0, 0, i))
    ins = ([cx, ag] if part == 0 else []) + [fl, ug]
    return pl.pallas_call(
        functools.partial(up_grad_kernel, ns, nz, r, split),
        name="up_grad",
        out_shape=[jax.ShapeDtypeStruct((nz, ns, r, width), BF16)] * 2,
        grid=(width // WIDE,),
        in_specs=[sspec()]
        + [one((total, model))] * (len(ins) - 1)
        + [pl.BlockSpec((total, WIDE), lambda i: (0, jnp.maximum(i - split, 0) + skip))],
        out_specs=[block, block],
        scratch_shapes=[VMEM((model, total), BF16), VMEM((model, WIDE), F32)],
        compiler_params=params(40, 1),
        cost_estimate=cost(2 * total * model * width, 10 << 20),
    )(idx, *ins)


def down_grad_kernel(ns, nz, r, idx, act_ref, dg_ref, keep_ref, send_ref, flipped, total):
    @pl.when(pl.program_id(0) == 0)
    def _():
        flipped[...] = act_ref[...].T

    total[...] = nn(flipped[...], dg_ref[...])
    scatter_rows(ns, nz, 4 * r, True, idx, total, keep_ref, send_ref)


def down_grad(ns, nz, r, idx, act, dg):
    total, ff = act.shape
    model = dg.shape[1]
    width = 256
    block = pl.BlockSpec((nz, ns, 4 * r, width), lambda i: (0, 0, 0, i))
    return pl.pallas_call(
        functools.partial(down_grad_kernel, ns, nz, r),
        name="down_grad",
        out_shape=[jax.ShapeDtypeStruct((nz, ns, 4 * r, model), BF16)] * 2,
        grid=(model // width,),
        in_specs=[
            sspec(),
            pl.BlockSpec((total, ff), lambda i: (0, 0)),
            pl.BlockSpec((total, width), lambda i: (0, i)),
        ],
        out_specs=[block, block],
        scratch_shapes=[VMEM((ff, total), BF16), VMEM((ff, width), F32)],
        compiler_params=params(40, 1),
        cost_estimate=cost(2 * total * model * ff, 14 << 20),
    )(idx, act, dg)


def qkv_grad_kernel(ns, nz, r, idx, low_ref, g0_ref, g1_ref, sums_ref, gbup_ref, s0_ref, s1_ref, b0_ref, b1_ref, keep_ref, send_ref, total, own, vec):
    z, c, j = idx[0], idx[1], idx[2]
    ndev = ns * nz * 2
    model = low_ref.shape[2]
    hg = g0_ref.shape[1] // 3
    total[...] = nn(low_ref[0].T, g0_ref[...]) + nn(low_ref[1].T, g1_ref[...])
    vec[...] = jnp.zeros_like(vec)
    heads = pl.ds(pl.multiple_of(j * hg, 128), hg)
    both = b0_ref[0:1, :] + b1_ref[0:1, :]
    vec[0:1, heads] = both[:, :hg]
    vec[1:2, heads] = both[:, 2 * hg :]
    vec[2:8, :] = sums_ref[0:6, :]
    vec[8:10, :] = sums_ref[6:8, :] + s0_ref[0:2, :] + s1_ref[0:2, :]
    own[...] = jnp.zeros_like(own)

    def split(row, width):
        d = lax.broadcasted_iota(jnp.int32, (ndev, ndev * width), 0)
        l = lax.broadcasted_iota(jnp.int32, (ndev, ndev * width), 1)
        spread = jnp.where(l // width == d, row, 0.0).astype(BF16)
        i = lax.broadcasted_iota(jnp.int32, (width, ndev * width), 0)
        l = lax.broadcasted_iota(jnp.int32, (width, ndev * width), 1)
        return nt(spread, jnp.where(l % width == i, 1.0, 0.0).astype(BF16))

    pieces = [split(vec[g : g + 1, :], r) for g in range(10)]
    pieces.append(split(gbup_ref[0:1, :], 4 * r))
    own[:, 0 : 14 * r] = jnp.concatenate(pieces, axis=1)
    for cc, dst in enumerate((keep_ref, send_ref)):
        for a in range(nz):
            for b in range(ns):
                d = ((z ^ a) * 2 + (c ^ cc)) * ns + (j ^ b)
                dst[a, b, PAD:, :] = total[pl.ds(pl.multiple_of(d * r, r), r), :].astype(BF16)
                dst[a, b, 0:PAD, :] = jnp.broadcast_to(
                    own[pl.ds(d, 1), :], (PAD, own.shape[1])
                ).astype(BF16)


def qkv_grad(ns, nz, r, idx, low, g0, g1, sums, gbup, s0, s1, b0, b1):
    seqs, full, model = low.shape
    width = g0.shape[1]
    out = jax.ShapeDtypeStruct((nz, ns, PAD + r, width), BF16)
    return pl.pallas_call(
        functools.partial(qkv_grad_kernel, ns, nz, r),
        name="qkv_grad",
        out_shape=[out, out],
        in_specs=[sspec()] + [vspec()] * 9,
        out_specs=[vspec()] * 2,
        scratch_shapes=[
            VMEM((model, width), F32),
            VMEM((ns * nz * 2, width), F32),
            VMEM((16, model), F32),
        ],
        compiler_params=params(40),
        cost_estimate=cost(2 * seqs * full * model * width, 12 << 20),
    )(idx, low, g0, g1, sums, gbup, s0, s1, b0, b1)


def finish_kernel(ns, r, idx, own_ref, *refs):
    others = refs[: ns - 1]
    q_ref, k_ref, v_ref, small_ref = refs[ns - 1 :]
    j = idx[2]
    hg = own_ref.shape[1] // 3
    small = own_ref[0:1, :]
    for k in range(ns):
        part = own_ref[...] if k == 0 else others[k - 1][...].astype(F32)
        cols = pl.ds(pl.multiple_of((j ^ k) * hg, 128), hg)
        for n, dst in enumerate((q_ref, k_ref, v_ref)):
            dst[:, cols] = part[PAD:, n * hg : (n + 1) * hg]
        if k:
            small = small + part[0:1, :]
    small_ref[...] = jnp.broadcast_to(small, small_ref.shape)


def finish(ns, r, model, idx, own, others):
    width = own.shape[1]
    out = jax.ShapeDtypeStruct((r, model), F32)
    return pl.pallas_call(
        functools.partial(finish_kernel, ns, r),
        name="finish",
        out_shape=[out, out, out, jax.ShapeDtypeStruct((8, width), F32)],
        in_specs=[sspec()] + [vspec()] * ns,
        out_specs=[vspec()] * 4,
        compiler_params=params(16),
    )(idx, own, *others)


def to_seq(value, k):
    ns = lax.axis_size("seq")
    return lax.ppermute(value, "seq", [(i, i ^ k) for i in range(ns)])


def to_mate(value):
    nd = lax.axis_size("dp")
    return lax.ppermute(value, "dp", [(i, i ^ 1) for i in range(nd)])


def to_z(value, a):
    nd = lax.axis_size("dp")
    return lax.ppermute(value, "dp", [(i, i ^ (2 * a)) for i in range(nd)])


def to_ring(value):
    nd = lax.axis_size("dp")
    return lax.ppermute(value, "dp", [(i, (i + 2) % nd) for i in range(nd)])


def bits_of(ns):
    return list(range(ns.bit_length() - 1))


def gather_direct(block, order, nz):
    cur = jnp.stack([block] + [to_z(block, a) for a in range(1, nz)])[None]
    for bit in order[:-1]:
        cur = jnp.concatenate([cur, to_seq(cur, 1 << bit)], axis=0)
    last = to_seq(cur, 1 << order[-1])
    offs = []
    for m in range(cur.shape[0]):
        offs.append(sum(((m >> i) & 1) << bit for i, bit in enumerate(order[:-1])))
    far = tuple(o | (1 << order[-1]) for o in offs)
    rel = ((0, tuple(offs)), (0, far), (1, tuple(offs)), (1, far))
    return [cur, last, to_mate(cur), to_mate(last)], rel


def gather_ring(block, order, nz):
    cur = block[None]
    offs = [0]
    for bit in order:
        cur = jnp.concatenate([cur, to_seq(cur, 1 << bit)], axis=0)
        offs = offs + [o | (1 << bit) for o in offs]
    arrays = [cur, to_mate(cur)]
    for _ in range(1, nz):
        cur = to_ring(cur)
        arrays += [cur, to_mate(cur)]
    return arrays, tuple(offs)


def added(terms):
    return functools.reduce(lambda a, b: a + b, [t.astype(F32) for t in terms])


def scatter_bits(terms, order, axis):
    left = sorted(order)
    for bit in order:
        place = axis + len(left) - 1 - left.index(bit)
        away = added([lax.index_in_dim(t, 1, place, keepdims=False) for t in terms])
        got = to_seq(away.astype(BF16), 1 << bit)
        terms = [lax.index_in_dim(t, 0, place, keepdims=False) for t in terms] + [got]
        left.remove(bit)
    return terms


def in_bits(value, ns, axis):
    shape = value.shape
    return value.reshape(shape[:axis] + (2,) * (ns.bit_length() - 1) + shape[axis + 1 :])


def scatter_direct(keep, send, order, ns, nz):
    terms = [in_bits(t, ns, 1) for t in (keep, to_mate(send))]
    terms = scatter_bits(terms, order, 1)
    got = [to_z(added([t[a] for t in terms]).astype(BF16), a) for a in range(1, nz)]
    return added([t[0] for t in terms] + got)


def scatter_ring(keep, send, order, ns, nz):
    terms = [in_bits(t, ns, 1) for t in (keep, to_mate(send))]
    moving = []
    for slot in range(nz - 1, 0, -1):
        moving = [to_ring(added([t[slot] for t in terms] + moving).astype(BF16))]
    terms = scatter_bits([t[0] for t in terms] + moving, order, 0)
    return added(terms)


def body(
    tokens,
    lengths,
    timesteps,
    w_query,
    b_query,
    w_key,
    w_value,
    b_value,
    w_out,
    b_out,
    gain_one,
    shift_one,
    w_up,
    b_up,
    w_down,
    b_down,
    gain_two,
    shift_two,
    w_time,
    b_time,
    cotangent,
):
    seqs, rows, model = tokens.shape
    ns = lax.axis_size("seq")
    nz = lax.axis_size("dp") // 2
    r = w_query.shape[0]
    hg = model // ns
    dp = lax.axis_index("dp")
    j = lax.axis_index("seq")
    idx = jnp.stack([dp // 2, dp % 2, j]).astype(jnp.int32)
    bits = bits_of(ns)
    back = bits[::-1]

    toks = [tokens] + [to_seq(tokens, k) for k in range(1, ns)]
    row = jnp.concatenate(
        [b_query, b_value, b_out, gain_one, shift_one, b_down, gain_two, shift_two, w_time, b_time, b_up]
    )
    row = jnp.zeros((PAD, 3 * hg), BF16).at[0, : row.shape[0]].set(row)
    blocks = jnp.concatenate(
        [w.reshape(r, ns, hg).transpose(1, 0, 2) for w in (w_query, w_key, w_value)], axis=2
    )
    blocks = jnp.concatenate([jnp.broadcast_to(row, (ns,) + row.shape), blocks], axis=1)
    mine = [lax.dynamic_index_in_dim(blocks, j ^ k, 0, keepdims=False) for k in range(ns)]
    near = jnp.stack([mine[0]] + [to_seq(mine[k], k) for k in range(1, ns)])
    qa = jnp.stack([near] + [to_z(near, a) for a in range(1, nz)])
    qb = to_mate(qa)

    half = (5 * model) // 2
    outer = jnp.concatenate([w_out, w_up], axis=1)
    u1, rel1 = gather_direct(outer[:, :half], back, nz)
    u2, rel2 = gather_direct(outer[:, half:], bits, nz)
    dn, rel3 = gather_ring(w_down, bits, nz)

    q, k, v, low, w_qkv, small, bup = project(ns, nz, lengths, timesteps, idx, toks, qa, qb)
    ctx_out, ctxt, lse = attend(ns, lengths, idx, q, k, v)
    ctxs = [ctx_out[0]] + [to_seq(ctx_out[n], n) for n in range(1, ns)]
    kept, dctx_out, sums, gbup = middle(
        ns, nz, r, (rel1, rel2, rel3), lengths, timesteps, idx, tokens, cotangent, small, bup, ctxs, u1, u2, dn
    )
    output, act, dg, ug, fl, cx, ag, r1 = kept
    dctx = [dctx_out[0]] + [to_seq(dctx_out[n], n) for n in range(1, ns)]
    grad_u1 = scatter_direct(*up_grad(ns, nz, r, idx, cx, ag, fl, ug, 0), bits, ns, nz)
    grad_u2 = scatter_direct(*up_grad(ns, nz, r, idx, cx, ag, fl, ug, 1), back, ns, nz)
    grad_down = scatter_ring(*down_grad(ns, nz, r, idx, act, dg), bits, ns, nz)
    backs = [
        attend_back(ns, s, lengths, timesteps, idx, q, k, v, ctxt, lse, w_qkv, dctx)
        for s in range(seqs)
    ]
    r1 = r1.reshape(seqs, rows, model)
    grad_tokens = []
    for s in range(seqs):
        parts = backs[s][1]
        got = [to_seq(parts[n], n) for n in range(1, ns)]
        grad_tokens.append(added([r1[s], parts[0]] + got).astype(BF16))
    grad_tokens = jnp.stack(grad_tokens)
    keep, send = qkv_grad(
        ns, nz, r, idx, low, backs[0][0], backs[1][0], sums, gbup, backs[0][2], backs[1][2], backs[0][3], backs[1][3]
    )
    terms = [keep, to_mate(send)]
    got = [to_z(added([t[a] for t in terms]).astype(BF16), a) for a in range(1, nz)]
    own = added([t[0] for t in terms] + got)
    others = [to_seq(own[n].astype(BF16), n) for n in range(1, ns)]
    g_query, g_key, g_value, vectors = finish(ns, r, model, idx, own[0], others)
    pick = lambda n: vectors[0, n * r : (n + 1) * r]
    g_up = jnp.concatenate([grad_u1[:, model:], grad_u2], axis=1)
    return (
        output,
        grad_tokens,
        g_query,
        pick(0),
        g_key,
        g_value,
        pick(1),
        grad_u1[:, :model],
        pick(2),
        pick(3),
        pick(4),
        g_up,
        vectors[0, 10 * r : 14 * r],
        grad_down,
        pick(5),
        pick(6),
        pick(7),
        pick(8),
        pick(9),
    )


def solution(mesh):
    split = P(("dp", "seq"))
    rows = P(("dp", "seq"), None)
    token = P("dp", "seq", None)
    items = P("dp", None)
    return jax.shard_map(
        body,
        mesh=mesh,
        in_specs=(
            token, items, items, rows, split, rows, rows, split, rows, split, split, split,
            rows, split, rows, split, split, split, split, split, token,
        ),
        out_specs=(
            token, token, rows, split, rows, rows, split, rows, split, split, split,
            rows, split, rows, split, split, split, split, split,
        ),
        check_vma=False,
    )
```

```python
import functools

import jax
import jax.numpy as jnp
from jax import lax
from jax.experimental import pallas as pl
from jax.experimental.pallas import tpu as pltpu
from jax.sharding import PartitionSpec as P

HD = 64
TSTEPS = 5000
EPSILON = 1e-05
NEGATIVE = -1e30
ROOT_HALF = 0.7071067811865476
DENSITY_SCALE = 0.3989422804014327
PAD = 128
WIDE = 512
BF16 = jnp.bfloat16
F32 = jnp.float32
VMEM = pltpu.VMEM
SMEM = pltpu.SMEM


def nn(a, b):
    return lax.dot_general(a, b, (((1,), (0,)), ((), ())), preferred_element_type=F32)


def nt(a, b):
    return lax.dot_general(a, b, (((1,), (1,)), ((), ())), preferred_element_type=F32)


def flipped_bits(value, count):
    return sum(((value >> i) & 1) << (count - 1 - i) for i in range(count))


def tn(a, b):
    return lax.dot_general(a, b, (((0,), (0,)), ((), ())), preferred_element_type=F32)


def shift_of(ns, core, slot):
    other = flipped_bits(slot, ns.bit_length() - 1)
    return slot + core * (other - slot)


def vspec():
    return pl.BlockSpec(memory_space=VMEM)


def sspec():
    return pl.BlockSpec(memory_space=SMEM)


def aspec():
    return pl.BlockSpec(memory_space=pl.ANY)


def params(mib, grid=0):
    if grid:
        return pltpu.CompilerParams(
            vmem_limit_bytes=mib << 20, dimension_semantics=("arbitrary",) * grid
        )
    return pltpu.CompilerParams(vmem_limit_bytes=mib << 20)


def cost(flops, nbytes, trans=0):
    return pl.CostEstimate(flops=int(flops), bytes_accessed=int(nbytes), transcendentals=int(trans))


def tau_rows(len_ref, tim_ref, seq, first, rows):
    spot = first + lax.broadcasted_iota(jnp.int32, (rows, 128), 0)
    begin = jnp.int32(0)
    step = jnp.zeros((rows, 128), jnp.int32)
    for i in range(len_ref.shape[1]):
        end = begin + len_ref[seq, i]
        step = jnp.where((spot >= begin) & (spot < end), tim_ref[seq, i], step)
        begin = end
    return (step.astype(F32) / TSTEPS)[:, :1]


def segments(len_ref, seq, spot):
    end = jnp.int32(0)
    found = jnp.zeros(spot.shape, jnp.int32)
    for i in range(len_ref.shape[1]):
        end = end + len_ref[seq, i]
        found = found + (spot >= end).astype(jnp.int32)
    return found


def item_bias(len_ref, seq, first, keys, rows, out_ref):
    mine = segments(len_ref, seq, first + lax.broadcasted_iota(jnp.int32, (8, rows), 1))
    theirs = segments(len_ref, seq, lax.broadcasted_iota(jnp.int32, (keys, 128), 0))
    for lane in range(rows // 128):
        same = theirs == mine[:1, lane * 128 : (lane + 1) * 128]
        out_ref[:, lane * 128 : (lane + 1) * 128] = jnp.where(same, 0.0, NEGATIVE)


def fold(block):
    rows, width = block.shape
    return block.reshape(rows // 8, 8, width)


def pack_kernel(ns, count, idx, *refs):
    srcs, (out_ref, outer_ref), dsts, sem = refs[:count], refs[count : count + 2], refs[count + 2 : -1], refs[-1]
    r, model = srcs[0].shape
    ff = srcs[-1].shape[1]
    hg = model // ns
    targets = list(dsts) + [outer_ref.at[:, 0:model], outer_ref.at[:, model : model + ff]]
    copies = [pltpu.make_async_copy(a, b, sem.at[n]) for n, (a, b) in enumerate(zip(srcs, targets))]
    for copy in copies:
        copy.start()
    for copy in copies:
        copy.wait()
    c, j = idx[1], idx[2]
    rows = [v[...].astype(F32).reshape(1, r) for v in dsts[3:-1]]
    rows.append(jnp.zeros((PAD - len(rows), r), F32))
    small = jnp.concatenate(rows, axis=0).T.astype(BF16)
    for m in range(ns):
        at = pl.ds(pl.multiple_of((j ^ shift_of(ns, c, m)) * hg, 128), hg)
        for n in range(3):
            out_ref[m, :, n * hg : (n + 1) * hg] = dsts[n][:, at]
        out_ref[m, :, 3 * hg :] = small
    row = dsts[-1][...].astype(F32).reshape(1, 4 * r)
    if PAD > 4 * r:
        row = jnp.concatenate([row, jnp.zeros((1, PAD - 4 * r), F32)], axis=1)
    outer_ref[:, model + ff :] = jnp.broadcast_to(row, (r, PAD)).astype(BF16)


def pack(ns, idx, w_query, w_key, w_value, vectors, b_up, w_out, w_up):
    r, model = w_query.shape
    args = (w_query, w_key, w_value, *vectors, b_up, w_out, w_up)
    return pl.pallas_call(
        functools.partial(pack_kernel, ns, len(args)),
        name="pack",
        out_shape=[
            jax.ShapeDtypeStruct((ns, r, 3 * (model // ns) + PAD), BF16),
            jax.ShapeDtypeStruct((r, model + w_up.shape[1] + PAD), BF16),
        ],
        in_specs=[sspec()] + [aspec()] * len(args),
        out_specs=[vspec()] * 2,
        scratch_shapes=[VMEM(a.shape, a.dtype) for a in args[:-2]]
        + [pltpu.SemaphoreType.DMA((len(args),))],
        compiler_params=params(60),
    )(idx, *args)


def qkv_kernel(ns, nz, r, len_ref, tim_ref, idx, *refs):
    toks = refs[:2]
    qa, qb = refs[2:4]
    q_ref, k_ref, v_ref, low_ref, w_ref, small_ref, wide = refs[4:]
    z, c, j = idx[0], idx[1], idx[2]
    half, seqs, rows, model = toks[0].shape
    hg = q_ref.shape[2]
    for cc, src in enumerate((qa, qb)):
        for a in range(nz):
            for b in range(ns):
                d = ((z ^ a) * 2 + (c ^ cc)) * ns + (j ^ shift_of(ns, c ^ cc, b))
                wide[pl.ds(pl.multiple_of(d * r, r), r), :] = src[a, b].astype(wide.dtype)
    w_ref[...] = wide[:, : 3 * hg].astype(BF16)
    small_ref[...] = wide[:, 3 * hg :].astype(F32).T[:16, :]
    heads = pl.ds(pl.multiple_of(j * hg, 128), hg)
    bq = small_ref[0:1, heads]
    bv = small_ref[1:2, heads]
    wt = small_ref[8:9, :]
    bt = small_ref[9:10, :]
    for k in range(ns):
        first = pl.multiple_of((j ^ shift_of(ns, c, k)) * rows, rows)
        here = pl.ds(first, rows)
        for s in range(seqs):
            tau = tau_rows(len_ref, tim_ref, s, first, rows)
            low = (toks[k // half][k % half, s].astype(F32) + tau * wt + bt).astype(BF16)
            low_ref[s, here, :] = low
            got = nn(low, w_ref[...])
            q_ref[s, here, :] = ((got[:, :hg] + bq) * (HD**-0.5)).astype(BF16)
            k_ref[s, here, :] = got[:, hg : 2 * hg].astype(BF16)
            v_ref[s, here, :] = (got[:, 2 * hg :] + bv).astype(BF16)


def project(ns, nz, lengths, timesteps, idx, toks, qa, qb):
    seqs, rows, model = toks[0].shape[1:]
    r = qa.shape[2]
    hg = (qa.shape[3] - PAD) // 3
    full = rows * ns
    heads = jax.ShapeDtypeStruct((seqs, full, hg), BF16)
    outs = [
        heads,
        heads,
        heads,
        jax.ShapeDtypeStruct((seqs, full, model), BF16),
        jax.ShapeDtypeStruct((model, 3 * hg), BF16),
        jax.ShapeDtypeStruct((16, model), F32),
    ]
    return pl.pallas_call(
        functools.partial(qkv_kernel, ns, nz, r),
        name="project",
        out_shape=outs,
        in_specs=[sspec()] * 3 + [vspec()] * 4,
        out_specs=[vspec()] * 6,
        scratch_shapes=[VMEM((model, 3 * hg + PAD), BF16 if r % 16 == 0 else F32)],
        compiler_params=params(58),
        cost_estimate=cost(2 * seqs * full * model * 3 * hg, 14 << 20),
    )(lengths, timesteps, idx, *toks, qa, qb)


PAIR = 128
QUERIES = 512


def slots_of(full):
    return 2 if full <= 1024 else 1


def item_bias_all(len_ref, seq, bias):
    keys = bias.shape[0]
    for b in range(keys // QUERIES):
        item_bias(len_ref, seq, b * QUERIES, keys, QUERIES, bias.at[:, b * QUERIES : (b + 1) * QUERIES])


def attend_kernel(ns, s, len_ref, idx, q_ref, k_ref, v_ref, *refs):
    ctx_refs = refs[:ns]
    ctxf_ref, lse_ref, bias, probs, scale = refs[ns:]
    j = idx[2]
    full = k_ref.shape[1]
    rows = full // ns

    alone = whole_sequence(len_ref, s, full)

    @pl.when((pl.program_id(0) == 0) & jnp.logical_not(alone))
    def _():
        item_bias_all(len_ref, s, bias)

    scale[...] = jnp.zeros_like(scale)
    lse_ref[...] = jnp.zeros_like(lse_ref)

    def heads(add):
        attend_heads(full, add, q_ref, k_ref, v_ref, ctxf_ref, lse_ref, probs, scale)

    pl.when(alone)(lambda: heads(lambda st, at: st))
    pl.when(jnp.logical_not(alone))(lambda: heads(lambda st, at: st + bias[:, at]))
    for k in range(ns):
        here = pl.ds(pl.multiple_of((j ^ k) * rows, rows), rows)
        ctx_refs[k][...] = ctxf_ref[0, here, :].astype(BF16)


def whole_sequence(len_ref, seq, full):
    end = jnp.int32(0)
    same = jnp.bool_(True)
    for i in range(len_ref.shape[1]):
        end = end + len_ref[seq, i]
        same = same & ((end <= 0) | (end >= full))
    return same


def attend_heads(full, add, q_ref, k_ref, v_ref, ctxf_ref, lse_ref, probs, scale):
    for h in range(PAIR // HD):
        cols = slice(h * HD, (h + 1) * HD)
        kh, vh = k_ref[0, :, cols], v_ref[0, :, cols]
        for b in range(full // QUERIES):
            at = slice(b * QUERIES, (b + 1) * QUERIES)
            st = add(nt(kh, q_ref[0, at, cols]), at)
            top = jnp.max(jnp.max(fold(st), axis=0), axis=0, keepdims=True)
            p = jnp.exp(st - top)
            total = jnp.sum(jnp.sum(fold(p), axis=0), axis=0, keepdims=True)
            probs[h % probs.shape[0], :, at] = p.astype(BF16)
            scale[h : h + 1, at] = 1.0 / total
            lse_ref[0, h : h + 1, at] = top + jnp.log(total)
        by_row = scale[...].T
        ctxf_ref[0, :, cols] = tn(probs[h % probs.shape[0]], vh) * by_row[:, h : h + 1]


def attend(ns, seq, lengths, idx, q, k, v):
    seqs, full, hg = q.shape
    rows = full // ns
    groups = hg // PAIR
    outs = [jax.ShapeDtypeStruct((rows, hg), BF16)] * ns + [
        jax.ShapeDtypeStruct((1, full, hg), F32),
        jax.ShapeDtypeStruct((1, 8 * groups, full), F32),
    ]
    wide = pl.BlockSpec((1, full, PAIR), lambda i: (seq, 0, i))
    res = pl.pallas_call(
        functools.partial(attend_kernel, ns, seq),
        name="attend",
        out_shape=outs,
        grid=(groups,),
        in_specs=[sspec(), sspec(), wide, wide, wide],
        out_specs=[pl.BlockSpec((rows, PAIR), lambda i: (0, i))] * ns
        + [
            pl.BlockSpec((1, full, PAIR), lambda i: (0, 0, i)),
            pl.BlockSpec((1, 8, full), lambda i: (0, i, 0)),
        ],
        scratch_shapes=[
            VMEM((full, full), F32),
            VMEM((slots_of(full), full, full), BF16),
            VMEM((8, full), F32),
        ],
        compiler_params=params(58, 1),
        cost_estimate=cost(4 * 4 * full * full * hg, 4 << 20),
    )(lengths, idx, q, k, v)
    return res[:ns], res[ns], res[ns + 1]


def attend_back_kernel(ns, seq, len_ref, tim_ref, idx, q_ref, k_ref, v_ref, ctxf_ref, lse_ref, w_ref, *refs):
    dctx = refs[:ns]
    grad_ref, pk_ref, ps_ref, sum_ref, bsum_ref, bias, dcx, probs, score = refs[ns:]
    i = pl.program_id(0)
    c, j = idx[1], idx[2]
    full = k_ref.shape[1]
    rows = full // ns
    hg = grad_ref.shape[1] // 3

    alone = whole_sequence(len_ref, seq, full)

    @pl.when((i == 0) & jnp.logical_not(alone))
    def _():
        item_bias_all(len_ref, seq, bias)

    for k in range(ns):
        dcx[pl.ds(pl.multiple_of((j ^ k) * rows, rows), rows), :] = dctx[k][0]

    def heads(add):
        back_heads(full, add, i, q_ref, k_ref, v_ref, ctxf_ref, lse_ref, grad_ref, dcx, probs, score)

    pl.when(alone)(lambda: heads(lambda st, at: st))
    pl.when(jnp.logical_not(alone))(lambda: heads(lambda st, at: st + bias[:, at]))
    @pl.when(i == pl.num_programs(0) - 1)
    def _():
        plain = jnp.zeros((8, w_ref.shape[0]), F32)
        timed = jnp.zeros((8, w_ref.shape[0]), F32)
        bias_sum = jnp.zeros((8, 3 * hg), F32)
        for k in range(ns):
            first = pl.multiple_of((j ^ shift_of(ns, c, k)) * rows, rows)
            block = grad_ref[pl.ds(first, rows), :]
            part = nt(block, w_ref[...])
            (pk_ref if k < ns // 2 else ps_ref)[k % (ns // 2)] = part.astype(BF16)
            plain = plain + jnp.sum(fold(part), axis=0)
            tau = tau_rows(len_ref, tim_ref, seq, first, rows)
            timed = timed + jnp.sum(fold(part * tau), axis=0)
            bias_sum = bias_sum + jnp.sum(fold(block.astype(F32)), axis=0)
        sum_ref[...] = jnp.zeros_like(sum_ref)
        sum_ref[0:1, :] = jnp.sum(timed, axis=0, keepdims=True)
        sum_ref[1:2, :] = jnp.sum(plain, axis=0, keepdims=True)
        bsum_ref[...] = jnp.broadcast_to(jnp.sum(bias_sum, axis=0, keepdims=True), bsum_ref.shape)


def back_heads(full, add, i, q_ref, k_ref, v_ref, ctxf_ref, lse_ref, grad_ref, dcx, probs, score):
    grads = []
    for h in range(PAIR // HD):
        cols = slice(h * HD, (h + 1) * HD)
        qh, kh, vh = q_ref[0, :, cols], k_ref[0, :, cols], v_ref[0, :, cols]
        dch = dcx[:, cols]
        row_total = jnp.sum((ctxf_ref[0, :, cols] * dch.astype(F32)).T, axis=0, keepdims=True)
        for b in range(full // QUERIES):
            at = slice(b * QUERIES, (b + 1) * QUERIES)
            p = jnp.exp(add(nt(kh, qh[at, :]), at) - lse_ref[0, h : h + 1, at])
            ds = p * (nt(vh, dch[at, :]) - row_total[:, at])
            probs[h % probs.shape[0], :, at] = p.astype(BF16)
            score[h % score.shape[0], :, at] = ds.astype(BF16)
        dq = tn(score[h % score.shape[0]], kh).astype(BF16).astype(F32) * (HD**-0.5)
        grads.append((dq, nn(score[h % score.shape[0]], qh), nn(probs[h % probs.shape[0]], dch)))
    hg = grad_ref.shape[1] // 3
    for n in range(3):
        at = pl.ds(pl.multiple_of(n * hg + i * PAIR, PAIR), PAIR)
        grad_ref[:, at] = jnp.concatenate([g[n] for g in grads], axis=1).astype(BF16)


def attend_back(ns, seq, lengths, timesteps, idx, q, k, v, ctxf, lse, w, dctx):
    seqs, full, hg = q.shape
    rows = full // ns
    groups = hg // PAIR
    model = w.shape[0]
    one = lambda shape: pl.BlockSpec(shape, lambda i: (0,) * len(shape))
    wide = pl.BlockSpec((1, full, PAIR), lambda i: (seq, 0, i))
    outs = (
        [jax.ShapeDtypeStruct((full, 3 * hg), BF16)]
        + [jax.ShapeDtypeStruct((ns // 2, rows, model), BF16)] * 2
        + [jax.ShapeDtypeStruct((8, model), F32), jax.ShapeDtypeStruct((8, 3 * hg), F32)]
    )
    return pl.pallas_call(
        functools.partial(attend_back_kernel, ns, seq),
        name="attend_back",
        out_shape=outs,
        grid=(groups,),
        in_specs=[sspec()] * 3
        + [
            wide,
            wide,
            wide,
            pl.BlockSpec((1, full, PAIR), lambda i: (0, 0, i)),
            pl.BlockSpec((1, 8, full), lambda i: (0, i, 0)),
            one((model, 3 * hg)),
        ]
        + [pl.BlockSpec((1, rows, PAIR), lambda i: (seq, 0, i))] * ns,
        out_specs=[one((full, 3 * hg))]
        + [one((ns // 2, rows, model))] * 2
        + [one((8, model)), one((8, 3 * hg))],
        scratch_shapes=[
            VMEM((full, full), F32),
            VMEM((full, PAIR), BF16),
            VMEM((slots_of(full), full, full), BF16),
            VMEM((slots_of(full), full, full), BF16),
        ],
        compiler_params=params(58, 1),
        cost_estimate=cost(10 * 4 * full * full * hg, 10 << 20),
    )(lengths, timesteps, idx, q, k, v, ctxf, lse, w, *dctx)


def middle_kernel(ns, nz, r, len_ref, tim_ref, idx, tok_ref, cot_ref, small_ref, *refs):
    ctxs = refs[: 2 * ns]
    refs = refs[2 * ns :]
    outer, dn, rest = refs[:4], refs[4 : 4 + 2 * nz], refs[4 + 2 * nz :]
    out_ref, keep_o, send_o, ug_o, fl_o, cx_o, ag_o, r1_o = rest[:8]
    dctx = rest[8 : 8 + ns]
    sum_ref, gbup_ref = rest[8 + ns : 10 + ns]
    wu, wd, act, slope, ug, fl, cx, dg, first, norm, inv, stage, bup_ref, slots, wsem, osem, gsem = rest[10 + ns :]
    z, c, j = idx[0], idx[1], idx[2]
    seqs, rows, model = tok_ref.shape
    ff = wd.shape[0]
    hg = ctxs[0].shape[1]
    tokens = seqs * rows
    ends = (0, model, wu.shape[1])
    for part in range(2):
        at = slice(ends[part], ends[part + 1])
        for n, src in enumerate(outer):
            core = c ^ (n // 2)
            for m in range(ns // 2):
                shift = shift_of(ns, core, m + (n % 2) * (ns // 2))
                for a in range(nz):
                    d = ((z ^ a) * 2 + core) * ns + (j ^ shift)
                    pltpu.make_async_copy(
                        src.at[m, a, :, at],
                        wu.at[pl.ds(pl.multiple_of(d * r, r), r), at],
                        wsem.at[part],
                    ).start()
    for n, src in enumerate(dn):
        core = c ^ (n % 2)
        for m in range(ns):
            d = (lax.rem(z + nz - n // 2, nz) * 2 + core) * ns + (j ^ shift_of(ns, core, m))
            pltpu.make_async_copy(
                src.at[m],
                wd.at[pl.ds(pl.multiple_of(d * 4 * r, 4 * r), 4 * r), :],
                wsem.at[2],
            ).start()
    for k in range(ns):
        at = pl.ds(pl.multiple_of((j ^ k) * hg, 128), hg)
        for s in range(seqs):
            cx[s * rows : (s + 1) * rows, at] = ctxs[s * ns + k][...]
    sum_ref[...] = jnp.zeros_like(sum_ref)
    pltpu.make_async_copy(cx, cx_o, osem.at[0]).start()
    u1_all = wu.at[:, 0 : ends[1]]
    pltpu.make_async_copy(u1_all, u1_all, wsem.at[0]).wait()

    b_out = small_ref[2:3, :]
    gain_one, shift_one = small_ref[3:4, :], small_ref[4:5, :]
    b_down = small_ref[5:6, :]
    gain_two, shift_two = small_ref[6:7, :], small_ref[7:8, :]
    w_time, b_time = small_ref[8:9, :], small_ref[9:10, :]
    block = rows
    per = 1

    def add_sum(row, value):
        sum_ref[row : row + 1, :] += jnp.sum(jnp.sum(fold(value), axis=0), axis=0, keepdims=True)

    def mean(value):
        return jnp.sum(value, axis=-1, keepdims=True) * (1.0 / model)

    def one_first(s, b):
        at = pl.ds(pl.multiple_of((s * per + b) * block, block), block)
        inside = pl.ds(pl.multiple_of(b * block, block), block)
        attn = nn(cx[at, :], wu[:, 0:model])
        tau = tau_rows(len_ref, tim_ref, s, j * rows + b * block, block)
        start = tok_ref[s, inside, :].astype(F32) + tau * w_time + b_time
        res = start + (attn + b_out)
        center = res - mean(res)
        inverse = lax.rsqrt(mean(center * center) + EPSILON)
        normed = center * inverse
        norm[at, :] = normed
        inv[at, :] = jnp.broadcast_to(inverse, (block, 128))
        value = normed * gain_one + shift_one
        first[at, :] = value
        fl[at, :] = value.astype(BF16)

    for s in range(seqs):
        one_first(s, 0)
    pltpu.make_async_copy(fl, fl_o, osem.at[1]).start()
    u2_all = wu.at[:, ends[1] : ends[2]]
    pltpu.make_async_copy(u2_all, u2_all, wsem.at[1]).wait()
    for d in range(ns * nz * 2):
        bup_ref[0:1, d * 4 * r : (d + 1) * 4 * r] = wu[d * r : d * r + 1, model + ff : model + ff + 4 * r].astype(F32)

    def one_up(n, _):
        at = pl.ds(pl.multiple_of(n * WIDE, WIDE), WIDE)
        wat = pl.ds(pl.multiple_of(model + n * WIDE, WIDE), WIDE)
        for h in range(2):
            rr = slice(h * tokens // 2, (h + 1) * tokens // 2)
            pre = nn(fl[rr, :], wu[:, wat]) + bup_ref[0:1, at]
            cumulative = 0.5 * (1.0 + lax.erf(pre * ROOT_HALF))
            density = jnp.exp(-0.5 * pre * pre) * DENSITY_SCALE
            act[rr, at] = (pre * cumulative).astype(BF16)
            slope[rr, at] = cumulative + pre * density
        return 0

    lax.fori_loop(0, ff // WIDE, one_up, 0)
    pltpu.make_async_copy(wd, wd, wsem.at[2]).wait()

    def one_second(s, b):
        at = pl.ds(pl.multiple_of((s * per + b) * block, block), block)
        inside = pl.ds(pl.multiple_of(b * block, block), block)
        res = first[at, :] + (nn(act[at, :], wd[...]) + b_down)
        center = res - mean(res)
        inverse = lax.rsqrt(mean(center * center) + EPSILON)
        normed = center * inverse
        out_ref[s, inside, :] = (normed * gain_two + shift_two).astype(BF16)
        g = cot_ref[s, inside, :].astype(F32)
        add_sum(4, g * normed)
        add_sum(5, g)
        gn = g * gain_two
        grad = inverse * (gn - mean(gn) - normed * mean(gn * normed))
        first[at, :] = grad
        low = grad.astype(BF16)
        dg[at, :] = low
        add_sum(3, low.astype(F32))

    for s in range(seqs):
        one_second(s, 0)

    wide = ns * 4 * r

    def grad_copy(n, dst):
        return pltpu.make_async_copy(slots.at[n % 2], dst.at[n % nz], gsem.at[n % 2])

    for n in range(2 * nz):
        core = c ^ 1 if n < nz else c
        dst = send_o if n < nz else keep_o
        own = pl.multiple_of((lax.rem(z + n % nz, nz) * 2 + core) * wide, wide)
        total = tn(act[:, pl.ds(own, wide)], dg[...])
        if n >= 2:
            grad_copy(n - 2, send_o if n - 2 < nz else keep_o).wait()
        for b in range(ns):
            slots[n % 2, place_of(ns, core, j ^ b)] = total[b * 4 * r : (b + 1) * 4 * r].astype(BF16)
        grad_copy(n, dst).start()

    def one_up_grad(n, _):
        at = pl.ds(pl.multiple_of(n * WIDE, WIDE), WIDE)
        total = jnp.zeros((8, WIDE), F32)
        for h in range(2):
            rr = slice(h * tokens // 2, (h + 1) * tokens // 2)
            low = (nt(dg[rr, :], wd[at, :]) * slope[rr, at]).astype(BF16)
            ug[rr, at] = low
            total = total + jnp.sum(fold(low.astype(F32)), axis=0)
        row = jnp.sum(total, axis=0, keepdims=True)
        for m in range(WIDE // (4 * r)):
            gbup_ref[pl.ds(n * (WIDE // (4 * r)) + m, 1), :] = row[:, m * 4 * r : (m + 1) * 4 * r]
        return 0

    lax.fori_loop(0, ff // WIDE, one_up_grad, 0)
    pltpu.make_async_copy(ug, ug_o, osem.at[4]).start()
    pltpu.make_async_copy(fl, fl_o, osem.at[1]).wait()

    def one_first_grad(s, b):
        at = pl.ds(pl.multiple_of((s * per + b) * block, block), block)
        inside = pl.ds(pl.multiple_of(b * block, block), block)
        fg = nt(ug[at, :], wu[:, model : model + ff]) + first[at, :]
        normed = norm[at, :]
        add_sum(1, fg * normed)
        add_sum(2, fg)
        gn = fg * gain_one
        grad = inv[at, :][:, :1] * (gn - mean(gn) - normed * mean(gn * normed))
        first[at, :] = grad
        low = grad.astype(BF16)
        fl[at, :] = low
        add_sum(0, low.astype(F32))
        tau = tau_rows(len_ref, tim_ref, s, j * rows + b * block, block)
        add_sum(6, grad * tau)
        add_sum(7, grad)
        stage[...] = nt(low, wu[:, 0:model]).astype(BF16)
        for k in range(ns):
            cols = pl.ds(pl.multiple_of((j ^ k) * hg, 128), hg)
            dctx[k][s, inside, :] = stage[:, cols]

    for s in range(seqs):
        one_first_grad(s, 0)
    ag_copy = pltpu.make_async_copy(fl, ag_o, osem.at[5])
    ag_copy.start()
    r1_copy = pltpu.make_async_copy(first, r1_o, osem.at[6])
    r1_copy.start()
    pltpu.make_async_copy(cx, cx_o, osem.at[0]).wait()
    for n in (2 * nz - 2, 2 * nz - 1):
        grad_copy(n, keep_o).wait()
    pltpu.make_async_copy(ug, ug_o, osem.at[4]).wait()
    ag_copy.wait()
    r1_copy.wait()


def middle(ns, nz, r, lengths, timesteps, idx, tokens, cotangent, small, ctxs, outer, dn):
    seqs, rows, model = tokens.shape
    total = seqs * rows
    ff = dn[0].shape[1] * ns * nz * 2
    hg = ctxs[0].shape[1]
    sh = lambda *a: jax.ShapeDtypeStruct(a[:-1], a[-1])
    outs = [
        sh(seqs, rows, model, BF16),
        sh(nz, ns, 4 * r, model, BF16),
        sh(nz, ns, 4 * r, model, BF16),
        sh(total, ff, BF16),
        sh(total, model, BF16),
        sh(total, model, BF16),
        sh(total, model, BF16),
        sh(total, model, F32),
    ]
    outs += [sh(seqs, rows, hg, BF16)] * ns + [sh(16, model, F32), sh(ff // (4 * r), 4 * r, F32)]
    res = pl.pallas_call(
        functools.partial(middle_kernel, ns, nz, r),
        name="middle",
        out_shape=outs,
        in_specs=[sspec()] * 3
        + [vspec()] * (3 + 2 * ns)
        + [aspec()] * (len(outer) + len(dn)),
        out_specs=[vspec()] + [aspec()] * 7 + [vspec()] * (ns + 2),
        scratch_shapes=[
            VMEM((model, model + ff + PAD), BF16),
            VMEM((ff, model), BF16),
            VMEM((total, ff), BF16),
            VMEM((total, ff), F32),
            VMEM((total, ff), BF16),
            VMEM((total, model), BF16),
            VMEM((total, model), BF16),
            VMEM((total, model), BF16),
            VMEM((total, model), F32),
            VMEM((total, model), F32),
            VMEM((total, 128), F32),
            VMEM((rows, model), BF16),
            VMEM((8, ff), F32),
            VMEM((2, ns, 4 * r, model), BF16),
            pltpu.SemaphoreType.DMA((3,)),
            pltpu.SemaphoreType.DMA((7,)),
            pltpu.SemaphoreType.DMA((2,)),
        ],
        compiler_params=params(60),
        cost_estimate=cost(
            2 * total * (2 * model * model + 4 * model * ff), 40 << 20, 3 * total * ff
        ),
    )(lengths, timesteps, idx, tokens, cotangent, small, *ctxs, *outer, *dn)
    return res[:8], res[8 : 8 + ns], res[8 + ns], res[9 + ns]


def place_of(ns, core, offset):
    return offset + core * (flipped_bits(offset, ns.bit_length() - 1) - offset)


def gather_columns(ns, nz, r, core, idx, src, dst, first):
    wide = ns * r
    for a in range(nz):
        pair = pl.multiple_of((idx[0] ^ a) * 2 * wide, 2 * wide)
        if wide % 128 == 0:
            got = src[:, pl.ds(pl.multiple_of(pair + core * wide, wide), wide)]
        else:
            both = src[:, pl.ds(pair, 2 * wide)]
            got = jnp.where(core == 0, both[:, :wide], both[:, wide:])
        dst[:, first + a * wide : first + (a + 1) * wide] = got


def store_slots(ns, nz, r, core, walk, idx, total, dst, at=slice(None)):
    for a in range(nz):
        for b in range(ns):
            slot = place_of(ns, core if walk else 0, idx[2] ^ b)
            n = (a * ns + b) * r
            dst[a, slot, :, at] = total[n : n + r].astype(BF16)


def up_grad_kernel(ns, nz, r, idx, cx_ref, ag_ref, fl_ref, ug_ref, gbup_ref, keep_ref, send_ref, left):
    i = pl.program_id(0)
    split = ag_ref.shape[1] // WIDE
    last = pl.num_programs(0) - 1
    half = cx_ref.shape[1] // 2
    c = idx[1]

    def both(right):
        total = tn(left[...], right)
        store_slots(ns, nz, r, c, True, idx, total[:half], keep_ref)
        store_slots(ns, nz, r, c ^ 1, True, idx, total[half:], send_ref)

    @pl.when(i == 0)
    def _():
        gather_columns(ns, nz, r, c, idx, cx_ref, left, 0)
        gather_columns(ns, nz, r, c ^ 1, idx, cx_ref, left, half)

    @pl.when(i < split)
    def _():
        both(ag_ref[:, pl.ds(pl.multiple_of(jnp.minimum(i, split - 1) * WIDE, WIDE), WIDE)])

    @pl.when(i == split)
    def _():
        gather_columns(ns, nz, r, c, idx, fl_ref, left, 0)
        gather_columns(ns, nz, r, c ^ 1, idx, fl_ref, left, half)

    @pl.when((i >= split) & (i < last))
    def _():
        both(ug_ref[...])

    @pl.when(i == last)
    def _():
        keep_ref[...] = jnp.zeros_like(keep_ref)
        send_ref[...] = jnp.zeros_like(send_ref)
        for cc, dst in enumerate((keep_ref, send_ref)):
            core = c ^ cc
            for a in range(nz):
                for b in range(ns):
                    d = ((idx[0] ^ a) * 2 + core) * ns + (idx[2] ^ shift_of(ns, core, b))
                    row = gbup_ref[pl.ds(d, 1), :]
                    dst[a, b, :, 0 : 4 * r] = jnp.broadcast_to(row, (r, 4 * r)).astype(BF16)


def up_grad(ns, nz, r, idx, cx, ag, fl, ug, gbup):
    total, model = fl.shape
    ff = ug.shape[1]
    width = model + ff + PAD
    split, top = model // WIDE, ff // WIDE - 1
    one = lambda shape: pl.BlockSpec(shape, lambda i: (0,) * len(shape))
    block = pl.BlockSpec((nz, ns, r, WIDE), lambda i: (0, 0, 0, i))
    return pl.pallas_call(
        functools.partial(up_grad_kernel, ns, nz, r),
        name="up_grad",
        out_shape=[jax.ShapeDtypeStruct((nz, ns, r, width), BF16)] * 2,
        grid=(pl.cdiv(width, WIDE),),
        in_specs=[
            sspec(),
            one(cx.shape),
            one(ag.shape),
            one(fl.shape),
            pl.BlockSpec((total, WIDE), lambda i: (0, jnp.minimum(jnp.maximum(i - split, 0), top))),
            one(gbup.shape),
        ],
        out_specs=[block, block],
        scratch_shapes=[VMEM((total, model), BF16)],
        compiler_params=params(58, 1),
        cost_estimate=cost(2 * total * model * width, 10 << 20),
    )(idx, cx, ag, fl, ug, gbup)


def qkv_grad_kernel(ns, nz, r, idx, low_ref, g0_ref, g1_ref, sums_ref, s0_ref, s1_ref, b0_ref, b1_ref, keep_ref, send_ref, left, vec, tall):
    c, j = idx[1], idx[2]
    hg = g0_ref.shape[1] // 3
    vec[...] = jnp.zeros_like(vec)
    heads = pl.ds(pl.multiple_of(j * hg, 128), hg)
    both = b0_ref[0:1, :] + b1_ref[0:1, :]
    vec[0:1, heads] = both[:, :hg]
    vec[1:2, heads] = both[:, 2 * hg :]
    vec[2:8, :] = sums_ref[0:6, :]
    vec[8:10, :] = sums_ref[6:8, :] + s0_ref[0:2, :] + s1_ref[0:2, :]
    tall[...] = vec[...].T
    half = left.shape[1] // 2
    for cc, dst in enumerate((keep_ref, send_ref)):
        core = c ^ cc
        total = 0.0
        for s, g in enumerate((g0_ref, g1_ref)):
            gather_columns(ns, nz, r, core, idx, low_ref.at[s], left, cc * half)
            total = total + tn(left[:, cc * half : (cc + 1) * half], g[...])
        store_slots(ns, nz, r, 0, False, idx, total, dst, slice(0, 3 * hg))
        for a in range(nz):
            for b in range(ns):
                d = ((idx[0] ^ a) * 2 + core) * ns + (j ^ b)
                dst[a, b, :, 3 * hg :] = tall[pl.ds(pl.multiple_of(d * r, r), r), :].astype(BF16)


def qkv_grad(ns, nz, r, idx, low, g0, g1, sums, s0, s1, b0, b1):
    seqs, full, model = low.shape
    width = g0.shape[1] + PAD
    out = jax.ShapeDtypeStruct((nz, ns, r, width), BF16)
    return pl.pallas_call(
        functools.partial(qkv_grad_kernel, ns, nz, r),
        name="qkv_grad",
        out_shape=[out, out],
        in_specs=[sspec()] + [vspec()] * 8,
        out_specs=[vspec()] * 2,
        scratch_shapes=[
            VMEM((full, model), BF16),
            VMEM((PAD, model), F32),
            VMEM((model, PAD), F32),
        ],
        compiler_params=params(58),
        cost_estimate=cost(2 * seqs * full * model * width, 12 << 20),
    )(idx, low, g0, g1, sums, s0, s1, b0, b1)


def finish_kernel(ns, r, idx, own_ref, *refs):
    others = refs[: ns - 1]
    q_ref, k_ref, v_ref, small_ref = refs[ns - 1 :]
    j = idx[2]
    hg = (own_ref.shape[1] - PAD) // 3
    small = own_ref[:, 3 * hg :]
    for k in range(ns):
        part = own_ref[...] if k == 0 else others[k - 1][...].astype(F32)
        cols = pl.ds(pl.multiple_of((j ^ k) * hg, 128), hg)
        for n, dst in enumerate((q_ref, k_ref, v_ref)):
            dst[:, cols] = part[:, n * hg : (n + 1) * hg]
        if k:
            small = small + part[:, 3 * hg :]
    small_ref[...] = small.T[:16, :]


def finish(ns, r, model, idx, own, others):
    out = jax.ShapeDtypeStruct((r, model), F32)
    return pl.pallas_call(
        functools.partial(finish_kernel, ns, r),
        name="finish",
        out_shape=[out, out, out, jax.ShapeDtypeStruct((16, r), F32)],
        in_specs=[sspec()] + [vspec()] * ns,
        out_specs=[vspec()] * 4,
        compiler_params=params(16),
    )(idx, own, *others)


def to_seq(value, k):
    ns = lax.axis_size("seq")
    return lax.ppermute(value, "seq", [(i, i ^ k) for i in range(ns)])


def to_mate(value):
    nd = lax.axis_size("dp")
    return lax.ppermute(value, "dp", [(i, i ^ 1) for i in range(nd)])


def to_z(value, a):
    nd = lax.axis_size("dp")
    return lax.ppermute(value, "dp", [(i, i ^ (2 * a)) for i in range(nd)])


def to_ring(value):
    nd = lax.axis_size("dp")
    return lax.ppermute(value, "dp", [(i, (i + 2) % nd) for i in range(nd)])


def to_bit(value, place):
    ns, nd = lax.axis_size("seq"), lax.axis_size("dp")
    high = ns.bit_length() - 2
    pairs = []
    for dp in range(nd):
        bit = 1 << (high - place if dp % 2 else place)
        pairs += [(dp * ns + i, dp * ns + (i ^ bit)) for i in range(ns)]
    return lax.ppermute(value, ("dp", "seq"), pairs)


def gather_plane(block, ns):
    cur = block[None]
    high = ns.bit_length() - 2
    for place in range(high):
        cur = jnp.concatenate([cur, to_bit(cur, place)], axis=0)
    return [cur, to_bit(cur, high)]


def exchange_plane(blocks, ns):
    kept = [blocks[m] for m in range(ns)]
    early = None
    for place in range(ns.bit_length() - 1):
        bit = 1 << place
        away = [m for m in range(ns) if m & bit]
        got = to_bit(jnp.stack([kept[m] for m in away]), place)
        early = got if early is None else early
        for n, m in enumerate(away):
            kept[m] = got[n]
    return jnp.stack(kept), early


def added(terms):
    return functools.reduce(lambda a, b: a + b, [t.astype(F32) for t in terms])


def added_rows(lists):
    return jnp.stack([added(terms) for terms in lists]).astype(BF16)


def hold(*values):
    return lax.optimization_barrier(values)


def after(values, others):
    return lax.optimization_barrier((values, others))


class Scatter:
    def __init__(self, keep, send, ns, nz):
        self.ns, self.nz = ns, nz
        self.terms = [keep] + self.exchange(send)
        self.last = None

    def exchange(self, send):
        return [to_mate(send)]

    def high(self, half):
        return [t[: self.nz, half : self.ns] for t in self.terms]

    def bit(self):
        half = self.ns // 2
        self.last = added(self.high(half)).astype(BF16)
        self.terms = self.terms + [to_bit(self.last, self.ns.bit_length() - 2)]
        self.ns = half

    def finish(self, at=slice(None), row=slice(None)):
        while self.step():
            pass
        return added([t[0, 0, row, at] for t in self.terms])


class ScatterDirect(Scatter):
    ahead = None

    def exchange(self, send):
        half = self.ns // 2
        self.ahead = to_mate(send[:, half:])
        return [to_mate(send[:, :half])]

    def high(self, half):
        if self.ahead is None:
            return super().high(half)
        parts = [t[: self.nz, half : self.ns] for t in self.terms[:1]] + [self.ahead]
        self.ahead = None
        return parts

    def step(self):
        if self.ns > 1:
            self.bit()
        elif self.nz > 1:
            self.last = [added([t[a, 0] for t in self.terms]).astype(BF16) for a in range(1, self.nz)]
            self.terms = self.terms + [to_z(v, a + 1)[None, None] for a, v in enumerate(self.last)]
            self.nz = 1
        else:
            return False
        return True


class ScatterRing(Scatter):
    moving = None

    def fix(self):
        self.terms = self.terms + [self.moving[None]]

    def step(self):
        if self.nz > 1:
            self.nz -= 1
            parts = [t[self.nz] for t in self.terms] + ([] if self.moving is None else [self.moving])
            self.last = added(parts).astype(BF16)
            self.moving = to_ring(self.last)
        elif self.ns > 1:
            self.bit()
        else:
            return False
        return True


def body(
    tokens,
    lengths,
    timesteps,
    w_query,
    b_query,
    w_key,
    w_value,
    b_value,
    w_out,
    b_out,
    gain_one,
    shift_one,
    w_up,
    b_up,
    w_down,
    b_down,
    gain_two,
    shift_two,
    w_time,
    b_time,
    cotangent,
):
    seqs, rows, model = tokens.shape
    ns = lax.axis_size("seq")
    nz = lax.axis_size("dp") // 2
    r = w_query.shape[0]
    hg = model // ns
    dp = lax.axis_index("dp")
    j = lax.axis_index("seq")
    idx = jnp.stack([dp // 2, dp % 2, j]).astype(jnp.int32)

    high = ns.bit_length() - 1
    vectors = [b_query, b_value, b_out, gain_one, shift_one, b_down, gain_two, shift_two, w_time, b_time]
    mine, outer = pack(ns, idx, w_query, w_key, w_value, vectors, b_up, w_out, w_up)
    tok, down = tokens[None], w_down[None]
    kept = [mine[m] for m in range(ns)]
    outer_z, near_z = [], []
    waiting = list(range(1, nz))
    for place in range(high):
        got = [to_bit(tok, place), to_bit(down, place) if place < high - 1 else None]
        away = [m for m in range(ns) if m & (1 << place)]
        pieces = to_bit(jnp.stack([kept[m] for m in away]), place)
        now = waiting[:1] if place < high - 1 else waiting
        waiting = waiting[len(now) :]
        outer_z = outer_z + [to_z(outer, a) for a in now]
        tok, down, outer, kept, got, pieces, outer_z = hold(tok, down, outer, kept, got, pieces, outer_z)
        for n, m in enumerate(away):
            kept[m] = pieces[n]
        if place < high - 1:
            tok = jnp.concatenate([tok, got[0]], axis=0)
            down = jnp.concatenate([down, got[1]], axis=0)
    toks = [tok, got[0]]
    near = jnp.stack(kept)
    near_z = [to_z(near, a) for a in range(1, nz)]
    cur = jnp.stack([outer] + outer_z)[None]
    down_next, cur_next = to_bit(down, high - 1), to_bit(cur, 0)
    toks, near, near_z, down, down_next, cur, cur_next = hold(
        toks, near, near_z, down, down_next, cur, cur_next
    )
    qa = jnp.stack([near] + near_z)
    qb = to_mate(qa)
    down = jnp.concatenate([down, down_next], axis=0)
    downs = [down, to_ring(down)]
    for place in range(1, high):
        cur = jnp.concatenate([cur, cur_next], axis=0)
        cur_next = to_bit(cur, place)
    qa, _ = after(qa, (down, cur))

    projected = project(ns, nz, lengths, timesteps, idx, toks, qa, qb)
    q, k, v, low, w_qkv, small = projected
    fronts, ctxs = [], []
    for s in range(seqs):
        front = attend(ns, s, lengths, idx, q, k, v)
        front, downs = hold(front, downs)
        downs.append(to_ring(downs[-1]))
        if s == seqs - 1:
            front, ctxs, cur_next = hold(front, ctxs, cur_next)
        fronts.append(front)
        ctxs = ctxs + [front[0][0]] + [to_seq(front[0][n], n) for n in range(1, ns)]
        q, _ = after(q, front[0])
    near_half, _ = after(cur, fronts[-1][0])
    outer = [cur, cur_next, to_mate(near_half), to_mate(cur_next)]
    while len(downs) < nz:
        downs.append(to_ring(downs[-1]))
    downs = [x for d in downs for x in (d, to_mate(d))]
    kept, dctx_out, sums, gbup = middle(
        ns, nz, r, lengths, timesteps, idx, tokens, cotangent, small, ctxs, outer, downs
    )
    output, keep, send, ug, fl, cx, ag, r1 = kept

    two = ScatterRing(keep, send, ns, nz)
    dctx = [to_seq(dctx_out[n], n) for n in range(1, ns)]
    (fl, ug), _ = after((fl, ug), dctx_out)
    got = up_grad(ns, nz, r, idx, cx, ag, fl, ug, gbup)
    got, (dctx, two.terms[-1]) = after(got, (dctx, two.terms[-1]))
    dctx = [dctx_out[0]] + list(dctx)
    one = ScatterDirect(*got, ns, nz)
    two.step()
    one.step()
    dctx, _ = after(dctx, (one.last, two.last))
    r1 = r1.reshape(seqs, rows, model)
    backs = []
    for s in range(seqs):
        back = attend_back(ns, s, lengths, timesteps, idx, q, k, v, fronts[s][1], fronts[s][2], w_qkv, dctx)
        back, two.moving = hold(back, two.moving)
        backs.append(back)
        two.step()
        dctx, _ = after(dctx, two.last)
    low, _ = after(low, two.last)
    keep, send = qkv_grad(
        ns, nz, r, idx, low, backs[0][0], backs[1][0], sums, backs[0][3], backs[1][3], backs[0][4], backs[1][4]
    )
    near = [keep, to_mate(send)]

    one.terms[-1], near[0] = hold(one.terms[-1], near[0])
    one.step()
    one.terms[-1], near[1] = hold(one.terms[-1], near[1])
    planes = [[b[1], b[2]] for b in backs]
    planes, _ = after(planes, one.terms[-1])
    planes = [[p[0], to_bit(p[1], high - 1)] for p in planes]
    one.step()
    near, two.moving, planes, one.terms = hold(near, two.moving, planes, one.terms)
    two.fix()
    near_z = [to_z(added([t[a] for t in near]).astype(BF16), a) for a in range(1, nz)]
    two.step()
    n = ns // 2
    while n > 1:
        away = added_rows([[t[n // 2 : n] for t in p] for p in planes])
        n //= 2
        got = to_bit(away, n.bit_length() - 1)
        planes = [p + [got[i]] for i, p in enumerate(planes)]
    near_z, two.terms, planes = hold(near_z, two.terms, planes)
    own = added([t[0] for t in near] + near_z)
    others = [to_seq(own[n].astype(BF16), n) for n in range(1, ns)]
    grad_down = two.finish()
    grad_tokens = jnp.stack([added([t[0] for t in p] + [r1[s]]).astype(BF16) for s, p in enumerate(planes)])
    g_query, g_key, g_value, vectors = finish(ns, r, model, idx, own[0], others)
    return (
        output,
        grad_tokens,
        g_query,
        vectors[0],
        g_key,
        g_value,
        vectors[1],
        one.finish(slice(0, model)),
        vectors[2],
        vectors[3],
        vectors[4],
        one.finish(slice(model, 5 * model)),
        one.finish(slice(5 * model, 5 * model + 4 * r), 0),
        grad_down,
        vectors[5],
        vectors[6],
        vectors[7],
        vectors[8],
        vectors[9],
    )


def solution(mesh):
    split = P(("dp", "seq"))
    rows = P(("dp", "seq"), None)
    token = P("dp", "seq", None)
    items = P("dp", None)
    return jax.shard_map(
        body,
        mesh=mesh,
        in_specs=(
            token, items, items, rows, split, rows, rows, split, rows, split, split, split,
            rows, split, rows, split, split, split, split, split, token,
        ),
        out_specs=(
            token, token, rows, split, rows, rows, split, rows, split, split, split,
            rows, split, rows, split, split, split, split, split,
        ),
        check_vma=False,
    )
```

```python
import functools

import jax
import jax.numpy as jnp
from jax import lax
from jax.experimental import pallas as pl
from jax.experimental.pallas import tpu as pltpu
from jax.sharding import PartitionSpec as P

HD = 64
TSTEPS = 5000
EPSILON = 1e-05
NEGATIVE = -1e30
ROOT_HALF = 0.7071067811865476
DENSITY_SCALE = 0.3989422804014327
PAD = 128
WIDE = 512
BF16 = jnp.bfloat16
F32 = jnp.float32
VMEM = pltpu.VMEM
SMEM = pltpu.SMEM


def nn(a, b):
    return lax.dot_general(a, b, (((1,), (0,)), ((), ())), preferred_element_type=F32)


def nt(a, b):
    return lax.dot_general(a, b, (((1,), (1,)), ((), ())), preferred_element_type=F32)


def flipped_bits(value, count):
    return sum(((value >> i) & 1) << (count - 1 - i) for i in range(count))


def tn(a, b):
    return lax.dot_general(a, b, (((0,), (0,)), ((), ())), preferred_element_type=F32)


def shift_of(ns, core, slot):
    other = flipped_bits(slot, ns.bit_length() - 1)
    return slot + core * (other - slot)


def vspec():
    return pl.BlockSpec(memory_space=VMEM)


def sspec():
    return pl.BlockSpec(memory_space=SMEM)


def aspec():
    return pl.BlockSpec(memory_space=pl.ANY)


def params(mib, grid=0):
    if grid:
        return pltpu.CompilerParams(
            vmem_limit_bytes=mib << 20, dimension_semantics=("arbitrary",) * grid
        )
    return pltpu.CompilerParams(vmem_limit_bytes=mib << 20)


def cost(flops, nbytes, trans=0):
    return pl.CostEstimate(flops=int(flops), bytes_accessed=int(nbytes), transcendentals=int(trans))


def tau_rows(len_ref, tim_ref, seq, first, rows):
    spot = first + lax.broadcasted_iota(jnp.int32, (rows, 128), 0)
    begin = jnp.int32(0)
    step = jnp.zeros((rows, 128), jnp.int32)
    for i in range(len_ref.shape[1]):
        end = begin + len_ref[seq, i]
        step = jnp.where((spot >= begin) & (spot < end), tim_ref[seq, i], step)
        begin = end
    return (step.astype(F32) / TSTEPS)[:, :1]


def segments(len_ref, seq, spot):
    end = jnp.int32(0)
    found = jnp.zeros(spot.shape, jnp.int32)
    for i in range(len_ref.shape[1]):
        end = end + len_ref[seq, i]
        found = found + (spot >= end).astype(jnp.int32)
    return found


def item_bias(len_ref, seq, first, keys, rows, out_ref):
    mine = segments(len_ref, seq, first + lax.broadcasted_iota(jnp.int32, (8, rows), 1))
    theirs = segments(len_ref, seq, lax.broadcasted_iota(jnp.int32, (keys, 128), 0))
    for lane in range(rows // 128):
        same = theirs == mine[:1, lane * 128 : (lane + 1) * 128]
        out_ref[:, lane * 128 : (lane + 1) * 128] = jnp.where(same, 0.0, NEGATIVE)


def fold(block):
    rows, width = block.shape
    return block.reshape(rows // 8, 8, width)


def pack_kernel(ns, count, idx, *refs):
    srcs, (out_ref, outer_ref), dsts, sem = refs[:count], refs[count : count + 2], refs[count + 2 : -1], refs[-1]
    r, model = srcs[0].shape
    ff = srcs[-2].shape[1]
    hg = model // ns
    targets = list(dsts) + [outer_ref.at[:, 0:model], outer_ref.at[:, model : model + ff]]
    targets.append(outer_ref.at[:, model + ff + PAD :])
    srcs = list(srcs[:-1]) + [srcs[-1].at[0:r]]
    copies = [pltpu.make_async_copy(a, b, sem.at[n]) for n, (a, b) in enumerate(zip(srcs, targets))]
    for copy in copies:
        copy.start()
    for copy in copies:
        copy.wait()
    c, j = idx[1], idx[2]
    rows = [v[...].astype(F32).reshape(1, r) for v in dsts[3:-1]]
    rows.append(jnp.zeros((PAD - len(rows), r), F32))
    small = jnp.concatenate(rows, axis=0).T.astype(BF16)
    for m in range(ns):
        at = pl.ds(pl.multiple_of((j ^ shift_of(ns, c, m)) * hg, 128), hg)
        for n in range(3):
            out_ref[m, :, n * hg : (n + 1) * hg] = dsts[n][:, at]
        out_ref[m, :, 3 * hg :] = small
    row = dsts[-1][...].astype(F32).reshape(1, 4 * r)
    if PAD > 4 * r:
        row = jnp.concatenate([row, jnp.zeros((1, PAD - 4 * r), F32)], axis=1)
    outer_ref[:, model + ff : model + ff + PAD] = jnp.broadcast_to(row, (r, PAD)).astype(BF16)


def pack(ns, idx, w_query, w_key, w_value, vectors, b_up, w_out, w_up, w_down):
    r, model = w_query.shape
    args = (w_query, w_key, w_value, *vectors, b_up, w_out, w_up, w_down)
    return pl.pallas_call(
        functools.partial(pack_kernel, ns, len(args)),
        name="pack",
        out_shape=[
            jax.ShapeDtypeStruct((ns, r, 3 * (model // ns) + PAD), BF16),
            jax.ShapeDtypeStruct((r, model + w_up.shape[1] + PAD + model), BF16),
        ],
        in_specs=[sspec()] + [aspec()] * len(args),
        out_specs=[vspec()] * 2,
        scratch_shapes=[VMEM(a.shape, a.dtype) for a in args[:-3]]
        + [pltpu.SemaphoreType.DMA((len(args),))],
        compiler_params=params(60),
    )(idx, *args)


def qkv_kernel(ns, nz, r, len_ref, tim_ref, idx, *refs):
    toks = refs[:2]
    qa, qb = refs[2:4]
    q_ref, k_ref, v_ref, low_ref, w_ref, small_ref, wide = refs[4:]
    z, c, j = idx[0], idx[1], idx[2]
    half, seqs, rows, model = toks[0].shape
    hg = q_ref.shape[2]
    for cc, src in enumerate((qa, qb)):
        for a in range(nz):
            for b in range(ns):
                d = ((z ^ a) * 2 + (c ^ cc)) * ns + (j ^ shift_of(ns, c ^ cc, b))
                wide[pl.ds(pl.multiple_of(d * r, r), r), :] = src[a, b].astype(wide.dtype)
    w_ref[...] = wide[:, : 3 * hg].astype(BF16)
    small_ref[...] = wide[:, 3 * hg :].astype(F32).T[:16, :]
    heads = pl.ds(pl.multiple_of(j * hg, 128), hg)
    bq = small_ref[0:1, heads]
    bv = small_ref[1:2, heads]
    wt = small_ref[8:9, :]
    bt = small_ref[9:10, :]
    for k in range(ns):
        first = pl.multiple_of((j ^ shift_of(ns, c, k)) * rows, rows)
        here = pl.ds(first, rows)
        for s in range(seqs):
            tau = tau_rows(len_ref, tim_ref, s, first, rows)
            low = (toks[k // half][k % half, s].astype(F32) + tau * wt + bt).astype(BF16)
            low_ref[s, here, :] = low
            got = nn(low, w_ref[...])
            q_ref[s, here, :] = ((got[:, :hg] + bq) * (HD**-0.5)).astype(BF16)
            k_ref[s, here, :] = got[:, hg : 2 * hg].astype(BF16)
            v_ref[s, here, :] = (got[:, 2 * hg :] + bv).astype(BF16)


def project(ns, nz, lengths, timesteps, idx, toks, qa, qb):
    seqs, rows, model = toks[0].shape[1:]
    r = qa.shape[2]
    hg = (qa.shape[3] - PAD) // 3
    full = rows * ns
    heads = jax.ShapeDtypeStruct((seqs, full, hg), BF16)
    outs = [
        heads,
        heads,
        heads,
        jax.ShapeDtypeStruct((seqs, full, model), BF16),
        jax.ShapeDtypeStruct((model, 3 * hg), BF16),
        jax.ShapeDtypeStruct((16, model), F32),
    ]
    return pl.pallas_call(
        functools.partial(qkv_kernel, ns, nz, r),
        name="project",
        out_shape=outs,
        in_specs=[sspec()] * 3 + [vspec()] * 4,
        out_specs=[vspec()] * 6,
        scratch_shapes=[VMEM((model, 3 * hg + PAD), BF16 if r % 16 == 0 else F32)],
        compiler_params=params(58),
        cost_estimate=cost(2 * seqs * full * model * 3 * hg, 14 << 20),
    )(lengths, timesteps, idx, *toks, qa, qb)


PAIR = 128
QUERIES = 512


def slots_of(full):
    return 2 if full <= 1024 else 1


def item_bias_all(len_ref, seq, bias):
    keys = bias.shape[0]
    for b in range(keys // QUERIES):
        item_bias(len_ref, seq, b * QUERIES, keys, QUERIES, bias.at[:, b * QUERIES : (b + 1) * QUERIES])


def attend_kernel(ns, s, len_ref, idx, q_ref, k_ref, v_ref, *refs):
    refs = refs[ns:] if s else refs
    ctx_refs = refs[:ns]
    ctxf_ref, lse_ref, bias, probs, scale = refs[ns:]
    j = idx[2]
    full = k_ref.shape[1]
    rows = full // ns

    alone = whole_sequence(len_ref, s, full)

    @pl.when((pl.program_id(0) == 0) & jnp.logical_not(alone))
    def _():
        item_bias_all(len_ref, s, bias)

    scale[...] = jnp.zeros_like(scale)
    lse_ref[...] = jnp.zeros_like(lse_ref)

    def heads(add):
        attend_heads(full, add, q_ref, k_ref, v_ref, ctxf_ref, lse_ref, probs, scale)

    pl.when(alone)(lambda: heads(lambda st, at: st))
    pl.when(jnp.logical_not(alone))(lambda: heads(lambda st, at: st + bias[:, at]))
    for k in range(ns):
        here = pl.ds(pl.multiple_of((j ^ k) * rows, rows), rows)
        ctx_refs[k][0] = ctxf_ref[0, here, :].astype(BF16)


def whole_sequence(len_ref, seq, full):
    end = jnp.int32(0)
    same = jnp.bool_(True)
    for i in range(len_ref.shape[1]):
        end = end + len_ref[seq, i]
        same = same & ((end <= 0) | (end >= full))
    return same


def attend_heads(full, add, q_ref, k_ref, v_ref, ctxf_ref, lse_ref, probs, scale):
    for h in range(PAIR // HD):
        cols = slice(h * HD, (h + 1) * HD)
        kh, vh = k_ref[0, :, cols], v_ref[0, :, cols]
        for b in range(full // QUERIES):
            at = slice(b * QUERIES, (b + 1) * QUERIES)
            st = add(nt(kh, q_ref[0, at, cols]), at)
            top = jnp.max(jnp.max(fold(st), axis=0), axis=0, keepdims=True)
            p = jnp.exp(st - top)
            total = jnp.sum(jnp.sum(fold(p), axis=0), axis=0, keepdims=True)
            probs[h % probs.shape[0], :, at] = p.astype(BF16)
            scale[h : h + 1, at] = 1.0 / total
            lse_ref[0, h : h + 1, at] = top + jnp.log(total)
        by_row = scale[...].T
        ctxf_ref[0, :, cols] = tn(probs[h % probs.shape[0]], vh) * by_row[:, h : h + 1]


def attend(ns, seq, lengths, idx, q, k, v, before):
    seqs, full, hg = q.shape
    rows = full // ns
    groups = hg // PAIR
    outs = [jax.ShapeDtypeStruct((seqs, rows, hg), BF16)] * ns + [
        jax.ShapeDtypeStruct((1, full, hg), F32),
        jax.ShapeDtypeStruct((1, 8 * groups, full), F32),
    ]
    wide = pl.BlockSpec((1, full, PAIR), lambda i: (seq, 0, i))
    res = pl.pallas_call(
        functools.partial(attend_kernel, ns, seq),
        name="attend",
        out_shape=outs,
        grid=(groups,),
        in_specs=[sspec(), sspec(), wide, wide, wide] + [aspec()] * len(before),
        out_specs=[pl.BlockSpec((1, rows, PAIR), lambda i: (seq, 0, i))] * ns
        + [
            pl.BlockSpec((1, full, PAIR), lambda i: (0, 0, i)),
            pl.BlockSpec((1, 8, full), lambda i: (0, i, 0)),
        ],
        scratch_shapes=[
            VMEM((full, full), F32),
            VMEM((slots_of(full), full, full), BF16),
            VMEM((8, full), F32),
        ],
        compiler_params=params(58, 1),
        cost_estimate=cost(4 * 4 * full * full * hg, 4 << 20),
        input_output_aliases={5 + n: n for n in range(len(before))},
    )(lengths, idx, q, k, v, *before)
    return res[:ns], res[ns], res[ns + 1]


def attend_back_kernel(ns, seq, len_ref, tim_ref, idx, q_ref, k_ref, v_ref, ctxf_ref, lse_ref, w_ref, *refs):
    dctx = refs[:ns]
    grad_ref, pk_ref, ps_ref, sum_ref, bsum_ref, bias, dcx, probs, score = refs[ns:]
    i = pl.program_id(0)
    c, j = idx[1], idx[2]
    full = k_ref.shape[1]
    rows = full // ns
    hg = grad_ref.shape[1] // 3

    alone = whole_sequence(len_ref, seq, full)

    @pl.when((i == 0) & jnp.logical_not(alone))
    def _():
        item_bias_all(len_ref, seq, bias)

    for k in range(ns):
        dcx[pl.ds(pl.multiple_of((j ^ k) * rows, rows), rows), :] = dctx[k][0]

    def heads(add):
        back_heads(full, add, i, q_ref, k_ref, v_ref, ctxf_ref, lse_ref, grad_ref, dcx, probs, score)

    pl.when(alone)(lambda: heads(lambda st, at: st))
    pl.when(jnp.logical_not(alone))(lambda: heads(lambda st, at: st + bias[:, at]))
    @pl.when(i == pl.num_programs(0) - 1)
    def _():
        plain = jnp.zeros((8, w_ref.shape[0]), F32)
        timed = jnp.zeros((8, w_ref.shape[0]), F32)
        bias_sum = jnp.zeros((8, 3 * hg), F32)
        for k in range(ns):
            first = pl.multiple_of((j ^ shift_of(ns, c, k)) * rows, rows)
            block = grad_ref[pl.ds(first, rows), :]
            part = nt(block, w_ref[...])
            (pk_ref if k < ns // 2 else ps_ref)[k % (ns // 2)] = part.astype(BF16)
            plain = plain + jnp.sum(fold(part), axis=0)
            tau = tau_rows(len_ref, tim_ref, seq, first, rows)
            timed = timed + jnp.sum(fold(part * tau), axis=0)
            bias_sum = bias_sum + jnp.sum(fold(block.astype(F32)), axis=0)
        sum_ref[...] = jnp.zeros_like(sum_ref)
        sum_ref[0:1, :] = jnp.sum(timed, axis=0, keepdims=True)
        sum_ref[1:2, :] = jnp.sum(plain, axis=0, keepdims=True)
        bsum_ref[...] = jnp.broadcast_to(jnp.sum(bias_sum, axis=0, keepdims=True), bsum_ref.shape)


def back_heads(full, add, i, q_ref, k_ref, v_ref, ctxf_ref, lse_ref, grad_ref, dcx, probs, score):
    grads = []
    for h in range(PAIR // HD):
        cols = slice(h * HD, (h + 1) * HD)
        qh, kh, vh = q_ref[0, :, cols], k_ref[0, :, cols], v_ref[0, :, cols]
        dch = dcx[:, cols]
        row_total = jnp.sum((ctxf_ref[0, :, cols] * dch.astype(F32)).T, axis=0, keepdims=True)
        for b in range(full // QUERIES):
            at = slice(b * QUERIES, (b + 1) * QUERIES)
            p = jnp.exp(add(nt(kh, qh[at, :]), at) - lse_ref[0, h : h + 1, at])
            ds = p * (nt(vh, dch[at, :]) - row_total[:, at])
            probs[h % probs.shape[0], :, at] = p.astype(BF16)
            score[h % score.shape[0], :, at] = ds.astype(BF16)
        dq = tn(score[h % score.shape[0]], kh).astype(BF16).astype(F32) * (HD**-0.5)
        grads.append((dq, nn(score[h % score.shape[0]], qh), nn(probs[h % probs.shape[0]], dch)))
    hg = grad_ref.shape[1] // 3
    for n in range(3):
        at = pl.ds(pl.multiple_of(n * hg + i * PAIR, PAIR), PAIR)
        grad_ref[:, at] = jnp.concatenate([g[n] for g in grads], axis=1).astype(BF16)


def attend_back(ns, seq, lengths, timesteps, idx, q, k, v, ctxf, lse, w, dctx):
    seqs, full, hg = q.shape
    rows = full // ns
    groups = hg // PAIR
    model = w.shape[0]
    one = lambda shape: pl.BlockSpec(shape, lambda i: (0,) * len(shape))
    wide = pl.BlockSpec((1, full, PAIR), lambda i: (seq, 0, i))
    outs = (
        [jax.ShapeDtypeStruct((full, 3 * hg), BF16)]
        + [jax.ShapeDtypeStruct((ns // 2, rows, model), BF16)] * 2
        + [jax.ShapeDtypeStruct((8, model), F32), jax.ShapeDtypeStruct((8, 3 * hg), F32)]
    )
    return pl.pallas_call(
        functools.partial(attend_back_kernel, ns, seq),
        name="attend_back",
        out_shape=outs,
        grid=(groups,),
        in_specs=[sspec()] * 3
        + [
            wide,
            wide,
            wide,
            pl.BlockSpec((1, full, PAIR), lambda i: (0, 0, i)),
            pl.BlockSpec((1, 8, full), lambda i: (0, i, 0)),
            one((model, 3 * hg)),
        ]
        + [pl.BlockSpec((1, rows, PAIR), lambda i: (seq, 0, i))] * ns,
        out_specs=[one((full, 3 * hg))]
        + [one((ns // 2, rows, model))] * 2
        + [one((8, model)), one((8, 3 * hg))],
        scratch_shapes=[
            VMEM((full, full), F32),
            VMEM((full, PAIR), BF16),
            VMEM((slots_of(full), full, full), BF16),
            VMEM((slots_of(full), full, full), BF16),
        ],
        compiler_params=params(58, 1),
        cost_estimate=cost(10 * 4 * full * full * hg, 10 << 20),
    )(lengths, timesteps, idx, q, k, v, ctxf, lse, w, *dctx)


def middle_kernel(ns, nz, r, len_ref, tim_ref, idx, tok_ref, cot_ref, small_ref, *refs):
    ctxs = refs[:ns]
    refs = refs[ns:]
    outer, dn, rest = refs[:4], refs[4 : 4 + 2 * nz], refs[4 + 2 * nz :]
    out_ref, keep_o, send_o, ahead_o, ug_o, fl_o, cx_o, ag_o, r1_o = rest[:9]
    rest = rest[1:]
    dctx = rest[8 : 8 + ns]
    sum_ref, gbup_ref = rest[8 + ns : 10 + ns]
    wu, wd, act, slope, ug, fl, cx, dg, first, norm, inv, stage, bup_ref, slots, wsem, osem, gsem = rest[10 + ns :]
    z, c, j = idx[0], idx[1], idx[2]
    seqs, rows, model = tok_ref.shape
    ff = wd.shape[0]
    hg = ctxs[0].shape[2]
    tokens = seqs * rows
    ends = (0, model, wu.shape[1], wu.shape[1] + model)
    for part in range(3):
        at = slice(ends[part], ends[part + 1])
        for n, src in enumerate(outer):
            core = c ^ (n // 2)
            for m in range(ns // 2):
                shift = shift_of(ns, core, m + (n % 2) * (ns // 2))
                for a in range(nz):
                    d = ((z ^ a) * 2 + core) * ns + (j ^ shift)
                    if part < 2:
                        dst = wu.at[pl.ds(pl.multiple_of(d * r, r), r), at]
                    else:
                        dst = wd.at[pl.ds(pl.multiple_of(d * 4 * r, 4 * r), r), :]
                    pltpu.make_async_copy(src.at[m, a, :, at], dst, wsem.at[part]).start()
    for n, src in enumerate(dn):
        core = c ^ (n % 2)
        for m in range(ns):
            d = (lax.rem(z + nz - n // 2, nz) * 2 + core) * ns + (j ^ shift_of(ns, core, m))
            pltpu.make_async_copy(
                src.at[m],
                wd.at[pl.ds(pl.multiple_of(d * 4 * r + r, r), 3 * r), :],
                wsem.at[2],
            ).start()
    for k in range(ns):
        at = pl.ds(pl.multiple_of((j ^ k) * hg, 128), hg)
        for s in range(seqs):
            cx[s * rows : (s + 1) * rows, at] = ctxs[k][s]
    sum_ref[...] = jnp.zeros_like(sum_ref)
    pltpu.make_async_copy(cx, cx_o, osem.at[0]).start()
    u1_all = wu.at[:, 0 : ends[1]]
    pltpu.make_async_copy(u1_all, u1_all, wsem.at[0]).wait()

    b_out = small_ref[2:3, :]
    gain_one, shift_one = small_ref[3:4, :], small_ref[4:5, :]
    b_down = small_ref[5:6, :]
    gain_two, shift_two = small_ref[6:7, :], small_ref[7:8, :]
    w_time, b_time = small_ref[8:9, :], small_ref[9:10, :]
    block = rows
    per = 1

    def add_sum(row, value):
        sum_ref[row : row + 1, :] += jnp.sum(jnp.sum(fold(value), axis=0), axis=0, keepdims=True)

    def mean(value):
        return jnp.sum(value, axis=-1, keepdims=True) * (1.0 / model)

    def one_first(s, b):
        at = pl.ds(pl.multiple_of((s * per + b) * block, block), block)
        inside = pl.ds(pl.multiple_of(b * block, block), block)
        attn = nn(cx[at, :], wu[:, 0:model])
        tau = tau_rows(len_ref, tim_ref, s, j * rows + b * block, block)
        start = tok_ref[s, inside, :].astype(F32) + tau * w_time + b_time
        res = start + (attn + b_out)
        center = res - mean(res)
        inverse = lax.rsqrt(mean(center * center) + EPSILON)
        normed = center * inverse
        norm[at, :] = normed
        inv[at, :] = jnp.broadcast_to(inverse, (block, 128))
        value = normed * gain_one + shift_one
        first[at, :] = value
        fl[at, :] = value.astype(BF16)

    for s in range(seqs):
        one_first(s, 0)
    pltpu.make_async_copy(fl, fl_o, osem.at[1]).start()
    u2_all = wu.at[:, ends[1] : ends[2]]
    pltpu.make_async_copy(u2_all, u2_all, wsem.at[1]).wait()
    for d in range(ns * nz * 2):
        bup_ref[0:1, d * 4 * r : (d + 1) * 4 * r] = wu[d * r : d * r + 1, model + ff : model + ff + 4 * r].astype(F32)

    def one_up(n, _):
        at = pl.ds(pl.multiple_of(n * WIDE, WIDE), WIDE)
        wat = pl.ds(pl.multiple_of(model + n * WIDE, WIDE), WIDE)
        for h in range(2):
            rr = slice(h * tokens // 2, (h + 1) * tokens // 2)
            pre = nn(fl[rr, :], wu[:, wat]) + bup_ref[0:1, at]
            cumulative = 0.5 * (1.0 + lax.erf(pre * ROOT_HALF))
            density = jnp.exp(-0.5 * pre * pre) * DENSITY_SCALE
            act[rr, at] = (pre * cumulative).astype(BF16)
            slope[rr, at] = cumulative + pre * density
        return 0

    lax.fori_loop(0, ff // WIDE, one_up, 0)
    pltpu.make_async_copy(wd, wd, wsem.at[2]).wait()

    def one_second(s, b):
        at = pl.ds(pl.multiple_of((s * per + b) * block, block), block)
        inside = pl.ds(pl.multiple_of(b * block, block), block)
        res = first[at, :] + (nn(act[at, :], wd[...]) + b_down)
        center = res - mean(res)
        inverse = lax.rsqrt(mean(center * center) + EPSILON)
        normed = center * inverse
        out_ref[s, inside, :] = (normed * gain_two + shift_two).astype(BF16)
        g = cot_ref[s, inside, :].astype(F32)
        add_sum(4, g * normed)
        add_sum(5, g)
        gn = g * gain_two
        grad = inverse * (gn - mean(gn) - normed * mean(gn * normed))
        first[at, :] = grad
        low = grad.astype(BF16)
        dg[at, :] = low
        add_sum(3, low.astype(F32))

    for s in range(seqs):
        one_second(s, 0)

    wide = ns * 4 * r

    def grad_copy(n):
        a = n % nz
        dst = keep_o.at[a] if n >= nz else ahead_o.at[0] if a == nz - 1 else send_o.at[a]
        return pltpu.make_async_copy(slots.at[n % 2], dst, gsem.at[n % 2])

    for n in range(2 * nz):
        core = c ^ 1 if n < nz else c
        own = pl.multiple_of((lax.rem(z + n % nz, nz) * 2 + core) * wide, wide)
        total = tn(act[:, pl.ds(own, wide)], dg[...])
        if n >= 2:
            grad_copy(n - 2).wait()
        for b in range(ns):
            slots[n % 2, place_of(ns, core, j ^ b)] = total[b * 4 * r : (b + 1) * 4 * r].astype(BF16)
        grad_copy(n).start()

    def one_up_grad(n, _):
        at = pl.ds(pl.multiple_of(n * WIDE, WIDE), WIDE)
        total = jnp.zeros((8, WIDE), F32)
        for h in range(2):
            rr = slice(h * tokens // 2, (h + 1) * tokens // 2)
            low = (nt(dg[rr, :], wd[at, :]) * slope[rr, at]).astype(BF16)
            ug[rr, at] = low
            total = total + jnp.sum(fold(low.astype(F32)), axis=0)
        row = jnp.sum(total, axis=0, keepdims=True)
        for m in range(WIDE // (4 * r)):
            gbup_ref[pl.ds(n * (WIDE // (4 * r)) + m, 1), :] = row[:, m * 4 * r : (m + 1) * 4 * r]
        return 0

    lax.fori_loop(0, ff // WIDE, one_up_grad, 0)
    pltpu.make_async_copy(ug, ug_o, osem.at[4]).start()
    pltpu.make_async_copy(fl, fl_o, osem.at[1]).wait()

    def one_first_grad(s, b):
        at = pl.ds(pl.multiple_of((s * per + b) * block, block), block)
        inside = pl.ds(pl.multiple_of(b * block, block), block)
        fg = nt(ug[at, :], wu[:, model : model + ff]) + first[at, :]
        normed = norm[at, :]
        add_sum(1, fg * normed)
        add_sum(2, fg)
        gn = fg * gain_one
        grad = inv[at, :][:, :1] * (gn - mean(gn) - normed * mean(gn * normed))
        first[at, :] = grad
        low = grad.astype(BF16)
        fl[at, :] = low
        add_sum(0, low.astype(F32))
        tau = tau_rows(len_ref, tim_ref, s, j * rows + b * block, block)
        add_sum(6, grad * tau)
        add_sum(7, grad)
        stage[...] = nt(low, wu[:, 0:model]).astype(BF16)
        for k in range(ns):
            cols = pl.ds(pl.multiple_of((j ^ k) * hg, 128), hg)
            dctx[k][s, inside, :] = stage[:, cols]

    for s in range(seqs):
        one_first_grad(s, 0)
    ag_copy = pltpu.make_async_copy(fl, ag_o, osem.at[5])
    ag_copy.start()
    r1_copy = pltpu.make_async_copy(first, r1_o, osem.at[6])
    r1_copy.start()
    pltpu.make_async_copy(cx, cx_o, osem.at[0]).wait()
    for n in (2 * nz - 2, 2 * nz - 1):
        grad_copy(n).wait()
    pltpu.make_async_copy(ug, ug_o, osem.at[4]).wait()
    ag_copy.wait()
    r1_copy.wait()


def middle(ns, nz, r, lengths, timesteps, idx, tokens, cotangent, small, ctxs, outer, dn):
    seqs, rows, model = tokens.shape
    total = seqs * rows
    ff = 4 * r * ns * nz * 2
    hg = ctxs[0].shape[2]
    sh = lambda *a: jax.ShapeDtypeStruct(a[:-1], a[-1])
    outs = [
        sh(seqs, rows, model, BF16),
        sh(nz, ns, 4 * r, model, BF16),
        sh(nz - 1, ns, 4 * r, model, BF16),
        sh(1, ns, 4 * r, model, BF16),
        sh(total, ff, BF16),
        sh(total, model, BF16),
        sh(total, model, BF16),
        sh(total, model, BF16),
        sh(total, model, F32),
    ]
    outs += [sh(seqs, rows, hg, BF16)] * ns + [sh(16, model, F32), sh(ff // (4 * r), 4 * r, F32)]
    res = pl.pallas_call(
        functools.partial(middle_kernel, ns, nz, r),
        name="middle",
        out_shape=outs,
        in_specs=[sspec()] * 3
        + [vspec()] * (3 + ns)
        + [aspec()] * (len(outer) + len(dn)),
        out_specs=[vspec()] + [aspec()] * 8 + [vspec()] * (ns + 2),
        scratch_shapes=[
            VMEM((model, model + ff + PAD), BF16),
            VMEM((ff, model), BF16),
            VMEM((total, ff), BF16),
            VMEM((total, ff), F32),
            VMEM((total, ff), BF16),
            VMEM((total, model), BF16),
            VMEM((total, model), BF16),
            VMEM((total, model), BF16),
            VMEM((total, model), F32),
            VMEM((total, model), F32),
            VMEM((total, 128), F32),
            VMEM((rows, model), BF16),
            VMEM((8, ff), F32),
            VMEM((2, ns, 4 * r, model), BF16),
            pltpu.SemaphoreType.DMA((3,)),
            pltpu.SemaphoreType.DMA((7,)),
            pltpu.SemaphoreType.DMA((2,)),
        ],
        compiler_params=params(60),
        cost_estimate=cost(
            2 * total * (2 * model * model + 4 * model * ff), 40 << 20, 3 * total * ff
        ),
    )(lengths, timesteps, idx, tokens, cotangent, small, *ctxs, *outer, *dn)
    return res[:9], res[9 : 9 + ns], res[9 + ns], res[10 + ns]


def place_of(ns, core, offset):
    return offset + core * (flipped_bits(offset, ns.bit_length() - 1) - offset)


def gather_columns(ns, nz, r, core, idx, src, dst, first):
    wide = ns * r
    for a in range(nz):
        pair = pl.multiple_of((idx[0] ^ a) * 2 * wide, 2 * wide)
        if wide % 128 == 0:
            got = src[:, pl.ds(pl.multiple_of(pair + core * wide, wide), wide)]
        else:
            both = src[:, pl.ds(pair, 2 * wide)]
            got = jnp.where(core == 0, both[:, :wide], both[:, wide:])
        dst[:, first + a * wide : first + (a + 1) * wide] = got


def store_halves(ns, nz, r, core, idx, total, low, high):
    for b in range(ns):
        slot = place_of(ns, core, idx[2] ^ b)

        def put(dst, slot):
            for a in range(nz):
                n = (a * ns + b) * r
                dst[a, slot] = total[n : n + r].astype(BF16)

        pl.when(slot < ns // 2)(lambda: put(low, slot))
        pl.when(slot >= ns // 2)(lambda: put(high, slot - ns // 2))


def store_slots(ns, nz, r, core, walk, idx, total, dst, at=slice(None)):
    for a in range(nz):
        for b in range(ns):
            slot = place_of(ns, core if walk else 0, idx[2] ^ b)
            n = (a * ns + b) * r
            dst[a, slot, :, at] = total[n : n + r].astype(BF16)


def up_grad_kernel(ns, nz, r, idx, cx_ref, ag_ref, fl_ref, ug_ref, gbup_ref, keep_ref, send_ref, ahead_ref, left):
    i = pl.program_id(0)
    split = ag_ref.shape[1] // WIDE
    last = pl.num_programs(0) - 1
    half = cx_ref.shape[1] // 2
    c = idx[1]

    def both(right):
        total = tn(left[...], right)
        store_slots(ns, nz, r, c, True, idx, total[:half], keep_ref)
        store_halves(ns, nz, r, c ^ 1, idx, total[half:], send_ref, ahead_ref)

    @pl.when(i == 0)
    def _():
        gather_columns(ns, nz, r, c, idx, cx_ref, left, 0)
        gather_columns(ns, nz, r, c ^ 1, idx, cx_ref, left, half)

    @pl.when(i < split)
    def _():
        both(ag_ref[:, pl.ds(pl.multiple_of(jnp.minimum(i, split - 1) * WIDE, WIDE), WIDE)])

    @pl.when(i == split)
    def _():
        gather_columns(ns, nz, r, c, idx, fl_ref, left, 0)
        gather_columns(ns, nz, r, c ^ 1, idx, fl_ref, left, half)

    @pl.when((i >= split) & (i < last))
    def _():
        both(ug_ref[...])

    @pl.when(i == last)
    def _():
        for dst in (keep_ref, send_ref, ahead_ref):
            dst[...] = jnp.zeros_like(dst)
        for cc in range(2):
            core = c ^ cc
            for a in range(nz):
                for b in range(ns):
                    d = ((idx[0] ^ a) * 2 + core) * ns + (idx[2] ^ shift_of(ns, core, b))
                    row = gbup_ref[pl.ds(d, 1), :]
                    dst = keep_ref if cc == 0 else send_ref if b < ns // 2 else ahead_ref
                    dst[a, b if cc == 0 else b % (ns // 2), :, 0 : 4 * r] = jnp.broadcast_to(row, (r, 4 * r)).astype(BF16)


def up_grad(ns, nz, r, idx, cx, ag, fl, ug, gbup):
    total, model = fl.shape
    ff = ug.shape[1]
    width = model + ff + PAD
    split, top = model // WIDE, ff // WIDE - 1
    one = lambda shape: pl.BlockSpec(shape, lambda i: (0,) * len(shape))
    block = lambda n: pl.BlockSpec((nz, n, r, WIDE), lambda i: (0, 0, 0, i))
    return pl.pallas_call(
        functools.partial(up_grad_kernel, ns, nz, r),
        name="up_grad",
        out_shape=[jax.ShapeDtypeStruct((nz, ns, r, width), BF16)]
        + [jax.ShapeDtypeStruct((nz, ns // 2, r, width), BF16)] * 2,
        grid=(pl.cdiv(width, WIDE),),
        in_specs=[
            sspec(),
            one(cx.shape),
            one(ag.shape),
            one(fl.shape),
            pl.BlockSpec((total, WIDE), lambda i: (0, jnp.minimum(jnp.maximum(i - split, 0), top))),
            one(gbup.shape),
        ],
        out_specs=[block(ns), block(ns // 2), block(ns // 2)],
        scratch_shapes=[VMEM((total, model), BF16)],
        compiler_params=params(58, 1),
        cost_estimate=cost(2 * total * model * width, 10 << 20),
    )(idx, cx, ag, fl, ug, gbup)


def qkv_grad_kernel(ns, nz, r, idx, low_ref, g0_ref, g1_ref, sums_ref, s0_ref, s1_ref, b0_ref, b1_ref, keep_ref, send_ref, left, vec, tall):
    c, j = idx[1], idx[2]
    hg = g0_ref.shape[1] // 3
    vec[...] = jnp.zeros_like(vec)
    heads = pl.ds(pl.multiple_of(j * hg, 128), hg)
    both = b0_ref[0:1, :] + b1_ref[0:1, :]
    vec[0:1, heads] = both[:, :hg]
    vec[1:2, heads] = both[:, 2 * hg :]
    vec[2:8, :] = sums_ref[0:6, :]
    vec[8:10, :] = sums_ref[6:8, :] + s0_ref[0:2, :] + s1_ref[0:2, :]
    tall[...] = vec[...].T
    half = left.shape[1] // 2
    for cc, dst in enumerate((keep_ref, send_ref)):
        core = c ^ cc
        total = 0.0
        for s, g in enumerate((g0_ref, g1_ref)):
            gather_columns(ns, nz, r, core, idx, low_ref.at[s], left, cc * half)
            total = total + tn(left[:, cc * half : (cc + 1) * half], g[...])
        store_slots(ns, nz, r, 0, False, idx, total, dst, slice(0, 3 * hg))
        for a in range(nz):
            for b in range(ns):
                d = ((idx[0] ^ a) * 2 + core) * ns + (j ^ b)
                dst[a, b, :, 3 * hg :] = tall[pl.ds(pl.multiple_of(d * r, r), r), :].astype(BF16)


def qkv_grad(ns, nz, r, idx, low, g0, g1, sums, s0, s1, b0, b1):
    seqs, full, model = low.shape
    width = g0.shape[1] + PAD
    out = jax.ShapeDtypeStruct((nz, ns, r, width), BF16)
    return pl.pallas_call(
        functools.partial(qkv_grad_kernel, ns, nz, r),
        name="qkv_grad",
        out_shape=[out, out],
        in_specs=[sspec()] + [vspec()] * 8,
        out_specs=[vspec()] * 2,
        scratch_shapes=[
            VMEM((full, model), BF16),
            VMEM((PAD, model), F32),
            VMEM((model, PAD), F32),
        ],
        compiler_params=params(58),
        cost_estimate=cost(2 * seqs * full * model * width, 12 << 20),
    )(idx, low, g0, g1, sums, s0, s1, b0, b1)


def finish_kernel(ns, r, idx, own_ref, *refs):
    others = refs[: ns - 1]
    q_ref, k_ref, v_ref, small_ref = refs[ns - 1 :]
    j = idx[2]
    hg = (own_ref.shape[1] - PAD) // 3
    small = own_ref[:, 3 * hg :]
    for k in range(ns):
        part = own_ref[...] if k == 0 else others[k - 1][...].astype(F32)
        cols = pl.ds(pl.multiple_of((j ^ k) * hg, 128), hg)
        for n, dst in enumerate((q_ref, k_ref, v_ref)):
            dst[:, cols] = part[:, n * hg : (n + 1) * hg]
        if k:
            small = small + part[:, 3 * hg :]
    small_ref[...] = small.T[:16, :]


def finish(ns, r, model, idx, own, others):
    out = jax.ShapeDtypeStruct((r, model), F32)
    return pl.pallas_call(
        functools.partial(finish_kernel, ns, r),
        name="finish",
        out_shape=[out, out, out, jax.ShapeDtypeStruct((16, r), F32)],
        in_specs=[sspec()] + [vspec()] * ns,
        out_specs=[vspec()] * 4,
        compiler_params=params(16),
    )(idx, own, *others)


def to_seq(value, k):
    ns = lax.axis_size("seq")
    return lax.ppermute(value, "seq", [(i, i ^ k) for i in range(ns)])


def to_mate(value):
    nd = lax.axis_size("dp")
    return lax.ppermute(value, "dp", [(i, i ^ 1) for i in range(nd)])


def to_z(value, a):
    nd = lax.axis_size("dp")
    return lax.ppermute(value, "dp", [(i, i ^ (2 * a)) for i in range(nd)])


def to_ring(value):
    nd = lax.axis_size("dp")
    return lax.ppermute(value, "dp", [(i, (i + 2) % nd) for i in range(nd)])


def to_bit(value, place):
    ns, nd = lax.axis_size("seq"), lax.axis_size("dp")
    high = ns.bit_length() - 2
    pairs = []
    for dp in range(nd):
        bit = 1 << (high - place if dp % 2 else place)
        pairs += [(dp * ns + i, dp * ns + (i ^ bit)) for i in range(ns)]
    return lax.ppermute(value, ("dp", "seq"), pairs)


def gather_plane(block, ns):
    cur = block[None]
    high = ns.bit_length() - 2
    for place in range(high):
        cur = jnp.concatenate([cur, to_bit(cur, place)], axis=0)
    return [cur, to_bit(cur, high)]


def exchange_plane(blocks, ns):
    kept = [blocks[m] for m in range(ns)]
    early = None
    for place in range(ns.bit_length() - 1):
        bit = 1 << place
        away = [m for m in range(ns) if m & bit]
        got = to_bit(jnp.stack([kept[m] for m in away]), place)
        early = got if early is None else early
        for n, m in enumerate(away):
            kept[m] = got[n]
    return jnp.stack(kept), early


def added(terms):
    return functools.reduce(lambda a, b: a + b, [t.astype(F32) for t in terms])


def added_rows(lists):
    return jnp.stack([added(terms) for terms in lists]).astype(BF16)


def hold(*values):
    return lax.optimization_barrier(values)


def after(values, others):
    return lax.optimization_barrier((values, others))


class Scatter:
    def __init__(self, keep, send, ahead, ns, nz):
        self.ns, self.nz = ns, nz
        self.ahead = to_mate(ahead)
        self.terms = [keep]
        self.send = send
        self.last = None

    def fetch(self):
        self.terms = self.terms + [to_mate(self.send)]

    def bit(self):
        half = self.ns // 2
        parts = [t[: self.nz, half : self.ns] for t in self.terms[: 2 if self.ahead is None else 1]]
        parts += [t[: self.nz, half : self.ns] for t in self.terms[2:]]
        if isinstance(self, ScatterDirect) and self.ahead is not None:
            parts, self.ahead = parts + [self.ahead], None
        self.last = added(parts).astype(BF16)
        self.got = to_bit(self.last, self.ns.bit_length() - 2)
        self.ns = half

    def take(self):
        self.terms = self.terms + [self.got]

    def total(self, at=slice(None), row=slice(None)):
        return added([t[0, 0, row, at] for t in self.terms])


class ScatterDirect(Scatter):
    def all_z(self):
        self.last = [added([t[a, 0] for t in self.terms]).astype(BF16) for a in range(1, self.nz)]
        self.got = [to_z(v, a + 1)[None, None] for a, v in enumerate(self.last)]
        self.nz = 1

    def take_z(self):
        self.terms = self.terms + list(self.got)


class ScatterRing(Scatter):
    def ring(self):
        self.nz -= 1
        if self.ahead is not None:
            parts, self.ahead = [self.terms[0][self.nz], self.ahead[0]], None
        else:
            parts = [t[self.nz] for t in self.terms] + [self.got]
        self.last = added(parts).astype(BF16)
        self.got = to_ring(self.last)

    def take_ring(self):
        self.terms = self.terms + [self.got[None]]


def body(
    tokens,
    lengths,
    timesteps,
    w_query,
    b_query,
    w_key,
    w_value,
    b_value,
    w_out,
    b_out,
    gain_one,
    shift_one,
    w_up,
    b_up,
    w_down,
    b_down,
    gain_two,
    shift_two,
    w_time,
    b_time,
    cotangent,
):
    seqs, rows, model = tokens.shape
    ns = lax.axis_size("seq")
    nz = lax.axis_size("dp") // 2
    r = w_query.shape[0]
    hg = model // ns
    dp = lax.axis_index("dp")
    j = lax.axis_index("seq")
    idx = jnp.stack([dp // 2, dp % 2, j]).astype(jnp.int32)

    high = ns.bit_length() - 1
    vectors = [b_query, b_value, b_out, gain_one, shift_one, b_down, gain_two, shift_two, w_time, b_time]
    mine, outer = pack(ns, idx, w_query, w_key, w_value, vectors, b_up, w_out, w_up, w_down)
    tok, down = tokens[None], w_down[r:][None]
    kept = [mine[m] for m in range(ns)]
    outer_z, near_z = [], []
    waiting = list(range(1, nz))
    for place in range(high):
        got = [to_bit(tok, place), to_bit(down, place) if place < high - 1 else None]
        away = [m for m in range(ns) if m & (1 << place)]
        pieces = to_bit(jnp.stack([kept[m] for m in away]), place)
        now = waiting[:2] if place < high - 1 else waiting
        waiting = waiting[len(now) :]
        outer_z = outer_z + [to_z(outer, a) for a in now]
        tok, down, outer, kept, got, pieces, outer_z = hold(tok, down, outer, kept, got, pieces, outer_z)
        for n, m in enumerate(away):
            kept[m] = pieces[n]
        if place < high - 1:
            tok = jnp.concatenate([tok, got[0]], axis=0)
            down = jnp.concatenate([down, got[1]], axis=0)
    toks = [tok, got[0]]
    near = jnp.stack(kept)
    near_z = [to_z(near, a) for a in range(1, nz)]
    cur = jnp.stack([outer] + outer_z)[None]
    down_next, cur_next = to_bit(down, high - 1), to_bit(cur, 0)
    toks, near, near_z, down, down_next, cur, cur_next = hold(
        toks, near, near_z, down, down_next, cur, cur_next
    )
    qa = jnp.stack([near] + near_z)
    qb = to_mate(qa)
    down = jnp.concatenate([down, down_next], axis=0)
    downs = [down, to_ring(down)]
    for place in range(1, high):
        cur = jnp.concatenate([cur, cur_next], axis=0)
        cur_next = to_bit(cur, place)
    qa, _ = after(qa, (down, cur))

    projected = project(ns, nz, lengths, timesteps, idx, toks, qa, qb)
    q, k, v, low, w_qkv, small = projected
    mates, _ = after([cur, down], qb)
    fronts, mates, before = [], [to_mate(m) for m in mates], []
    for s in range(seqs):
        front = attend(ns, s, lengths, idx, q, k, v, before)
        front, downs, mates = hold(front, downs, mates)
        downs.append(to_ring(downs[-1]))
        if s == 0:
            mates = list(mates) + [to_mate(downs[1])]
        else:
            front, cur_next = hold(front, cur_next)
        fronts.append(front)
        before = front[0]
        q, _ = after(q, front[0])
    ctxs = [before[0]] + [to_seq(before[n], n) for n in range(1, ns)]
    while len(downs) < nz:
        downs.append(to_ring(downs[-1]))
    ctxs, downs = hold(ctxs, downs)
    outer = [cur, cur_next, mates[0], to_mate(cur_next)]
    mates = list(mates[1:]) + [to_mate(d) for d in downs[2:]]
    downs = [x for pair in zip(downs, mates) for x in pair]
    kept, dctx_out, sums, gbup = middle(
        ns, nz, r, lengths, timesteps, idx, tokens, cotangent, small, ctxs, outer, downs
    )
    output, keep, send, ahead, ug, fl, cx, ag, r1 = kept

    two = ScatterRing(keep, send, ahead, ns, nz)
    dctx = [to_seq(dctx_out[n], n) for n in range(1, ns)]
    two.send, two.ahead = hold(two.send, two.ahead)
    two.fetch()
    two.ring()
    (fl, ug), _ = after((fl, ug), (dctx_out, two.last))
    got = up_grad(ns, nz, r, idx, cx, ag, fl, ug, gbup)
    got, dctx, two.got, two.terms = hold(got, dctx, two.got, two.terms)
    dctx = [dctx_out[0]] + list(dctx)
    one = ScatterDirect(*got, ns, nz)
    two.ring()
    one.bit()
    one.send, _ = after(one.send, one.last)
    one.fetch()
    dctx, _ = after(dctx, (one.last, two.last))
    r1 = r1.reshape(seqs, rows, model)
    backs, planes = [], []
    for s in range(seqs):
        back = attend_back(ns, s, lengths, timesteps, idx, q, k, v, fronts[s][1], fronts[s][2], w_qkv, dctx)
        back, two.got, one.got, planes = hold(back, two.got, one.got, planes)
        backs.append(back)
        planes = list(planes)
        one.take()
        sent = []
        if two.nz > 1:
            two.ring()
            sent.append(two.last)
        if one.ns > 1:
            one.bit()
            sent.append(one.last)
        elif one.nz > 1:
            one.all_z()
            sent.append(one.last)
        away = after(back[2], sent)[0] if s else back[2]
        planes.append([back[1], to_bit(away, high - 1)])
        dctx, _ = after(dctx, (sent, back[2]))
    two.got, _ = after(two.got, one.last)
    while two.nz > 1:
        two.ring()
    two.take_ring()
    while one.ns > 1:
        one.take()
        one.bit()
    if one.nz > 1:
        one.take()
        one.all_z()
    low, _ = after(low, (one.last, backs[-1][2]))
    keep, send = qkv_grad(
        ns, nz, r, idx, low, backs[0][0], backs[1][0], sums, backs[0][3], backs[1][3], backs[0][4], backs[1][4]
    )
    keep, send, one.got, planes = hold(keep, send, one.got, planes)
    near = [keep, to_mate(send)]
    one.take_z()
    two.bit()
    n = ns // 2
    away = []
    while n > 1:
        away = added_rows([[t[n // 2 : n] for t in p] for p in planes])
        n //= 2
        got = to_bit(away, n.bit_length() - 1)
        planes = [list(p) + [got[i]] for i, p in enumerate(planes)]
    near[0], _ = after(near[0], (two.last, away))
    away = [added([t[a] for t in near]).astype(BF16) for a in range(1, nz)]
    near_z = [to_z(v, a + 1) for a, v in enumerate(away)]
    one.terms, _ = after(one.terms, near_z[-1])
    ends = (slice(0, model), slice(model, 5 * model))
    outs = [one.total(at) for at in ends] + [one.total(slice(5 * model, 5 * model + 4 * r), 0)]
    near_z, two.got, planes, outs = hold(near_z, two.got, planes, outs)
    two.take()
    while two.ns > 1:
        two.bit()
        two.take()
    own = added([t[0] for t in near] + near_z)
    others = [to_seq(own[n].astype(BF16), n) for n in range(1, ns)]
    grad_down = two.total()
    grad_tokens = jnp.stack([added([t[0] for t in p] + [r1[s]]).astype(BF16) for s, p in enumerate(planes)])
    g_query, g_key, g_value, vectors = finish(ns, r, model, idx, own[0], others)
    return (
        output,
        grad_tokens,
        g_query,
        vectors[0],
        g_key,
        g_value,
        vectors[1],
        outs[0],
        vectors[2],
        vectors[3],
        vectors[4],
        outs[1],
        outs[2],
        grad_down,
        vectors[5],
        vectors[6],
        vectors[7],
        vectors[8],
        vectors[9],
    )


def solution(mesh):
    split = P(("dp", "seq"))
    rows = P(("dp", "seq"), None)
    token = P("dp", "seq", None)
    items = P("dp", None)
    return jax.shard_map(
        body,
        mesh=mesh,
        in_specs=(
            token, items, items, rows, split, rows, rows, split, rows, split, split, split,
            rows, split, rows, split, split, split, split, split, token,
        ),
        out_specs=(
            token, token, rows, split, rows, rows, split, rows, split, split, split,
            rows, split, rows, split, split, split, split, split,
        ),
        check_vma=False,
    )
```

```python
import functools

import jax
import jax.numpy as jnp
from jax import lax
from jax.experimental import pallas as pl
from jax.experimental.pallas import tpu as pltpu
from jax.sharding import PartitionSpec as P

HD = 64
TSTEPS = 5000
EPSILON = 1e-05
NEGATIVE = -1e30
ROOT_HALF = 0.7071067811865476
DENSITY_SCALE = 0.3989422804014327
PAD = 128
WIDE = 512
BF16 = jnp.bfloat16
F32 = jnp.float32
VMEM = pltpu.VMEM
SMEM = pltpu.SMEM


def nn(a, b):
    return lax.dot_general(a, b, (((1,), (0,)), ((), ())), preferred_element_type=F32)


def nt(a, b):
    return lax.dot_general(a, b, (((1,), (1,)), ((), ())), preferred_element_type=F32)


def flipped_bits(value, count):
    return sum(((value >> i) & 1) << (count - 1 - i) for i in range(count))


def tn(a, b):
    return lax.dot_general(a, b, (((0,), (0,)), ((), ())), preferred_element_type=F32)


def shift_of(ns, core, slot):
    other = flipped_bits(slot, ns.bit_length() - 1)
    return slot + core * (other - slot)


def vspec():
    return pl.BlockSpec(memory_space=VMEM)


def sspec():
    return pl.BlockSpec(memory_space=SMEM)


def aspec():
    return pl.BlockSpec(memory_space=pl.ANY)


def params(mib, grid=0):
    if grid:
        return pltpu.CompilerParams(
            vmem_limit_bytes=mib << 20, dimension_semantics=("arbitrary",) * grid
        )
    return pltpu.CompilerParams(vmem_limit_bytes=mib << 20)


def cost(flops, nbytes, trans=0):
    return pl.CostEstimate(flops=int(flops), bytes_accessed=int(nbytes), transcendentals=int(trans))


def tau_rows(len_ref, tim_ref, seq, first, rows):
    spot = first + lax.broadcasted_iota(jnp.int32, (rows, 128), 0)
    begin = jnp.int32(0)
    step = jnp.zeros((rows, 128), jnp.int32)
    for i in range(len_ref.shape[1]):
        end = begin + len_ref[seq, i]
        step = jnp.where((spot >= begin) & (spot < end), tim_ref[seq, i], step)
        begin = end
    return (step.astype(F32) / TSTEPS)[:, :1]


def segments(len_ref, seq, spot):
    end = jnp.int32(0)
    found = jnp.zeros(spot.shape, jnp.int32)
    for i in range(len_ref.shape[1]):
        end = end + len_ref[seq, i]
        found = found + (spot >= end).astype(jnp.int32)
    return found


def item_bias(len_ref, seq, first, keys, rows, out_ref):
    mine = segments(len_ref, seq, first + lax.broadcasted_iota(jnp.int32, (8, rows), 1))
    theirs = segments(len_ref, seq, lax.broadcasted_iota(jnp.int32, (keys, 128), 0))
    for lane in range(rows // 128):
        same = theirs == mine[:1, lane * 128 : (lane + 1) * 128]
        out_ref[:, lane * 128 : (lane + 1) * 128] = jnp.where(same, 0.0, NEGATIVE)


def fold(block):
    rows, width = block.shape
    return block.reshape(rows // 8, 8, width)


def pack_kernel(ns, count, idx, *refs):
    srcs, (out_ref, outer_ref), dsts, sem = refs[:count], refs[count : count + 2], refs[count + 2 : -1], refs[-1]
    r, model = srcs[0].shape
    ff = srcs[-2].shape[1]
    hg = model // ns
    targets = list(dsts) + [outer_ref.at[:, 0:model], outer_ref.at[:, model : model + ff]]
    targets.append(outer_ref.at[:, model + ff + PAD :])
    srcs = list(srcs[:-1]) + [srcs[-1].at[0:r]]
    copies = [pltpu.make_async_copy(a, b, sem.at[n]) for n, (a, b) in enumerate(zip(srcs, targets))]
    for copy in copies:
        copy.start()
    for copy in copies:
        copy.wait()
    c, j = idx[1], idx[2]
    rows = [v[...].astype(F32).reshape(1, r) for v in dsts[3:-1]]
    rows.append(jnp.zeros((PAD - len(rows), r), F32))
    small = jnp.concatenate(rows, axis=0).T.astype(BF16)
    for m in range(ns):
        at = pl.ds(pl.multiple_of((j ^ shift_of(ns, c, m)) * hg, 128), hg)
        for n in range(3):
            out_ref[m, :, n * hg : (n + 1) * hg] = dsts[n][:, at]
        out_ref[m, :, 3 * hg :] = small
    row = dsts[-1][...].astype(F32).reshape(1, 4 * r)
    if PAD > 4 * r:
        row = jnp.concatenate([row, jnp.zeros((1, PAD - 4 * r), F32)], axis=1)
    outer_ref[:, model + ff : model + ff + PAD] = jnp.broadcast_to(row, (r, PAD)).astype(BF16)


def pack(ns, idx, w_query, w_key, w_value, vectors, b_up, w_out, w_up, w_down):
    r, model = w_query.shape
    args = (w_query, w_key, w_value, *vectors, b_up, w_out, w_up, w_down)
    return pl.pallas_call(
        functools.partial(pack_kernel, ns, len(args)),
        name="pack",
        out_shape=[
            jax.ShapeDtypeStruct((ns, r, 3 * (model // ns) + PAD), BF16),
            jax.ShapeDtypeStruct((r, model + w_up.shape[1] + PAD + model), BF16),
        ],
        in_specs=[sspec()] + [aspec()] * len(args),
        out_specs=[vspec()] * 2,
        scratch_shapes=[VMEM(a.shape, a.dtype) for a in args[:-3]]
        + [pltpu.SemaphoreType.DMA((len(args),))],
        compiler_params=params(60),
    )(idx, *args)


def qkv_kernel(ns, nz, r, len_ref, tim_ref, idx, *refs):
    toks = refs[:2]
    qa, qb = refs[2:4]
    q_ref, k_ref, v_ref, low_ref, w_ref, small_ref, wide = refs[4:]
    z, c, j = idx[0], idx[1], idx[2]
    half, seqs, rows, model = toks[0].shape
    hg = q_ref.shape[2]
    for cc, src in enumerate((qa, qb)):
        for a in range(nz):
            for b in range(ns):
                d = ((z ^ a) * 2 + (c ^ cc)) * ns + (j ^ shift_of(ns, c ^ cc, b))
                wide[pl.ds(pl.multiple_of(d * r, r), r), :] = src[a, b].astype(wide.dtype)
    w_ref[...] = wide[:, : 3 * hg].astype(BF16)
    small_ref[...] = wide[:, 3 * hg :].astype(F32).T[:16, :]
    heads = pl.ds(pl.multiple_of(j * hg, 128), hg)
    bq = small_ref[0:1, heads]
    bv = small_ref[1:2, heads]
    wt = small_ref[8:9, :]
    bt = small_ref[9:10, :]
    for k in range(ns):
        first = pl.multiple_of((j ^ shift_of(ns, c, k)) * rows, rows)
        here = pl.ds(first, rows)
        for s in range(seqs):
            tau = tau_rows(len_ref, tim_ref, s, first, rows)
            low = (toks[k // half][k % half, s].astype(F32) + tau * wt + bt).astype(BF16)
            low_ref[s, here, :] = low
            got = nn(low, w_ref[...])
            q_ref[s, here, :] = ((got[:, :hg] + bq) * (HD**-0.5)).astype(BF16)
            k_ref[s, here, :] = got[:, hg : 2 * hg].astype(BF16)
            v_ref[s, here, :] = (got[:, 2 * hg :] + bv).astype(BF16)


def project(ns, nz, lengths, timesteps, idx, toks, qa, qb):
    seqs, rows, model = toks[0].shape[1:]
    r = qa.shape[2]
    hg = (qa.shape[3] - PAD) // 3
    full = rows * ns
    heads = jax.ShapeDtypeStruct((seqs, full, hg), BF16)
    outs = [
        heads,
        heads,
        heads,
        jax.ShapeDtypeStruct((seqs, full, model), BF16),
        jax.ShapeDtypeStruct((model, 3 * hg), BF16),
        jax.ShapeDtypeStruct((16, model), F32),
    ]
    return pl.pallas_call(
        functools.partial(qkv_kernel, ns, nz, r),
        name="project",
        out_shape=outs,
        in_specs=[sspec()] * 3 + [vspec()] * 4,
        out_specs=[vspec()] * 6,
        scratch_shapes=[VMEM((model, 3 * hg + PAD), BF16 if r % 16 == 0 else F32)],
        compiler_params=params(58),
        cost_estimate=cost(2 * seqs * full * model * 3 * hg, 14 << 20),
    )(lengths, timesteps, idx, *toks, qa, qb)


PAIR = 128
QUERIES = 512


def slots_of(full):
    return 2 if full <= 1024 else 1


def item_bias_all(len_ref, seq, bias):
    keys = bias.shape[0]
    for b in range(keys // QUERIES):
        item_bias(len_ref, seq, b * QUERIES, keys, QUERIES, bias.at[:, b * QUERIES : (b + 1) * QUERIES])


def attend_kernel(ns, s, len_ref, idx, q_ref, k_ref, v_ref, *refs):
    refs = refs[ns:] if s else refs
    ctx_refs = refs[:ns]
    ctxf_ref, lse_ref, bias, probs, scale = refs[ns:]
    j = idx[2]
    full = k_ref.shape[1]
    rows = full // ns

    alone = whole_sequence(len_ref, s, full)

    @pl.when((pl.program_id(0) == 0) & jnp.logical_not(alone))
    def _():
        item_bias_all(len_ref, s, bias)

    scale[...] = jnp.zeros_like(scale)
    lse_ref[...] = jnp.zeros_like(lse_ref)

    def heads(add):
        attend_heads(full, add, q_ref, k_ref, v_ref, ctxf_ref, lse_ref, probs, scale)

    pl.when(alone)(lambda: heads(lambda st, at: st))
    pl.when(jnp.logical_not(alone))(lambda: heads(lambda st, at: st + bias[:, at]))
    for k in range(ns):
        here = pl.ds(pl.multiple_of((j ^ k) * rows, rows), rows)
        ctx_refs[k][0] = ctxf_ref[0, here, :].astype(BF16)


def whole_sequence(len_ref, seq, full):
    end = jnp.int32(0)
    same = jnp.bool_(True)
    for i in range(len_ref.shape[1]):
        end = end + len_ref[seq, i]
        same = same & ((end <= 0) | (end >= full))
    return same


def attend_heads(full, add, q_ref, k_ref, v_ref, ctxf_ref, lse_ref, probs, scale):
    for h in range(PAIR // HD):
        cols = slice(h * HD, (h + 1) * HD)
        kh, vh = k_ref[0, :, cols], v_ref[0, :, cols]
        for b in range(full // QUERIES):
            at = slice(b * QUERIES, (b + 1) * QUERIES)
            st = add(nt(kh, q_ref[0, at, cols]), at)
            top = jnp.max(jnp.max(fold(st), axis=0), axis=0, keepdims=True)
            p = jnp.exp(st - top)
            total = jnp.sum(jnp.sum(fold(p), axis=0), axis=0, keepdims=True)
            probs[h % probs.shape[0], :, at] = p.astype(BF16)
            scale[h : h + 1, at] = 1.0 / total
            lse_ref[0, h : h + 1, at] = top + jnp.log(total)
        by_row = scale[...].T
        ctxf_ref[0, :, cols] = tn(probs[h % probs.shape[0]], vh) * by_row[:, h : h + 1]


def attend(ns, seq, lengths, idx, q, k, v, before):
    seqs, full, hg = q.shape
    rows = full // ns
    groups = hg // PAIR
    outs = [jax.ShapeDtypeStruct((seqs, rows, hg), BF16)] * ns + [
        jax.ShapeDtypeStruct((1, full, hg), F32),
        jax.ShapeDtypeStruct((1, 8 * groups, full), F32),
    ]
    wide = pl.BlockSpec((1, full, PAIR), lambda i: (seq, 0, i))
    res = pl.pallas_call(
        functools.partial(attend_kernel, ns, seq),
        name="attend",
        out_shape=outs,
        grid=(groups,),
        in_specs=[sspec(), sspec(), wide, wide, wide] + [aspec()] * len(before),
        out_specs=[pl.BlockSpec((1, rows, PAIR), lambda i: (seq, 0, i))] * ns
        + [
            pl.BlockSpec((1, full, PAIR), lambda i: (0, 0, i)),
            pl.BlockSpec((1, 8, full), lambda i: (0, i, 0)),
        ],
        scratch_shapes=[
            VMEM((full, full), F32),
            VMEM((slots_of(full), full, full), BF16),
            VMEM((8, full), F32),
        ],
        compiler_params=params(58, 1),
        cost_estimate=cost(4 * 4 * full * full * hg, 4 << 20),
        input_output_aliases={5 + n: n for n in range(len(before))},
    )(lengths, idx, q, k, v, *before)
    return res[:ns], res[ns], res[ns + 1]


def attend_back_kernel(ns, seq, len_ref, tim_ref, idx, q_ref, k_ref, v_ref, ctxf_ref, lse_ref, w_ref, *refs):
    dctx = refs[:ns]
    grad_ref, pk_ref, ps_ref, sum_ref, bsum_ref, bias, dcx, probs, score = refs[ns:]
    i = pl.program_id(0)
    c, j = idx[1], idx[2]
    full = k_ref.shape[1]
    rows = full // ns
    hg = grad_ref.shape[1] // 3

    alone = whole_sequence(len_ref, seq, full)

    @pl.when((i == 0) & jnp.logical_not(alone))
    def _():
        item_bias_all(len_ref, seq, bias)

    for k in range(ns):
        dcx[pl.ds(pl.multiple_of((j ^ k) * rows, rows), rows), :] = dctx[k][0]

    def heads(add):
        back_heads(full, add, i, q_ref, k_ref, v_ref, ctxf_ref, lse_ref, grad_ref, dcx, probs, score)

    pl.when(alone)(lambda: heads(lambda st, at: st))
    pl.when(jnp.logical_not(alone))(lambda: heads(lambda st, at: st + bias[:, at]))
    @pl.when(i == pl.num_programs(0) - 1)
    def _():
        plain = jnp.zeros((8, w_ref.shape[0]), F32)
        timed = jnp.zeros((8, w_ref.shape[0]), F32)
        bias_sum = jnp.zeros((8, 3 * hg), F32)
        for k in range(ns):
            first = pl.multiple_of((j ^ shift_of(ns, c, k)) * rows, rows)
            block = grad_ref[pl.ds(first, rows), :]
            part = nt(block, w_ref[...])
            (pk_ref if k < ns // 2 else ps_ref)[k % (ns // 2)] = part.astype(BF16)
            plain = plain + jnp.sum(fold(part), axis=0)
            tau = tau_rows(len_ref, tim_ref, seq, first, rows)
            timed = timed + jnp.sum(fold(part * tau), axis=0)
            bias_sum = bias_sum + jnp.sum(fold(block.astype(F32)), axis=0)
        sum_ref[...] = jnp.zeros_like(sum_ref)
        sum_ref[0:1, :] = jnp.sum(timed, axis=0, keepdims=True)
        sum_ref[1:2, :] = jnp.sum(plain, axis=0, keepdims=True)
        bsum_ref[...] = jnp.broadcast_to(jnp.sum(bias_sum, axis=0, keepdims=True), bsum_ref.shape)


def back_heads(full, add, i, q_ref, k_ref, v_ref, ctxf_ref, lse_ref, grad_ref, dcx, probs, score):
    grads = []
    for h in range(PAIR // HD):
        cols = slice(h * HD, (h + 1) * HD)
        qh, kh, vh = q_ref[0, :, cols], k_ref[0, :, cols], v_ref[0, :, cols]
        dch = dcx[:, cols]
        row_total = jnp.sum((ctxf_ref[0, :, cols] * dch.astype(F32)).T, axis=0, keepdims=True)
        for b in range(full // QUERIES):
            at = slice(b * QUERIES, (b + 1) * QUERIES)
            p = jnp.exp(add(nt(kh, qh[at, :]), at) - lse_ref[0, h : h + 1, at])
            ds = p * (nt(vh, dch[at, :]) - row_total[:, at])
            probs[h % probs.shape[0], :, at] = p.astype(BF16)
            score[h % score.shape[0], :, at] = ds.astype(BF16)
        dq = tn(score[h % score.shape[0]], kh).astype(BF16).astype(F32) * (HD**-0.5)
        grads.append((dq, nn(score[h % score.shape[0]], qh), nn(probs[h % probs.shape[0]], dch)))
    hg = grad_ref.shape[1] // 3
    for n in range(3):
        at = pl.ds(pl.multiple_of(n * hg + i * PAIR, PAIR), PAIR)
        grad_ref[:, at] = jnp.concatenate([g[n] for g in grads], axis=1).astype(BF16)


def attend_back(ns, seq, lengths, timesteps, idx, q, k, v, ctxf, lse, w, dctx):
    seqs, full, hg = q.shape
    rows = full // ns
    groups = hg // PAIR
    model = w.shape[0]
    one = lambda shape: pl.BlockSpec(shape, lambda i: (0,) * len(shape))
    wide = pl.BlockSpec((1, full, PAIR), lambda i: (seq, 0, i))
    outs = (
        [jax.ShapeDtypeStruct((full, 3 * hg), BF16)]
        + [jax.ShapeDtypeStruct((ns // 2, rows, model), BF16)] * 2
        + [jax.ShapeDtypeStruct((8, model), F32), jax.ShapeDtypeStruct((8, 3 * hg), F32)]
    )
    return pl.pallas_call(
        functools.partial(attend_back_kernel, ns, seq),
        name="attend_back",
        out_shape=outs,
        grid=(groups,),
        in_specs=[sspec()] * 3
        + [
            wide,
            wide,
            wide,
            pl.BlockSpec((1, full, PAIR), lambda i: (0, 0, i)),
            pl.BlockSpec((1, 8, full), lambda i: (0, i, 0)),
            one((model, 3 * hg)),
        ]
        + [pl.BlockSpec((1, rows, PAIR), lambda i: (seq, 0, i))] * ns,
        out_specs=[one((full, 3 * hg))]
        + [one((ns // 2, rows, model))] * 2
        + [one((8, model)), one((8, 3 * hg))],
        scratch_shapes=[
            VMEM((full, full), F32),
            VMEM((full, PAIR), BF16),
            VMEM((slots_of(full), full, full), BF16),
            VMEM((slots_of(full), full, full), BF16),
        ],
        compiler_params=params(58, 1),
        cost_estimate=cost(10 * 4 * full * full * hg, 10 << 20),
    )(lengths, timesteps, idx, q, k, v, ctxf, lse, w, *dctx)


def middle_kernel(ns, nz, r, len_ref, tim_ref, idx, tok_ref, cot_ref, small_ref, *refs):
    ctxs = refs[:ns]
    refs = refs[ns:]
    outer, dn, rest = refs[:4], refs[4 : 4 + 2 * nz], refs[4 + 2 * nz :]
    out_ref, keep_o, send_o, ahead_o, ug_o, fl_o, cx_o, ag_o, r1_o = rest[:9]
    rest = rest[1:]
    dctx = rest[8 : 8 + ns]
    sum_ref, gbup_ref = rest[8 + ns : 10 + ns]
    wu, wd, act, slope, ug, fl, cx, dg, first, norm, inv, stage, bup_ref, slots, wsem, osem, gsem = rest[10 + ns :]
    z, c, j = idx[0], idx[1], idx[2]
    seqs, rows, model = tok_ref.shape
    ff = wd.shape[0]
    hg = ctxs[0].shape[2]
    tokens = seqs * rows
    ends = (0, model, wu.shape[1], wu.shape[1] + model)
    for part in range(3):
        at = slice(ends[part], ends[part + 1])
        for n, src in enumerate(outer):
            core = c ^ (n // 2)
            for m in range(ns // 2):
                shift = shift_of(ns, core, m + (n % 2) * (ns // 2))
                for a in range(nz):
                    d = ((z ^ a) * 2 + core) * ns + (j ^ shift)
                    if part < 2:
                        dst = wu.at[pl.ds(pl.multiple_of(d * r, r), r), at]
                    else:
                        dst = wd.at[pl.ds(pl.multiple_of(d * 4 * r, 4 * r), r), :]
                    pltpu.make_async_copy(src.at[m, a, :, at], dst, wsem.at[part]).start()
    for n, src in enumerate(dn):
        core = c ^ (n % 2)
        for m in range(ns):
            d = (lax.rem(z + nz - n // 2, nz) * 2 + core) * ns + (j ^ shift_of(ns, core, m))
            pltpu.make_async_copy(
                src.at[m],
                wd.at[pl.ds(pl.multiple_of(d * 4 * r + r, r), 3 * r), :],
                wsem.at[2],
            ).start()
    for k in range(ns):
        at = pl.ds(pl.multiple_of((j ^ k) * hg, 128), hg)
        for s in range(seqs):
            cx[s * rows : (s + 1) * rows, at] = ctxs[k][s]
    sum_ref[...] = jnp.zeros_like(sum_ref)
    pltpu.make_async_copy(cx, cx_o, osem.at[0]).start()
    u1_all = wu.at[:, 0 : ends[1]]
    pltpu.make_async_copy(u1_all, u1_all, wsem.at[0]).wait()

    b_out = small_ref[2:3, :]
    gain_one, shift_one = small_ref[3:4, :], small_ref[4:5, :]
    b_down = small_ref[5:6, :]
    gain_two, shift_two = small_ref[6:7, :], small_ref[7:8, :]
    w_time, b_time = small_ref[8:9, :], small_ref[9:10, :]
    block = rows
    per = 1

    def add_sum(row, value):
        sum_ref[row : row + 1, :] += jnp.sum(jnp.sum(fold(value), axis=0), axis=0, keepdims=True)

    def mean(value):
        return jnp.sum(value, axis=-1, keepdims=True) * (1.0 / model)

    def one_first(s, b):
        at = pl.ds(pl.multiple_of((s * per + b) * block, block), block)
        inside = pl.ds(pl.multiple_of(b * block, block), block)
        attn = nn(cx[at, :], wu[:, 0:model])
        tau = tau_rows(len_ref, tim_ref, s, j * rows + b * block, block)
        start = tok_ref[s, inside, :].astype(F32) + tau * w_time + b_time
        res = start + (attn + b_out)
        center = res - mean(res)
        inverse = lax.rsqrt(mean(center * center) + EPSILON)
        normed = center * inverse
        norm[at, :] = normed
        inv[at, :] = jnp.broadcast_to(inverse, (block, 128))
        value = normed * gain_one + shift_one
        first[at, :] = value
        fl[at, :] = value.astype(BF16)

    for s in range(seqs):
        one_first(s, 0)
    pltpu.make_async_copy(fl, fl_o, osem.at[1]).start()
    u2_all = wu.at[:, ends[1] : ends[2]]
    pltpu.make_async_copy(u2_all, u2_all, wsem.at[1]).wait()
    for d in range(ns * nz * 2):
        bup_ref[0:1, d * 4 * r : (d + 1) * 4 * r] = wu[d * r : d * r + 1, model + ff : model + ff + 4 * r].astype(F32)

    def one_up(n, _):
        at = pl.ds(pl.multiple_of(n * WIDE, WIDE), WIDE)
        wat = pl.ds(pl.multiple_of(model + n * WIDE, WIDE), WIDE)
        for h in range(2):
            rr = slice(h * tokens // 2, (h + 1) * tokens // 2)
            pre = nn(fl[rr, :], wu[:, wat]) + bup_ref[0:1, at]
            cumulative = 0.5 * (1.0 + lax.erf(pre * ROOT_HALF))
            density = jnp.exp(-0.5 * pre * pre) * DENSITY_SCALE
            act[rr, at] = (pre * cumulative).astype(BF16)
            slope[rr, at] = cumulative + pre * density
        return 0

    lax.fori_loop(0, ff // WIDE, one_up, 0)
    pltpu.make_async_copy(wd, wd, wsem.at[2]).wait()

    def one_second(s, b):
        at = pl.ds(pl.multiple_of((s * per + b) * block, block), block)
        inside = pl.ds(pl.multiple_of(b * block, block), block)
        res = first[at, :] + (nn(act[at, :], wd[...]) + b_down)
        center = res - mean(res)
        inverse = lax.rsqrt(mean(center * center) + EPSILON)
        normed = center * inverse
        out_ref[s, inside, :] = (normed * gain_two + shift_two).astype(BF16)
        g = cot_ref[s, inside, :].astype(F32)
        add_sum(4, g * normed)
        add_sum(5, g)
        gn = g * gain_two
        grad = inverse * (gn - mean(gn) - normed * mean(gn * normed))
        first[at, :] = grad
        low = grad.astype(BF16)
        dg[at, :] = low
        add_sum(3, low.astype(F32))

    for s in range(seqs):
        one_second(s, 0)

    wide = ns * 4 * r

    def grad_copy(n):
        a = n % nz
        dst = keep_o.at[a] if n >= nz else ahead_o.at[0] if a == nz - 1 else send_o.at[a]
        return pltpu.make_async_copy(slots.at[n % 2], dst, gsem.at[n % 2])

    for n in range(2 * nz):
        core = c ^ 1 if n < nz else c
        own = pl.multiple_of((lax.rem(z + n % nz, nz) * 2 + core) * wide, wide)
        total = tn(act[:, pl.ds(own, wide)], dg[...])
        if n >= 2:
            grad_copy(n - 2).wait()
        for b in range(ns):
            slots[n % 2, place_of(ns, core, j ^ b)] = total[b * 4 * r : (b + 1) * 4 * r].astype(BF16)
        grad_copy(n).start()

    def one_up_grad(n, _):
        at = pl.ds(pl.multiple_of(n * WIDE, WIDE), WIDE)
        total = jnp.zeros((8, WIDE), F32)
        for h in range(2):
            rr = slice(h * tokens // 2, (h + 1) * tokens // 2)
            low = (nt(dg[rr, :], wd[at, :]) * slope[rr, at]).astype(BF16)
            ug[rr, at] = low
            total = total + jnp.sum(fold(low.astype(F32)), axis=0)
        row = jnp.sum(total, axis=0, keepdims=True)
        for m in range(WIDE // (4 * r)):
            gbup_ref[pl.ds(n * (WIDE // (4 * r)) + m, 1), :] = row[:, m * 4 * r : (m + 1) * 4 * r]
        return 0

    lax.fori_loop(0, ff // WIDE, one_up_grad, 0)
    pltpu.make_async_copy(ug, ug_o, osem.at[4]).start()
    pltpu.make_async_copy(fl, fl_o, osem.at[1]).wait()

    def one_first_grad(s, b):
        at = pl.ds(pl.multiple_of((s * per + b) * block, block), block)
        inside = pl.ds(pl.multiple_of(b * block, block), block)
        fg = nt(ug[at, :], wu[:, model : model + ff]) + first[at, :]
        normed = norm[at, :]
        add_sum(1, fg * normed)
        add_sum(2, fg)
        gn = fg * gain_one
        grad = inv[at, :][:, :1] * (gn - mean(gn) - normed * mean(gn * normed))
        first[at, :] = grad
        low = grad.astype(BF16)
        fl[at, :] = low
        add_sum(0, low.astype(F32))
        tau = tau_rows(len_ref, tim_ref, s, j * rows + b * block, block)
        add_sum(6, grad * tau)
        add_sum(7, grad)
        stage[...] = nt(low, wu[:, 0:model]).astype(BF16)
        for k in range(ns):
            cols = pl.ds(pl.multiple_of((j ^ k) * hg, 128), hg)
            dctx[k][s, inside, :] = stage[:, cols]

    for s in range(seqs):
        one_first_grad(s, 0)
    ag_copy = pltpu.make_async_copy(fl, ag_o, osem.at[5])
    ag_copy.start()
    r1_copy = pltpu.make_async_copy(first, r1_o, osem.at[6])
    r1_copy.start()
    pltpu.make_async_copy(cx, cx_o, osem.at[0]).wait()
    for n in (2 * nz - 2, 2 * nz - 1):
        grad_copy(n).wait()
    pltpu.make_async_copy(ug, ug_o, osem.at[4]).wait()
    ag_copy.wait()
    r1_copy.wait()


def middle(ns, nz, r, lengths, timesteps, idx, tokens, cotangent, small, ctxs, outer, dn):
    seqs, rows, model = tokens.shape
    total = seqs * rows
    ff = 4 * r * ns * nz * 2
    hg = ctxs[0].shape[2]
    sh = lambda *a: jax.ShapeDtypeStruct(a[:-1], a[-1])
    outs = [
        sh(seqs, rows, model, BF16),
        sh(nz, ns, 4 * r, model, BF16),
        sh(nz - 1, ns, 4 * r, model, BF16),
        sh(1, ns, 4 * r, model, BF16),
        sh(total, ff, BF16),
        sh(total, model, BF16),
        sh(total, model, BF16),
        sh(total, model, BF16),
        sh(total, model, F32),
    ]
    outs += [sh(seqs, rows, hg, BF16)] * ns + [sh(16, model, F32), sh(ff // (4 * r), 4 * r, F32)]
    res = pl.pallas_call(
        functools.partial(middle_kernel, ns, nz, r),
        name="middle",
        out_shape=outs,
        in_specs=[sspec()] * 3
        + [vspec()] * (3 + ns)
        + [aspec()] * (len(outer) + len(dn)),
        out_specs=[vspec()] + [aspec()] * 8 + [vspec()] * (ns + 2),
        scratch_shapes=[
            VMEM((model, model + ff + PAD), BF16),
            VMEM((ff, model), BF16),
            VMEM((total, ff), BF16),
            VMEM((total, ff), F32),
            VMEM((total, ff), BF16),
            VMEM((total, model), BF16),
            VMEM((total, model), BF16),
            VMEM((total, model), BF16),
            VMEM((total, model), F32),
            VMEM((total, model), F32),
            VMEM((total, 128), F32),
            VMEM((rows, model), BF16),
            VMEM((8, ff), F32),
            VMEM((2, ns, 4 * r, model), BF16),
            pltpu.SemaphoreType.DMA((3,)),
            pltpu.SemaphoreType.DMA((7,)),
            pltpu.SemaphoreType.DMA((2,)),
        ],
        compiler_params=params(60),
        cost_estimate=cost(
            2 * total * (2 * model * model + 4 * model * ff), 40 << 20, 3 * total * ff
        ),
    )(lengths, timesteps, idx, tokens, cotangent, small, *ctxs, *outer, *dn)
    return res[:9], res[9 : 9 + ns], res[9 + ns], res[10 + ns]


def place_of(ns, core, offset):
    return offset + core * (flipped_bits(offset, ns.bit_length() - 1) - offset)


def gather_columns(ns, nz, r, core, idx, src, dst, first):
    wide = ns * r
    for a in range(nz):
        pair = pl.multiple_of((idx[0] ^ a) * 2 * wide, 2 * wide)
        if wide % 128 == 0:
            got = src[:, pl.ds(pl.multiple_of(pair + core * wide, wide), wide)]
        else:
            both = src[:, pl.ds(pair, 2 * wide)]
            got = jnp.where(core == 0, both[:, :wide], both[:, wide:])
        dst[:, first + a * wide : first + (a + 1) * wide] = got


def store_halves(ns, nz, r, core, idx, total, low, high):
    for b in range(ns):
        slot = place_of(ns, core, idx[2] ^ b)

        def put(dst, slot):
            for a in range(nz):
                n = (a * ns + b) * r
                dst[a, slot] = total[n : n + r].astype(BF16)

        pl.when(slot < ns // 2)(lambda: put(low, slot))
        pl.when(slot >= ns // 2)(lambda: put(high, slot - ns // 2))


def store_slots(ns, nz, r, core, walk, idx, total, dst, at=slice(None)):
    for a in range(nz):
        for b in range(ns):
            slot = place_of(ns, core if walk else 0, idx[2] ^ b)
            n = (a * ns + b) * r
            dst[a, slot, :, at] = total[n : n + r].astype(BF16)


def up_grad_kernel(ns, nz, r, idx, cx_ref, ag_ref, fl_ref, ug_ref, gbup_ref, keep_ref, send_ref, ahead_ref, left):
    i = pl.program_id(0)
    split = ag_ref.shape[1] // WIDE
    last = pl.num_programs(0) - 1
    half = cx_ref.shape[1] // 2
    c = idx[1]

    def both(right):
        total = tn(left[...], right)
        store_slots(ns, nz, r, c, True, idx, total[:half], keep_ref)
        store_halves(ns, nz, r, c ^ 1, idx, total[half:], send_ref, ahead_ref)

    @pl.when(i == 0)
    def _():
        gather_columns(ns, nz, r, c, idx, cx_ref, left, 0)
        gather_columns(ns, nz, r, c ^ 1, idx, cx_ref, left, half)

    @pl.when(i < split)
    def _():
        both(ag_ref[:, pl.ds(pl.multiple_of(jnp.minimum(i, split - 1) * WIDE, WIDE), WIDE)])

    @pl.when(i == split)
    def _():
        gather_columns(ns, nz, r, c, idx, fl_ref, left, 0)
        gather_columns(ns, nz, r, c ^ 1, idx, fl_ref, left, half)

    @pl.when((i >= split) & (i < last))
    def _():
        both(ug_ref[...])

    @pl.when(i == last)
    def _():
        for dst in (keep_ref, send_ref, ahead_ref):
            dst[...] = jnp.zeros_like(dst)
        for cc in range(2):
            core = c ^ cc
            for a in range(nz):
                for b in range(ns):
                    d = ((idx[0] ^ a) * 2 + core) * ns + (idx[2] ^ shift_of(ns, core, b))
                    row = gbup_ref[pl.ds(d, 1), :]
                    dst = keep_ref if cc == 0 else send_ref if b < ns // 2 else ahead_ref
                    dst[a, b if cc == 0 else b % (ns // 2), :, 0 : 4 * r] = jnp.broadcast_to(row, (r, 4 * r)).astype(BF16)


def up_grad(ns, nz, r, idx, cx, ag, fl, ug, gbup):
    total, model = fl.shape
    ff = ug.shape[1]
    width = model + ff + PAD
    split, top = model // WIDE, ff // WIDE - 1
    one = lambda shape: pl.BlockSpec(shape, lambda i: (0,) * len(shape))
    block = lambda n: pl.BlockSpec((nz, n, r, WIDE), lambda i: (0, 0, 0, i))
    return pl.pallas_call(
        functools.partial(up_grad_kernel, ns, nz, r),
        name="up_grad",
        out_shape=[jax.ShapeDtypeStruct((nz, ns, r, width), BF16)]
        + [jax.ShapeDtypeStruct((nz, ns // 2, r, width), BF16)] * 2,
        grid=(pl.cdiv(width, WIDE),),
        in_specs=[
            sspec(),
            one(cx.shape),
            one(ag.shape),
            one(fl.shape),
            pl.BlockSpec((total, WIDE), lambda i: (0, jnp.minimum(jnp.maximum(i - split, 0), top))),
            one(gbup.shape),
        ],
        out_specs=[block(ns), block(ns // 2), block(ns // 2)],
        scratch_shapes=[VMEM((total, model), BF16)],
        compiler_params=params(58, 1),
        cost_estimate=cost(2 * total * model * width, 10 << 20),
    )(idx, cx, ag, fl, ug, gbup)


def qkv_grad_kernel(ns, nz, r, idx, low_ref, g0_ref, g1_ref, sums_ref, s0_ref, s1_ref, b0_ref, b1_ref, keep_ref, send_ref, left, vec, tall):
    c, j = idx[1], idx[2]
    hg = g0_ref.shape[1] // 3
    vec[...] = jnp.zeros_like(vec)
    heads = pl.ds(pl.multiple_of(j * hg, 128), hg)
    both = b0_ref[0:1, :] + b1_ref[0:1, :]
    vec[0:1, heads] = both[:, :hg]
    vec[1:2, heads] = both[:, 2 * hg :]
    vec[2:8, :] = sums_ref[0:6, :]
    vec[8:10, :] = sums_ref[6:8, :] + s0_ref[0:2, :] + s1_ref[0:2, :]
    tall[...] = vec[...].T
    half = left.shape[1] // 2
    for cc, dst in enumerate((keep_ref, send_ref)):
        core = c ^ cc
        total = 0.0
        for s, g in enumerate((g0_ref, g1_ref)):
            gather_columns(ns, nz, r, core, idx, low_ref.at[s], left, cc * half)
            total = total + tn(left[:, cc * half : (cc + 1) * half], g[...])
        store_slots(ns, nz, r, 0, False, idx, total, dst, slice(0, 3 * hg))
        for a in range(nz):
            for b in range(ns):
                d = ((idx[0] ^ a) * 2 + core) * ns + (j ^ b)
                dst[a, b, :, 3 * hg :] = tall[pl.ds(pl.multiple_of(d * r, r), r), :].astype(BF16)


def qkv_grad(ns, nz, r, idx, low, g0, g1, sums, s0, s1, b0, b1):
    seqs, full, model = low.shape
    width = g0.shape[1] + PAD
    out = jax.ShapeDtypeStruct((nz, ns, r, width), BF16)
    return pl.pallas_call(
        functools.partial(qkv_grad_kernel, ns, nz, r),
        name="qkv_grad",
        out_shape=[out, out],
        in_specs=[sspec()] + [vspec()] * 8,
        out_specs=[vspec()] * 2,
        scratch_shapes=[
            VMEM((full, model), BF16),
            VMEM((PAD, model), F32),
            VMEM((model, PAD), F32),
        ],
        compiler_params=params(58),
        cost_estimate=cost(2 * seqs * full * model * width, 12 << 20),
    )(idx, low, g0, g1, sums, s0, s1, b0, b1)


def finish_kernel(ns, r, idx, own_ref, *refs):
    others = refs[: ns - 1]
    q_ref, k_ref, v_ref, small_ref = refs[ns - 1 :]
    j = idx[2]
    hg = (own_ref.shape[1] - PAD) // 3
    small = own_ref[:, 3 * hg :]
    for k in range(ns):
        part = own_ref[...] if k == 0 else others[k - 1][...].astype(F32)
        cols = pl.ds(pl.multiple_of((j ^ k) * hg, 128), hg)
        for n, dst in enumerate((q_ref, k_ref, v_ref)):
            dst[:, cols] = part[:, n * hg : (n + 1) * hg]
        if k:
            small = small + part[:, 3 * hg :]
    small_ref[...] = small.T[:16, :]


def finish(ns, r, model, idx, own, others):
    out = jax.ShapeDtypeStruct((r, model), F32)
    return pl.pallas_call(
        functools.partial(finish_kernel, ns, r),
        name="finish",
        out_shape=[out, out, out, jax.ShapeDtypeStruct((16, r), F32)],
        in_specs=[sspec()] + [vspec()] * ns,
        out_specs=[vspec()] * 4,
        compiler_params=params(16),
    )(idx, own, *others)


def to_seq(value, k):
    ns = lax.axis_size("seq")
    return lax.ppermute(value, "seq", [(i, i ^ k) for i in range(ns)])


def to_mate(value):
    nd = lax.axis_size("dp")
    return lax.ppermute(value, "dp", [(i, i ^ 1) for i in range(nd)])


def to_z(value, a):
    nd = lax.axis_size("dp")
    return lax.ppermute(value, "dp", [(i, i ^ (2 * a)) for i in range(nd)])


def to_ring(value):
    nd = lax.axis_size("dp")
    return lax.ppermute(value, "dp", [(i, (i + 2) % nd) for i in range(nd)])


def to_bit(value, place):
    ns, nd = lax.axis_size("seq"), lax.axis_size("dp")
    high = ns.bit_length() - 2
    pairs = []
    for dp in range(nd):
        bit = 1 << (high - place if dp % 2 else place)
        pairs += [(dp * ns + i, dp * ns + (i ^ bit)) for i in range(ns)]
    return lax.ppermute(value, ("dp", "seq"), pairs)


def gather_plane(block, ns):
    cur = block[None]
    high = ns.bit_length() - 2
    for place in range(high):
        cur = jnp.concatenate([cur, to_bit(cur, place)], axis=0)
    return [cur, to_bit(cur, high)]


def exchange_plane(blocks, ns):
    kept = [blocks[m] for m in range(ns)]
    early = None
    for place in range(ns.bit_length() - 1):
        bit = 1 << place
        away = [m for m in range(ns) if m & bit]
        got = to_bit(jnp.stack([kept[m] for m in away]), place)
        early = got if early is None else early
        for n, m in enumerate(away):
            kept[m] = got[n]
    return jnp.stack(kept), early


def added(terms):
    return functools.reduce(lambda a, b: a + b, [t.astype(F32) for t in terms])


def added_rows(lists):
    return jnp.stack([added(terms) for terms in lists]).astype(BF16)


def hold(*values):
    return lax.optimization_barrier(values)


def after(values, others):
    return lax.optimization_barrier((values, others))


class Scatter:
    def __init__(self, keep, send, ahead, ns, nz):
        self.ns, self.nz = ns, nz
        self.ahead = to_mate(ahead)
        self.terms = [keep]
        self.send = send
        self.last = None

    def fetch(self):
        self.terms = self.terms + [to_mate(self.send)]

    def bit(self):
        half = self.ns // 2
        parts = [t[: self.nz, half : self.ns] for t in self.terms[: 2 if self.ahead is None else 1]]
        parts += [t[: self.nz, half : self.ns] for t in self.terms[2:]]
        if isinstance(self, ScatterDirect) and self.ahead is not None:
            parts, self.ahead = parts + [self.ahead], None
        self.last = added(parts).astype(BF16)
        self.got = to_bit(self.last, self.ns.bit_length() - 2)
        self.ns = half

    def take(self):
        self.terms = self.terms + [self.got]

    def total(self, at=slice(None), row=slice(None)):
        return added([t[0, 0, row, at] for t in self.terms])


class ScatterDirect(Scatter):
    def all_z(self):
        self.last = [added([t[a, 0] for t in self.terms]).astype(BF16) for a in range(1, self.nz)]
        self.got = [to_z(v, a + 1)[None, None] for a, v in enumerate(self.last)]
        self.nz = 1

    def take_z(self):
        self.terms = self.terms + list(self.got)


class ScatterRing(Scatter):
    def ring(self):
        self.nz -= 1
        if self.ahead is not None:
            parts, self.ahead = [self.terms[0][self.nz], self.ahead[0]], None
        else:
            parts = [t[self.nz] for t in self.terms] + [self.got]
        self.last = added(parts).astype(BF16)
        self.got = to_ring(self.last)

    def take_ring(self):
        self.terms = self.terms + [self.got[None]]


def body(
    tokens,
    lengths,
    timesteps,
    w_query,
    b_query,
    w_key,
    w_value,
    b_value,
    w_out,
    b_out,
    gain_one,
    shift_one,
    w_up,
    b_up,
    w_down,
    b_down,
    gain_two,
    shift_two,
    w_time,
    b_time,
    cotangent,
):
    seqs, rows, model = tokens.shape
    ns = lax.axis_size("seq")
    nz = lax.axis_size("dp") // 2
    r = w_query.shape[0]
    hg = model // ns
    dp = lax.axis_index("dp")
    j = lax.axis_index("seq")
    idx = jnp.stack([dp // 2, dp % 2, j]).astype(jnp.int32)

    high = ns.bit_length() - 1
    vectors = [b_query, b_value, b_out, gain_one, shift_one, b_down, gain_two, shift_two, w_time, b_time]
    mine, outer = pack(ns, idx, w_query, w_key, w_value, vectors, b_up, w_out, w_up, w_down)
    tok, down = tokens[None], w_down[r:][None]
    kept = [mine[m] for m in range(ns)]
    outer_z, near_z = [], []
    waiting = list(range(1, nz))
    for place in range(high):
        got = [to_bit(tok, place), to_bit(down, place) if place < high - 1 else None]
        away = [m for m in range(ns) if m & (1 << place)]
        pieces = to_bit(jnp.stack([kept[m] for m in away]), place)
        now = waiting[:2] if place < high - 1 else waiting
        waiting = waiting[len(now) :]
        outer_z = outer_z + [to_z(outer, a) for a in now]
        tok, down, outer, kept, got, pieces, outer_z = hold(tok, down, outer, kept, got, pieces, outer_z)
        for n, m in enumerate(away):
            kept[m] = pieces[n]
        if place < high - 1:
            tok = jnp.concatenate([tok, got[0]], axis=0)
            down = jnp.concatenate([down, got[1]], axis=0)
    toks = [tok, got[0]]
    near = jnp.stack(kept)
    near_z = [to_z(near, a) for a in range(1, nz)]
    cur = jnp.stack([outer] + outer_z)[None]
    down_next, cur_next = to_bit(down, high - 1), to_bit(cur, 0)
    toks, near, near_z, down, down_next, cur, cur_next = hold(
        toks, near, near_z, down, down_next, cur, cur_next
    )
    qa = jnp.stack([near] + near_z)
    qb = to_mate(qa)
    down = jnp.concatenate([down, down_next], axis=0)
    downs = [down, to_ring(down)]
    for place in range(1, high):
        cur = jnp.concatenate([cur, cur_next], axis=0)
        cur_next = to_bit(cur, place)
    qa, _ = after(qa, (down, cur))

    projected = project(ns, nz, lengths, timesteps, idx, toks, qa, qb)
    q, k, v, low, w_qkv, small = projected
    mates, _ = after([cur, down], qb)
    fronts, mates, before = [], [to_mate(m) for m in mates], []
    for s in range(seqs):
        front = attend(ns, s, lengths, idx, q, k, v, before)
        front, downs, mates = hold(front, downs, mates)
        downs.append(to_ring(downs[-1]))
        if s == 0:
            mates = list(mates) + [to_mate(downs[1])]
        else:
            front, cur_next = hold(front, cur_next)
        fronts.append(front)
        before = front[0]
        q, _ = after(q, front[0])
    ctxs = [before[0]] + [to_seq(before[n], n) for n in range(1, ns)]
    while len(downs) < nz:
        downs.append(to_ring(downs[-1]))
    ctxs, downs = hold(ctxs, downs)
    outer = [cur, cur_next, mates[0], to_mate(cur_next)]
    mates = list(mates[1:]) + [to_mate(d) for d in downs[2:]]
    downs = [x for pair in zip(downs, mates) for x in pair]
    kept, dctx_out, sums, gbup = middle(
        ns, nz, r, lengths, timesteps, idx, tokens, cotangent, small, ctxs, outer, downs
    )
    output, keep, send, ahead, ug, fl, cx, ag, r1 = kept

    two = ScatterRing(keep, send, ahead, ns, nz)
    dctx = [to_seq(dctx_out[n], n) for n in range(1, ns)]
    two.send, two.ahead = hold(two.send, two.ahead)
    two.fetch()
    two.ring()
    (fl, ug), _ = after((fl, ug), (dctx_out, two.last))
    got = up_grad(ns, nz, r, idx, cx, ag, fl, ug, gbup)
    got, dctx, two.got, two.terms = hold(got, dctx, two.got, two.terms)
    dctx = [dctx_out[0]] + list(dctx)
    one = ScatterDirect(*got, ns, nz)
    two.ring()
    one.bit()
    one.send, _ = after(one.send, one.last)
    one.fetch()
    dctx, _ = after(dctx, (one.last, two.last))
    r1 = r1.reshape(seqs, rows, model)
    backs, planes = [], []
    for s in range(seqs):
        back = attend_back(ns, s, lengths, timesteps, idx, q, k, v, fronts[s][1], fronts[s][2], w_qkv, dctx)
        back, two.got, one.got, planes = hold(back, two.got, one.got, planes)
        backs.append(back)
        planes = list(planes)
        one.take()
        sent = []
        if two.nz > 1:
            two.ring()
            sent.append(two.last)
        if one.ns > 1:
            one.bit()
            sent.append(one.last)
        elif one.nz > 1:
            one.all_z()
            sent.append(one.last)
        away = after(back[2], sent)[0] if s else back[2]
        planes.append([back[1], to_bit(away, high - 1)])
        dctx, _ = after(dctx, (sent, back[2]))
    two.got, _ = after(two.got, one.last)
    while two.nz > 1:
        two.ring()
    two.take_ring()
    while one.ns > 1:
        one.take()
        one.bit()
    if one.nz > 1:
        one.take()
        one.all_z()
    two.bit()
    low, _ = after(low, (one.last, backs[-1][2]))
    keep, send = qkv_grad(
        ns, nz, r, idx, low, backs[0][0], backs[1][0], sums, backs[0][3], backs[1][3], backs[0][4], backs[1][4]
    )
    keep, send, one.got, two.got, planes = hold(keep, send, one.got, two.got, planes)
    near = [keep, to_mate(send)]
    one.take_z()
    two.take()
    away = [added([t[a] for t in near]).astype(BF16) for a in range(1, nz)]
    near_z = [to_z(v, a + 1) for a, v in enumerate(away)]
    planes, two.terms, _ = hold(planes, two.terms, away)
    while two.ns > 1:
        two.bit()
        two.take()
    n = ns // 2
    while n > 1:
        away = added_rows([[t[n // 2 : n] for t in p] for p in planes])
        n //= 2
        got = to_bit(away, n.bit_length() - 1)
        planes = [list(p) + [got[i]] for i, p in enumerate(planes)]
    one.terms, _ = after(one.terms, near_z[-1])
    ends = (slice(0, model), slice(model, 5 * model))
    outs = [one.total(at) for at in ends] + [one.total(slice(5 * model, 5 * model + 4 * r), 0)]
    near_z, two.terms, outs = hold(near_z, two.terms, outs)
    own = added([t[0] for t in near] + near_z)
    others = [to_seq(own[n].astype(BF16), n) for n in range(1, ns)]
    grad_down = two.total()
    grad_tokens = jnp.stack([added([t[0] for t in p] + [r1[s]]).astype(BF16) for s, p in enumerate(planes)])
    others, grad_tokens, grad_down = hold(others, grad_tokens, grad_down)
    g_query, g_key, g_value, vectors = finish(ns, r, model, idx, own[0], others)
    return (
        output,
        grad_tokens,
        g_query,
        vectors[0],
        g_key,
        g_value,
        vectors[1],
        outs[0],
        vectors[2],
        vectors[3],
        vectors[4],
        outs[1],
        outs[2],
        grad_down,
        vectors[5],
        vectors[6],
        vectors[7],
        vectors[8],
        vectors[9],
    )


def solution(mesh):
    split = P(("dp", "seq"))
    rows = P(("dp", "seq"), None)
    token = P("dp", "seq", None)
    items = P("dp", None)
    return jax.shard_map(
        body,
        mesh=mesh,
        in_specs=(
            token, items, items, rows, split, rows, rows, split, rows, split, split, split,
            rows, split, rows, split, split, split, split, split, token,
        ),
        out_specs=(
            token, token, rows, split, rows, rows, split, rows, split, split, split,
            rows, split, rows, split, split, split, split, split,
        ),
        check_vma=False,
    )
```
